128 devices in a mesh: span: 8 (over y_lo, x), head: 16 (over z, y_hi, core).
Axes of the slice: x: 4, y: 4 (y_hi: 2, y_lo: 2; y = y_hi * 2 + y_lo), z: 4, core: 2. Of those that a mesh axis runs over, the one named last changes fastest.
Arguments:
- latents: bfloat16 [4096, 6144], P(('span', 'head')), may hold values from -6 to 6
- noise_level: int32 [8], replicated, may hold values from 0 to 7
- context_mask: int32 [8, 8], replicated, may hold values from 0 to 1, as said below
- mod_table: bfloat16 [8, 4, 6144], replicated, may hold values from -3 to 3
- w_query: bfloat16 [6144, 6144], P(None, 'head'), may hold values from -0.078125 to 0.078125
- w_key: bfloat16 [6144, 6144], P(None, 'head'), may hold values from -0.078125 to 0.078125
- w_value: bfloat16 [6144, 6144], P(None, 'head'), may hold values from -0.078125 to 0.078125
- q_gain: float32 [128], replicated, may hold values from 0.5 to 1.5
- k_gain: float32 [128], replicated, may hold values from 0.5 to 1.5
- w_out: bfloat16 [6144, 6144], P('head'), may hold values from -0.078125 to 0.078125
- w_up: bfloat16 [6144, 12288], P(None, ('span', 'head')), may hold values from -0.078125 to 0.078125
- w_down: bfloat16 [12288, 6144], P(('span', 'head')), may hold values from -0.0546875 to 0.0546875
Outputs:
- blended: bfloat16 [4096, 6144], P(('span', 'head'))
The draws below stay inside these ranges and needn't reach their ends.
Inputs may be any that keep to these rules, and one draw needn't show every extreme that they name: context_mask[c, c] = 1 and context_mask[c, c2] = 0 for c2 > c; earlier spans are 0 or 1.
All inputs are finite; a program needn't handle non-finite values.
Results may differ from the reference program's by a relative error of at most 0.014.
Values may be sent and summed in bfloat16 or wider, within the bound.
No kernel may reach another device: no remote copies, remote signals or barrier semaphores. Data moves between devices by JAX's collectives and lax.ppermute only.
A program may use at most 192 MiB of HBM per device.

```python
import math
import jax
import jax.numpy as jnp
from jax import lax

D = 6144
HD = 128
FF = 12288
LEVELS = 8
SPANS = 8
TOKENS = 4096
HEADS = 48
N_SPAN = 8
N_HEAD = 16


def draw_context_mask(key, part):
    key = jax.random.fold_in(key, 7)
    picked = jax.random.randint(key, (SPANS, SPANS), 0, 4)
    row_ids = jnp.arange(SPANS)[:, None]
    col_ids = jnp.arange(SPANS)[None, :]
    earlier = (col_ids < row_ids) & (picked < 3)
    return jnp.where((col_ids == row_ids) | earlier, 1, 0).astype(jnp.int32)


def plant(array, rng, smallest, top_value):
    longest = array.shape.index(max(array.shape))
    spots = []
    for shift in (0, 1):
        where = [jax.random.randint(jax.random.fold_in(rng, axis), (), 0, length) for axis, length in enumerate(array.shape)]
        where[longest] = (where[longest] + shift) % array.shape[longest]
        spots.append(tuple(where))
    return array.at[spots[0]].set(smallest).at[spots[1]].set(top_value)


def shard_levels(key, dims, cuts, least, top_value):
    gain = 1.0
    for axis_at, shards_of in cuts:
        heights = jax.random.uniform(jax.random.fold_in(jax.random.fold_in(key, 6), axis_at), (shards_of,), jnp.float32, least / len(cuts), top_value / len(cuts))
        gain = gain * jnp.repeat(jnp.exp(heights), dims[axis_at] // shards_of).reshape((-1,) + (1,) * (len(dims) - 1 - axis_at))
    return gain


def scatter_about(key, extent, width, most, split=(), kind=jnp.bfloat16):
    gain = shard_levels(key, extent, split, -0.22, 0.18) if split else 1.0
    entries = jax.random.normal(key, extent, jnp.float32) * width * gain
    return jnp.minimum(jnp.maximum(entries, -most), most).astype(kind)


def setup_inputs(seed: int = 0) -> dict:
    key_list = jax.random.split(jax.random.key(seed), 13)
    latents = scatter_about(key_list[0], (TOKENS, D), 1.0, 6.0, ((0, 128),))
    noise_level = plant(jax.random.randint(key_list[1], (SPANS,), 0, LEVELS), jax.random.fold_in(key_list[1], 1), 0, LEVELS - 1).astype(jnp.int32)
    context_mask = draw_context_mask(jax.random.fold_in(key_list[12], 71), 0)
    mod_table = scatter_about(key_list[3], (LEVELS, 4, D), 0.5, 3.0)
    w_query = scatter_about(key_list[4], (D, HEADS * HD), D ** -0.5, 0.078125, ((1, 16),))
    w_key = scatter_about(key_list[5], (D, HEADS * HD), D ** -0.5, 0.078125, ((1, 16),))
    w_value = scatter_about(key_list[6], (D, HEADS * HD), D ** -0.5, 0.078125, ((1, 16),))
    q_gain = jnp.clip(jnp.exp(jax.random.uniform(key_list[7], (HD,), jnp.float32, math.log(0.5), math.log(1.5))), 0.5, 1.5)
    k_gain = jnp.clip(jnp.exp(jax.random.uniform(key_list[8], (HD,), jnp.float32, math.log(0.5), math.log(1.5))), 0.5, 1.5)
    w_out = scatter_about(key_list[9], (HEADS * HD, D), (HEADS * HD) ** -0.5, 0.078125, ((0, 16),))
    w_up = scatter_about(key_list[10], (D, FF), D ** -0.5, 0.078125, ((1, 128),))
    w_down = scatter_about(key_list[11], (FF, D), FF ** -0.5, 0.0546875, ((0, 128),))
    return {"latents": latents, "noise_level": noise_level, "context_mask": context_mask, "mod_table": mod_table, "w_query": w_query, "w_key": w_key, "w_value": w_value, "q_gain": q_gain, "k_gain": k_gain, "w_out": w_out, "w_up": w_up, "w_down": w_down}


epsilon = 1e-06

def normed(values):
    return values * lax.rsqrt(lax.optimization_barrier(jnp.mean(values * values, axis=-1, keepdims=True)) + epsilon)

def reference(latents, noise_level, context_mask, mod_table, w_query, w_key, w_value, q_gain, k_gain, w_out, w_up, w_down):
    token_count = latents.shape[0]
    span_len = token_count // N_SPAN
    stream = latents.astype(jnp.float32).reshape(N_SPAN, span_len, D)
    modulation = mod_table[noise_level].astype(jnp.float32)
    scale_one = modulation[:, 0][:, None, :]
    gate_one = modulation[:, 1][:, None, :]
    scale_two = modulation[:, 2][:, None, :]
    gate_two = modulation[:, 3][:, None, :]
    attn_in = (normed(stream) * (1.0 + scale_one)).astype(jnp.bfloat16).reshape(token_count, D)
    head_count = w_query.shape[1] // HD

    def project(weight):
        return jnp.dot(attn_in, weight, preferred_element_type=jnp.float32).reshape(token_count, head_count, HD)
    queries_n = (normed(project(w_query)) * q_gain).astype(jnp.bfloat16)
    keys_n = (normed(project(w_key)) * k_gain).astype(jnp.bfloat16)
    value_vecs = project(w_value).astype(jnp.bfloat16)
    key_span = (jnp.arange(token_count) // span_len).astype(jnp.int32)

    def one_span(span_id):
        query_rows = lax.dynamic_slice_in_dim(queries_n, (span_id * span_len).astype(jnp.int32), span_len, 0)
        allowed = context_mask[span_id][key_span] > 0
        scores = jnp.einsum('qhd,khd->hqk', query_rows.astype(jnp.float32), keys_n.astype(jnp.float32)) * HD ** (-0.5)
        scores = jnp.where(allowed[None, None, :], scores, -1e+30)
        peak = lax.optimization_barrier(jnp.max(scores, axis=-1, keepdims=True))
        probs = jnp.where(allowed[None, None, :], jnp.exp(scores - peak), 0.0)
        denom = lax.optimization_barrier(jnp.sum(probs, axis=-1))
        weighted = jnp.einsum('hqk,khd->hqd', probs.astype(jnp.bfloat16).astype(jnp.float32), value_vecs.astype(jnp.float32))
        attended = weighted / denom[:, :, None]
        return jnp.transpose(attended, (1, 0, 2)).astype(jnp.bfloat16)
    attended = lax.map(one_span, jnp.arange(N_SPAN, dtype=jnp.int32)).reshape(token_count, head_count * HD)
    block_heads = head_count * HD // N_HEAD

    def add_head_block(block_id, total):
        offset = (block_id * block_heads).astype(jnp.int32)
        part_in = lax.dynamic_slice_in_dim(attended, offset, block_heads, 1)
        part_weight = lax.dynamic_slice_in_dim(w_out, offset, block_heads, 0)
        term = lax.optimization_barrier(jnp.dot(part_in, part_weight, preferred_element_type=jnp.float32).astype(jnp.bfloat16))
        return total + term.astype(jnp.float32)
    attn_out = lax.fori_loop(0, N_HEAD, add_head_block, jnp.zeros((token_count, D), jnp.float32))
    resid = stream + gate_one * attn_out.reshape(N_SPAN, span_len, D)
    mlp_in = (normed(resid) * (1.0 + scale_two)).astype(jnp.bfloat16).reshape(token_count, D)
    hidden = jax.nn.gelu(jnp.dot(mlp_in, w_up, preferred_element_type=jnp.float32), approximate=True).astype(jnp.bfloat16)
    slice_units = FF // (N_SPAN * N_HEAD)
    hidden_four = hidden.reshape(token_count, N_SPAN, N_HEAD, slice_units)
    down_four = w_down.reshape(N_SPAN, N_HEAD, slice_units, D)

    def add_unit_group(group_id, total):
        group = group_id.astype(jnp.int32)
        part_in = lax.dynamic_slice_in_dim(hidden_four, group, 1, 2).reshape(token_count, N_SPAN * slice_units)
        part_weight = lax.dynamic_slice_in_dim(down_four, group, 1, 1).reshape(N_SPAN * slice_units, D)
        term = lax.optimization_barrier(jnp.dot(part_in, part_weight, preferred_element_type=jnp.float32).astype(jnp.bfloat16))
        return total + term.astype(jnp.float32)
    mlp_out = lax.fori_loop(0, N_HEAD, add_unit_group, jnp.zeros((token_count, D), jnp.float32))
    blended = resid + gate_two * mlp_out.reshape(N_SPAN, span_len, D)
    return blended.reshape(token_count, D).astype(jnp.bfloat16)
```

```python
import jax
import jax.numpy as jnp
from jax import lax
from jax.sharding import Mesh, PartitionSpec as P

HD = 128
AXES = ("yl", "x", "z", "yh", "c")
SIZES = {"yl": 2, "x": 4, "z": 4, "yh": 2, "c": 2}

epsilon = 1e-06


def normed(values):
    return values * lax.rsqrt(jnp.mean(values * values, axis=-1, keepdims=True) + epsilon)


def take_from(value, axis, offset):
    size = SIZES[axis]
    return lax.ppermute(value, axis, [((i + offset) % size, i) for i in range(size)])


def gather_near(own, ring, pair):
    half = own.shape[0] // 2
    plus = take_from(own, ring, 1)
    minus = take_from(own, ring, -1)
    other = take_from(own, pair, 1)
    far = jnp.concatenate([take_from(plus[:half], ring, 1), take_from(minus[half:], ring, -1)])
    other_plus = take_from(other, ring, 1)
    other_minus = take_from(other, ring, -1)
    other_far = take_from(far, pair, 1)
    return [own, plus, minus, far], [other, other_plus, other_minus, other_far]


def add(a, b):
    return (a.astype(jnp.float32) + b.astype(jnp.float32)).astype(jnp.bfloat16)


def gather_rows(own):
    near, other = gather_near(own, "z", "yh")
    chunks = []
    for blocks in (near, other):
        mine = jnp.concatenate(blocks)
        chunks.append(jnp.concatenate([mine, take_from(mine, "c", 1)]))
    return chunks


def scatter_rows(near, other, rows):
    half = rows // 2
    cut = 4 * rows
    o = add(other[:cut], take_from(other[cut:], "c", 1))
    n = add(near[:cut], take_from(near[cut:], "c", 1))
    o0, op, om, of = (o[i * rows : (i + 1) * rows] for i in range(4))
    n0, np_, nm, nf = (n[i * rows : (i + 1) * rows] for i in range(4))
    from_plus = take_from(om, "z", 1)
    from_minus = take_from(op, "z", -1)
    from_pair = take_from(of, "yh", 1)
    o0 = (
        o0.astype(jnp.float32) + from_plus.astype(jnp.float32) + from_minus.astype(jnp.float32)
    ).astype(jnp.bfloat16)
    nf = add(nf, from_pair)
    first = take_from(nf[:half], "z", -1)
    second = take_from(nf[half:], "z", 1)
    np_ = jnp.concatenate([add(np_[:half], first), np_[half:]])
    nm = jnp.concatenate([nm[:half], add(nm[half:], second)])
    return (
        n0.astype(jnp.float32)
        + take_from(nm, "z", 1).astype(jnp.float32)
        + take_from(np_, "z", -1).astype(jnp.float32)
        + take_from(o0, "yh", 1).astype(jnp.float32)
    )


def on_device(
    latents,
    noise_level,
    context_mask,
    mod_table,
    w_query,
    w_key,
    w_value,
    q_gain,
    k_gain,
    w_out,
    w_up,
    w_down,
):
    rows = latents.shape[0]
    x_id, yl_id = lax.axis_index("x"), lax.axis_index("yl")
    span_id = yl_id * 4 + x_id
    level = lax.dynamic_index_in_dim(noise_level, span_id, 0, keepdims=False)
    modulation = lax.dynamic_index_in_dim(mod_table, level, 0, keepdims=False).astype(jnp.float32)
    scale_one, gate_one, scale_two, gate_two = (modulation[i] for i in range(4))
    mask_row = lax.dynamic_index_in_dim(context_mask, span_id, 0, keepdims=False)
    stream = latents.astype(jnp.float32)
    attn_own = (normed(stream) * (1.0 + scale_one)).astype(jnp.bfloat16)
    local_heads = w_query.shape[1] // HD

    chunks = gather_rows(attn_own)
    span_len = 16 * rows

    def head_norm(values, gain):
        shape = values.shape
        values = values.reshape(shape[0], local_heads, HD)
        return (normed(values) * gain).astype(jnp.bfloat16).reshape(shape)

    queries, keys, values = [], [], []
    for chunk in chunks:
        keys.append(head_norm(jnp.dot(chunk, w_key, preferred_element_type=jnp.float32), k_gain))
        values.append(jnp.dot(chunk, w_value, preferred_element_type=jnp.float32).astype(jnp.bfloat16))
        queries.append(head_norm(jnp.dot(chunk, w_query, preferred_element_type=jnp.float32), q_gain))
    queries = jnp.concatenate(queries)
    own_kv = jnp.concatenate([jnp.concatenate(keys), jnp.concatenate(values)], axis=1)
    near_kv, other_kv = gather_near(own_kv, "x", "yl")
    up_blocks = sum(gather_near(w_up.T, "x", "yl"), [])
    down_blocks = sum(gather_near(w_down, "x", "yl"), [])

    total = jnp.zeros((local_heads, span_len, HD), jnp.float32)
    denom = jnp.zeros((local_heads, span_len), jnp.float32)
    q_heads = queries.reshape(span_len, local_heads, HD)
    for dy, blocks in enumerate((near_kv, other_kv)):
        for dx, block in zip((0, 1, 3, 2), blocks):
            from_span = ((yl_id + dy) % 2) * 4 + (x_id + dx) % 4
            allowed = lax.dynamic_index_in_dim(mask_row, from_span, 0, keepdims=False) > 0
            k, v = (
                t.reshape(span_len, local_heads, HD) for t in jnp.split(block, 2, axis=1)
            )
            scores = jnp.einsum("qhd,khd->hqk", q_heads, k, preferred_element_type=jnp.float32)
            probs = jnp.where(allowed, jnp.exp(scores * HD ** (-0.5)), 0.0)
            denom = denom + jnp.sum(probs, axis=-1)
            total = total + jnp.einsum(
                "hqk,khd->hqd", probs.astype(jnp.bfloat16), v, preferred_element_type=jnp.float32
            )
    attended = (total / denom[:, :, None]).astype(jnp.bfloat16)
    attended = jnp.transpose(attended, (1, 0, 2)).reshape(span_len, local_heads * HD)
    part = [
        jnp.dot(attended[i : i + 8 * rows], w_out, preferred_element_type=jnp.float32).astype(jnp.bfloat16)
        for i in (0, 8 * rows)
    ]
    resid = stream + gate_one * scatter_rows(part[0], part[1], rows)
    mlp_own = (normed(resid) * (1.0 + scale_two)).astype(jnp.bfloat16)
    chunks = gather_rows(mlp_own)
    up = jnp.concatenate(up_blocks)
    down = jnp.concatenate(down_blocks)
    part = []
    for chunk in chunks:
        hidden = lax.dot_general(chunk, up, (((1,), (1,)), ((), ())), preferred_element_type=jnp.float32)
        hidden = jax.nn.gelu(hidden, approximate=True).astype(jnp.bfloat16)
        part.append(jnp.dot(hidden, down, preferred_element_type=jnp.float32).astype(jnp.bfloat16))
    return (resid + gate_two * scatter_rows(part[0], part[1], rows)).astype(jnp.bfloat16)


def solution(mesh):
    fine = Mesh(mesh.devices.reshape([SIZES[a] for a in AXES]), AXES)
    span, head = ("yl", "x"), ("z", "yh", "c")
    return jax.shard_map(
        on_device,
        mesh=fine,
        in_specs=(
            P(AXES, None),
            P(),
            P(),
            P(),
            P(None, head),
            P(None, head),
            P(None, head),
            P(),
            P(),
            P(head, None),
            P(None, AXES),
            P(AXES, None),
        ),
        out_specs=P(AXES, None),
        check_vma=False,
    )
```

```python
import functools

import jax
import jax.numpy as jnp
from jax import lax
from jax.experimental import pallas as pl
from jax.experimental.pallas import tpu as pltpu
from jax.sharding import Mesh, PartitionSpec as P

HD = 128
AXES = ("yl", "x", "z", "yh", "c")
SIZES = {"yl": 2, "x": 4, "z": 4, "yh": 2, "c": 2}
BLOCK = 768
MIB = 1024 * 1024

epsilon = 1e-06


def normed(values):
    return values * lax.rsqrt(jnp.mean(values * values, axis=-1, keepdims=True) + epsilon)


def take_from(value, axis, offset):
    size = SIZES[axis]
    return lax.ppermute(value, axis, [((i + offset) % size, i) for i in range(size)])


def after(value, *others):
    return lax.optimization_barrier((value, others))[0]


def params(mib):
    return pltpu.CompilerParams(vmem_limit_bytes=mib * MIB, dimension_semantics=("arbitrary",))


def qkv_kernel(heads, *refs):
    x_refs, (wq, wk, wv, q_gain, k_gain, q_ref, kv_ref, acc) = refs[:-8], refs[-8:]
    k = pl.program_id(0)
    x = jnp.concatenate([r[...] for r in x_refs], axis=0)
    w = jnp.concatenate([wq[...], wk[...], wv[...]], axis=1)
    part = jnp.dot(x, w, preferred_element_type=jnp.float32)

    @pl.when(k == 0)
    def _():
        acc[...] = part

    @pl.when(k > 0)
    def _():
        acc[...] += part

    @pl.when(k == pl.num_programs(0) - 1)
    def _():
        width = heads * HD
        for h in range(heads):
            at = pl.ds(h * HD, HD)
            q_ref[:, at] = (normed(acc[:, at]) * q_gain[...]).astype(jnp.bfloat16)
            kv_ref[:, at] = (normed(acc[:, pl.ds(width + h * HD, HD)]) * k_gain[...]).astype(jnp.bfloat16)
        kv_ref[:, width:] = acc[:, 2 * width :].astype(jnp.bfloat16)


def project(blocks, wq, wk, wv, q_gain, k_gain):
    depth, width = wq.shape
    rows = sum(b.shape[0] for b in blocks)
    heads = width // HD
    weight = pl.BlockSpec((BLOCK, width), lambda k: (k, 0))
    gain = pl.BlockSpec((1, HD), lambda k: (0, 0))
    return pl.pallas_call(
        functools.partial(qkv_kernel, heads),
        grid=(depth // BLOCK,),
        in_specs=[pl.BlockSpec((b.shape[0], BLOCK), lambda k: (0, k)) for b in blocks]
        + [weight] * 3
        + [gain] * 2,
        out_specs=[
            pl.BlockSpec((rows, width), lambda k: (0, 0)),
            pl.BlockSpec((rows, 2 * width), lambda k: (0, 0)),
        ],
        out_shape=[
            jax.ShapeDtypeStruct((rows, width), jnp.bfloat16),
            jax.ShapeDtypeStruct((rows, 2 * width), jnp.bfloat16),
        ],
        scratch_shapes=[pltpu.VMEM((rows, 3 * width), jnp.float32)],
        compiler_params=params(20),
        cost_estimate=pl.CostEstimate(
            flops=6 * rows * depth * width, bytes_accessed=6 * depth * width + 2 * rows * depth, transcendentals=0
        ),
        name="project",
    )(*blocks, wq, wk, wv, q_gain.reshape(1, HD), k_gain.reshape(1, HD))


def attend_kernel(heads, count, first, last, *refs):
    allowed, refs = refs[0], refs[1:]
    q_refs, refs = refs[:2], refs[2:]
    kv_refs, refs = refs[: 2 * count], refs[2 * count :]
    if not first:
        old_acc, old_sum, refs = refs[0], refs[1], refs[2:]
    if last:
        out_ref, acc, total = refs
    else:
        acc, total = refs
    rows = q_refs[0].shape[0]
    width = heads * HD
    if first:
        acc[...] = jnp.zeros_like(acc)
        total[...] = jnp.zeros_like(total)
    else:
        acc[...] = old_acc[...]
        total[...] = old_sum[...]
    factor = HD ** (-0.5) * 1.4426950408889634
    for b in range(2 * count):

        @pl.when(allowed[b // 2] > 0)
        def _(b=b):
            for part in range(2):
                at = pl.ds(part * rows, rows)
                for h in range(heads):
                    cols = pl.ds(h * HD, HD)
                    keys = kv_refs[b][:, cols]
                    values = kv_refs[b][:, pl.ds(width + h * HD, HD)]
                    scores = lax.dot_general(
                        q_refs[part][:, cols], keys, (((1,), (1,)), ((), ())), preferred_element_type=jnp.float32
                    )
                    probs = jnp.exp2(scores * factor)
                    lanes = probs[:, :HD]
                    for i in range(1, probs.shape[1] // HD):
                        lanes = lanes + probs[:, i * HD : (i + 1) * HD]
                    total[at, cols] += lanes
                    acc[at, cols] += jnp.dot(
                        probs.astype(jnp.bfloat16), values, preferred_element_type=jnp.float32
                    )

    if last:
        for h in range(heads):
            cols = pl.ds(h * HD, HD)
            denom = jnp.sum(total[:, cols], axis=-1, keepdims=True)
            out_ref[:, cols] = (acc[:, cols] / denom).astype(jnp.bfloat16)


def attend(queries, blocks, allowed, carry, last):
    rows, width = queries[0].shape
    heads = width // HD
    count = len(blocks)
    whole = pl.BlockSpec(memory_space=pltpu.VMEM)
    state = jax.ShapeDtypeStruct((2 * rows, width), jnp.float32)
    ops = [allowed, *queries] + [half for block in blocks for half in block] + list(carry or ())
    if last:
        out_shape = jax.ShapeDtypeStruct((2 * rows, width), jnp.bfloat16)
        scratch = [pltpu.VMEM(state.shape, jnp.float32)] * 2
        out_specs = whole
    else:
        out_shape, scratch, out_specs = [state, state], [], [whole, whole]
    return pl.pallas_call(
        functools.partial(attend_kernel, heads, count, carry is None, last),
        in_specs=[pl.BlockSpec(memory_space=pltpu.SMEM)] + [whole] * (len(ops) - 1),
        out_specs=out_specs,
        out_shape=out_shape,
        scratch_shapes=scratch,
        compiler_params=pltpu.CompilerParams(vmem_limit_bytes=32 * MIB),
        cost_estimate=pl.CostEstimate(
            flops=16 * count * rows * rows * width, bytes_accessed=8 * count * rows * width, transcendentals=0
        ),
        name="attend",
    )(*ops)


def out_kernel(a_ref, w_ref, keep_ref, send_ref):
    half = keep_ref.shape[0]
    r = jnp.dot(a_ref[...], w_ref[...], preferred_element_type=jnp.float32).astype(jnp.bfloat16)
    keep_ref[...] = r[:half]
    send_ref[...] = r[half:]


def project_out(attended, chunk, w_out):
    depth, width = w_out.shape
    rows = attended.shape[0] // 2
    return pl.pallas_call(
        out_kernel,
        grid=(width // BLOCK,),
        in_specs=[
            pl.BlockSpec((rows, depth), lambda n: (chunk, 0)),
            pl.BlockSpec((depth, BLOCK), lambda n: (0, n)),
        ],
        out_specs=[pl.BlockSpec((rows // 2, BLOCK), lambda n: (0, n))] * 2,
        out_shape=[jax.ShapeDtypeStruct((rows // 2, width), jnp.bfloat16)] * 2,
        compiler_params=params(16),
        cost_estimate=pl.CostEstimate(
            flops=2 * rows * depth * width, bytes_accessed=2 * (depth + rows) * width, transcendentals=0
        ),
        name="project_out",
    )(attended, w_out)


def mlp_kernel(xs, ups, steps, *refs):
    x_refs, up_refs, down_refs = refs[:xs], refs[xs : xs + ups], refs[xs + ups : xs + 2 * ups]
    keep_ref, send_ref, acc, hidden = refs[xs + 2 * ups :]
    k = pl.program_id(0)

    @pl.when(k < steps)
    def _():
        x = jnp.concatenate([r[...] for r in x_refs], axis=0)
        w = jnp.concatenate([r[...] for r in up_refs], axis=0)
        part = lax.dot_general(x, w, (((1,), (1,)), ((), ())), preferred_element_type=jnp.float32)

        @pl.when(k == 0)
        def _():
            acc[...] = part

        @pl.when(k > 0)
        def _():
            acc[...] += part

        @pl.when(k == steps - 1)
        def _():
            hidden[...] = jax.nn.gelu(acc[...], approximate=True).astype(jnp.bfloat16)

    @pl.when(k >= steps)
    def _():
        w = jnp.concatenate([r[...] for r in down_refs], axis=0)
        r = jnp.dot(hidden[...], w, preferred_element_type=jnp.float32).astype(jnp.bfloat16)
        half = keep_ref.shape[0]
        keep_ref[...] = r[:half]
        send_ref[...] = r[half:]


def feed_forward(blocks, ups, downs):
    width = ups[0].shape[1]
    units = sum(u.shape[0] for u in ups)
    rows = sum(b.shape[0] for b in blocks)
    steps = width // BLOCK
    first = lambda k: (0, jnp.minimum(k, steps - 1))
    second = lambda k: (0, jnp.maximum(k - steps, 0))
    return pl.pallas_call(
        functools.partial(mlp_kernel, len(blocks), len(ups), steps),
        grid=(2 * steps,),
        in_specs=[pl.BlockSpec((b.shape[0], BLOCK), first) for b in blocks]
        + [pl.BlockSpec((u.shape[0], BLOCK), first) for u in ups]
        + [pl.BlockSpec((d.shape[0], BLOCK), second) for d in downs],
        out_specs=[pl.BlockSpec((rows // 2, BLOCK), second)] * 2,
        out_shape=[jax.ShapeDtypeStruct((rows // 2, width), jnp.bfloat16)] * 2,
        scratch_shapes=[pltpu.VMEM((rows, units), jnp.float32), pltpu.VMEM((rows, units), jnp.bfloat16)],
        compiler_params=params(20),
        cost_estimate=pl.CostEstimate(
            flops=4 * rows * units * width, bytes_accessed=4 * units * width + 4 * rows * width, transcendentals=rows * units
        ),
        name="feed_forward",
    )(*blocks, *ups, *downs)


def gather_first(own, ring, pair):
    return take_from(own, ring, 1), take_from(own, ring, -1), take_from(own, pair, 1)


def gather_rest(plus, minus, other, ring, pair):
    half = plus.shape[0] // 2
    first = take_from(plus[:half], ring, 1)
    second = take_from(minus[half:], ring, -1)
    other_plus = take_from(other, ring, 1)
    other_minus = take_from(other, ring, -1)
    far = jnp.concatenate([first, second])
    return far, other_plus, other_minus, take_from(far, pair, 1)


def gather_rows(own):
    swap = lambda t: take_from(t, "c", 1)
    plus, minus, other = gather_first(own, "z", "yh")
    far, other_plus, other_minus, other_far = gather_rest(plus, minus, other, "z", "yh")
    near = [own, plus, minus, far]
    away = [other, other_plus, other_minus, other_far]
    return near + [swap(t) for t in near], away + [swap(t) for t in away]


def wide(t):
    return t.astype(jnp.float32)


def add(*terms):
    return functools.reduce(jnp.add, map(wide, terms)).astype(jnp.bfloat16)


def scatter_rows(near, away, rows):
    half = rows // 2
    cut = lambda t, i: t[i * rows : (i + 1) * rows]
    away_got = take_from(away[1], "c", 1)
    near_got = take_from(near[1], "c", 1)
    away_sum = [add(cut(away[0], i), cut(away_got, i)) for i in (1, 2, 3)]
    from_minus = take_from(away_sum[0], "z", -1)
    from_plus = take_from(away_sum[1], "z", 1)
    from_pair = take_from(away_sum[2], "yh", 1)
    far = add(cut(near[0], 3), cut(near_got, 3), from_pair)
    first = take_from(far[:half], "z", -1)
    second = take_from(far[half:], "z", 1)
    away_own = add(cut(away[0], 0), cut(away_got, 0), from_plus, from_minus)
    plus = wide(cut(near[0], 1)) + wide(cut(near_got, 1))
    minus = wide(cut(near[0], 2)) + wide(cut(near_got, 2))
    plus = jnp.concatenate([plus[:half] + wide(first), plus[half:]]).astype(jnp.bfloat16)
    minus = jnp.concatenate([minus[:half], minus[half:] + wide(second)]).astype(jnp.bfloat16)
    total = wide(cut(near[0], 0)) + wide(cut(near_got, 0))
    total = total + wide(take_from(plus, "z", -1)) + wide(take_from(minus, "z", 1))
    return total + wide(take_from(away_own, "yh", 1)), from_pair


def on_device(
    latents,
    noise_level,
    context_mask,
    mod_table,
    w_query,
    w_key,
    w_value,
    q_gain,
    k_gain,
    w_out,
    w_up,
    w_down,
):
    rows = latents.shape[0]
    x_id, yl_id = lax.axis_index("x"), lax.axis_index("yl")
    span_id = yl_id * 4 + x_id
    level = lax.dynamic_index_in_dim(noise_level, span_id, 0, keepdims=False)
    modulation = lax.dynamic_index_in_dim(mod_table, level, 0, keepdims=False).astype(jnp.float32)
    scale_one, gate_one, scale_two, gate_two = (modulation[i] for i in range(4))
    mask_row = lax.dynamic_index_in_dim(context_mask, span_id, 0, keepdims=False)

    def allowed(places):
        return jnp.stack(
            [
                lax.dynamic_index_in_dim(mask_row, ((yl_id + dy) % 2) * 4 + (x_id + dx) % 4, 0, keepdims=False)
                for dy, dx in places
            ]
        )

    stream = latents.astype(jnp.float32)
    attn_own = (normed(stream) * (1.0 + scale_one)).astype(jnp.bfloat16)

    up_own = w_up.T
    up_first = gather_first(up_own, "x", "yl")
    near, away = gather_rows(attn_own)
    up_rest = gather_rest(*(after(t, near[3]) for t in up_first), "x", "yl")
    ups = [up_own, *up_first, *up_rest]

    q_near, kv_near = project(near, w_query, w_key, w_value, q_gain, k_gain)
    q_away, kv_away = project(away, w_query, w_key, w_value, q_gain, k_gain)
    queries = (q_near, q_away)
    first = [gather_first(t, "x", "yl") for t in (kv_near, kv_away)]
    rest = [gather_rest(*t, "x", "yl") for t in first]
    blocks = [(kv_near, kv_away)] + [tuple(f[i] for f in first) for i in range(3)]
    carry = attend(queries, blocks, allowed([(0, 0), (0, 1), (0, -1), (1, 0)]), None, False)
    blocks = [tuple(r[i] for r in rest) for i in range(4)]
    attended = attend(queries, blocks, allowed([(0, 2), (1, 1), (1, -1), (1, 2)]), carry, True)

    down_own = after(w_down, rest[1][3])
    down_first = gather_first(down_own, "x", "yl")
    part_away = project_out(attended, 1, w_out)
    part_near = project_out(attended, 0, w_out)
    attn_sum, tie = scatter_rows(part_near, part_away, rows)
    down_rest = gather_rest(*(after(t, tie) for t in down_first), "x", "yl")
    downs = [w_down, *down_first, *down_rest]
    resid = stream + gate_one * attn_sum
    mlp_own = (normed(resid) * (1.0 + scale_two)).astype(jnp.bfloat16)
    near, away = gather_rows(mlp_own)
    part_near = feed_forward(near, ups, downs)
    part_away = feed_forward(away, ups, downs)
    mlp_sum, _ = scatter_rows(part_near, part_away, rows)
    return (resid + gate_two * mlp_sum).astype(jnp.bfloat16)


def solution(mesh):
    fine = Mesh(mesh.devices.reshape([SIZES[a] for a in AXES]), AXES)
    head = ("z", "yh", "c")
    return jax.shard_map(
        on_device,
        mesh=fine,
        in_specs=(
            P(AXES, None),
            P(),
            P(),
            P(),
            P(None, head),
            P(None, head),
            P(None, head),
            P(),
            P(),
            P(head, None),
            P(None, AXES),
            P(AXES, None),
        ),
        out_specs=P(AXES, None),
        check_vma=False,
    )
```

```python
import functools

import jax
import jax.numpy as jnp
from jax import lax
from jax.experimental import pallas as pl
from jax.experimental.pallas import tpu as pltpu
from jax.sharding import Mesh, PartitionSpec as P

HD = 128
AXES = ("yl", "x", "z", "yh", "c")
SIZES = {"yl": 2, "x": 4, "z": 4, "yh": 2, "c": 2}
BLOCK = 1536
MIB = 1024 * 1024

epsilon = 1e-06


def normed(values):
    return values * lax.rsqrt(jnp.mean(values * values, axis=-1, keepdims=True) + epsilon)


def take_from(value, axis, offset):
    size = SIZES[axis]
    return lax.ppermute(value, axis, [((i + offset) % size, i) for i in range(size)])


def params():
    return pltpu.CompilerParams(vmem_limit_bytes=56 * MIB, dimension_semantics=("arbitrary",))


def stack(refs, pieces):
    return jnp.concatenate([refs[i][lo:hi, :] for i, lo, hi in pieces], axis=0)


def qkv_kernel(heads, pieces, count, *refs):
    x_refs, (wq, wk, wv, q_gain, k_gain), (q_ref, kv_ref, acc) = refs[:count], refs[count : count + 5], refs[-3:]
    k = pl.program_id(0)
    x = stack(x_refs, pieces)
    w = jnp.concatenate([wq[...], wk[...], wv[...]], axis=1)
    part = jnp.dot(x, w, preferred_element_type=jnp.float32)

    @pl.when(k == 0)
    def _():
        acc[...] = part

    @pl.when(k > 0)
    def _():
        acc[...] += part

    @pl.when(k == pl.num_programs(0) - 1)
    def _():
        width = heads * HD
        for h in range(heads):
            at = pl.ds(h * HD, HD)
            q_ref[:, at] = (normed(acc[:, at]) * q_gain[...]).astype(jnp.bfloat16)
            kv_ref[:, at] = (normed(acc[:, pl.ds(width + h * HD, HD)]) * k_gain[...]).astype(jnp.bfloat16)
        kv_ref[:, width:] = acc[:, 2 * width :].astype(jnp.bfloat16)


def project(chunk, place, earlier, wq, wk, wv, q_gain, k_gain):
    blocks, pieces = chunk
    depth, width = wq.shape
    rows = sum(hi - lo for _, lo, hi in pieces)
    heads = width // HD
    weight = pl.BlockSpec((BLOCK, width), lambda k: (k, 0))
    gain = pl.BlockSpec((1, HD), lambda k: (0, 0))
    ops = [*blocks, wq, wk, wv, q_gain.reshape(1, HD), k_gain.reshape(1, HD), *earlier]
    return pl.pallas_call(
        functools.partial(qkv_kernel, heads, pieces, len(blocks)),
        grid=(depth // BLOCK,),
        in_specs=[pl.BlockSpec((b.shape[0], BLOCK), lambda k: (0, k)) for b in blocks]
        + [weight] * 3
        + [gain] * 2
        + [pl.BlockSpec(memory_space=pl.ANY)] * len(earlier),
        out_specs=[
            pl.BlockSpec((rows, width), lambda k: (place, 0)),
            pl.BlockSpec((rows, 2 * width), lambda k: (place, 0)),
        ],
        out_shape=[
            jax.ShapeDtypeStruct((2 * rows, width), jnp.bfloat16),
            jax.ShapeDtypeStruct((2 * rows, 2 * width), jnp.bfloat16),
        ],
        input_output_aliases={len(ops) - 2 + i: i for i in range(len(earlier))},
        scratch_shapes=[pltpu.VMEM((rows, 3 * width), jnp.float32)],
        compiler_params=params(),
        cost_estimate=pl.CostEstimate(
            flops=6 * rows * depth * width, bytes_accessed=6 * depth * width + 2 * rows * depth, transcendentals=0
        ),
        name="project",
    )(*ops)


def attend_kernel(heads, count, first, last, *refs):
    allowed, q_ref, kv_refs, refs = refs[0], refs[1], refs[2 : 2 + count], refs[2 + count :]
    if not first:
        old_acc, old_sum, refs = refs[0], refs[1], refs[2:]
    if last:
        out_ref, acc, total = refs
    else:
        acc, total = refs
    rows = q_ref.shape[0]
    width = heads * HD
    if first:
        acc[...] = jnp.zeros_like(acc)
        total[...] = jnp.zeros_like(total)
    else:
        acc[...] = old_acc[...]
        total[...] = old_sum[...]
    factor = HD ** (-0.5) * 1.4426950408889634
    half = rows // 2
    for b in range(count):

        @pl.when(allowed[b + (0 if first else 4)] > 0)
        def _(b=b):
            for part in range(4):
                at = pl.ds(part // 2 * half, half)
                keys_at = pl.ds(part % 2 * half, half)
                for h in range(heads):
                    cols = pl.ds(h * HD, HD)
                    keys = kv_refs[b][keys_at, cols]
                    values = kv_refs[b][keys_at, pl.ds(width + h * HD, HD)]
                    scores = lax.dot_general(
                        q_ref[at, cols], keys, (((1,), (1,)), ((), ())), preferred_element_type=jnp.float32
                    )
                    probs = jnp.exp2(scores * factor)
                    lanes = probs[:, :HD]
                    for i in range(1, probs.shape[1] // HD):
                        lanes = lanes + probs[:, i * HD : (i + 1) * HD]
                    total[at, cols] += lanes
                    acc[at, cols] += jnp.dot(
                        probs.astype(jnp.bfloat16), values, preferred_element_type=jnp.float32
                    )

    if last:
        for h in range(heads):
            cols = pl.ds(h * HD, HD)
            denom = jnp.sum(total[:, cols], axis=-1, keepdims=True)
            out_ref[:, cols] = (acc[:, cols] / denom).astype(jnp.bfloat16)


def attend(queries, blocks, allowed, carry, last):
    rows, width = queries.shape
    heads = width // HD
    count = len(blocks)
    whole = pl.BlockSpec(memory_space=pltpu.VMEM)
    state = jax.ShapeDtypeStruct((rows, width), jnp.float32)
    ops = [allowed, queries, *blocks, *(carry or ())]
    if last:
        out_shape = jax.ShapeDtypeStruct((rows, width), jnp.bfloat16)
        scratch = [pltpu.VMEM(state.shape, jnp.float32)] * 2
        out_specs = whole
    else:
        out_shape, scratch, out_specs = [state, state], [], [whole, whole]
    return pl.pallas_call(
        functools.partial(attend_kernel, heads, count, carry is None, last),
        in_specs=[pl.BlockSpec(memory_space=pltpu.SMEM)] + [whole] * (len(ops) - 1),
        out_specs=out_specs,
        out_shape=out_shape,
        scratch_shapes=scratch,
        compiler_params=pltpu.CompilerParams(vmem_limit_bytes=32 * MIB),
        cost_estimate=pl.CostEstimate(
            flops=4 * count * rows * rows * width, bytes_accessed=4 * count * rows * width, transcendentals=0
        ),
        name="attend",
    )(*ops)


def out_kernel(a_ref, w_ref, keep_ref, send_ref):
    half = keep_ref.shape[0]
    r = jnp.dot(a_ref[...], w_ref[...], preferred_element_type=jnp.float32).astype(jnp.bfloat16)
    keep_ref[...] = r[:half]
    send_ref[...] = r[half:]


def project_out(attended, chunk, w_out):
    depth, width = w_out.shape
    rows = attended.shape[0] // 2
    return pl.pallas_call(
        out_kernel,
        grid=(width // BLOCK,),
        in_specs=[
            pl.BlockSpec((rows, depth), lambda n: (chunk, 0)),
            pl.BlockSpec((depth, BLOCK), lambda n: (0, n)),
        ],
        out_specs=[pl.BlockSpec((rows // 2, BLOCK), lambda n: (0, n))] * 2,
        out_shape=[jax.ShapeDtypeStruct((rows // 2, width), jnp.bfloat16)] * 2,
        compiler_params=params(),
        cost_estimate=pl.CostEstimate(
            flops=2 * rows * depth * width, bytes_accessed=2 * (depth + rows) * width, transcendentals=0
        ),
        name="project_out",
    )(attended, w_out)


def mlp_kernel(pieces, count, steps, *refs):
    x_refs, (up_ref, down_ref, keep_ref, send_ref, acc, hidden) = refs[:count], refs[count:]
    k = pl.program_id(0)

    @pl.when(k < steps)
    def _():
        x = stack(x_refs, pieces)
        part = lax.dot_general(x, up_ref[...], (((1,), (1,)), ((), ())), preferred_element_type=jnp.float32)

        @pl.when(k == 0)
        def _():
            acc[...] = part

        @pl.when(k > 0)
        def _():
            acc[...] += part

        @pl.when(k == steps - 1)
        def _():
            hidden[...] = jax.nn.gelu(acc[...], approximate=True).astype(jnp.bfloat16)

    @pl.when(k >= steps)
    def _():
        r = jnp.dot(hidden[...], down_ref[...], preferred_element_type=jnp.float32).astype(jnp.bfloat16)
        half = keep_ref.shape[0]
        keep_ref[...] = r[:half]
        send_ref[...] = r[half:]


def feed_forward(chunk, up, down):
    blocks, pieces = chunk
    units, width = up.shape
    rows = sum(hi - lo for _, lo, hi in pieces)
    steps = width // BLOCK
    first = lambda k: (0, jnp.minimum(k, steps - 1))
    second = lambda k: (0, jnp.maximum(k - steps, 0))
    return pl.pallas_call(
        functools.partial(mlp_kernel, pieces, len(blocks), steps),
        grid=(2 * steps,),
        in_specs=[pl.BlockSpec((b.shape[0], BLOCK), first) for b in blocks]
        + [pl.BlockSpec((units, BLOCK), first), pl.BlockSpec((units, BLOCK), second)],
        out_specs=[pl.BlockSpec((rows // 2, BLOCK), second)] * 2,
        out_shape=[jax.ShapeDtypeStruct((rows // 2, width), jnp.bfloat16)] * 2,
        scratch_shapes=[pltpu.VMEM((rows, units), jnp.float32), pltpu.VMEM((rows, units), jnp.bfloat16)],
        compiler_params=params(),
        cost_estimate=pl.CostEstimate(
            flops=4 * rows * units * width, bytes_accessed=4 * units * width + 4 * rows * width, transcendentals=rows * units
        ),
        name="feed_forward",
    )(*blocks, up, down)


def gather_first(own, ring, pair):
    return take_from(own, ring, 1), take_from(own, ring, -1), take_from(own, pair, 1)


def gather_rest(plus, minus, other, ring, pair):
    half = plus.shape[0] // 2
    first = take_from(plus[:half], ring, 1)
    second = take_from(minus[half:], ring, -1)
    other_plus = take_from(other, ring, 1)
    other_minus = take_from(other, ring, -1)
    far = jnp.concatenate([first, second])
    return far, other_plus, other_minus, take_from(far, pair, 1)


def gather_rows(own):
    n = own.shape[0]
    swap = lambda t: take_from(t, "c", 1)
    plus, minus, other = gather_first(own, "z", "yh")
    own_s = swap(own)
    far, other_plus, other_minus, other_far = gather_rest(plus, minus, other, "z", "yh")
    first_s = swap(jnp.concatenate([plus, minus, other]))
    far_s = swap(far)
    last_s = swap(jnp.concatenate([other_plus, other_minus, other_far]))
    whole = [(i, 0, n) for i in range(4)]
    near = [own, plus, minus, far, own_s, first_s, far_s]
    away = [other, other_plus, other_minus, other_far, first_s, last_s]
    return (near, [*whole, (4, 0, n), (5, 0, 2 * n), (6, 0, n)]), (away, [*whole, (4, 2 * n, 3 * n), (5, 0, 3 * n)])


def wide(t):
    return t.astype(jnp.float32)


def add(*terms):
    return functools.reduce(jnp.add, map(wide, terms)).astype(jnp.bfloat16)


def scatter_rows(near, away, rows):
    half = rows // 2
    cut = lambda t, i: t[i * rows : (i + 1) * rows]
    away_got = take_from(away[1], "c", 1)
    near_got = take_from(near[1], "c", 1)
    away_sum = [add(cut(away[0], i), cut(away_got, i)) for i in (1, 2, 3)]
    from_minus = take_from(away_sum[0], "z", -1)
    from_plus = take_from(away_sum[1], "z", 1)
    from_pair = take_from(away_sum[2], "yh", 1)
    far = add(cut(near[0], 3), cut(near_got, 3), from_pair)
    first = take_from(far[:half], "z", -1)
    second = take_from(far[half:], "z", 1)
    away_own = add(cut(away[0], 0), cut(away_got, 0), from_plus, from_minus)
    plus = wide(cut(near[0], 1)) + wide(cut(near_got, 1))
    minus = wide(cut(near[0], 2)) + wide(cut(near_got, 2))
    plus = jnp.concatenate([plus[:half] + wide(first), plus[half:]]).astype(jnp.bfloat16)
    minus = jnp.concatenate([minus[:half], minus[half:] + wide(second)]).astype(jnp.bfloat16)
    total = wide(cut(near[0], 0)) + wide(cut(near_got, 0))
    total = total + wide(take_from(plus, "z", -1)) + wide(take_from(minus, "z", 1))
    return total + wide(take_from(away_own, "yh", 1))


def on_device(
    latents,
    noise_level,
    context_mask,
    mod_table,
    w_query,
    w_key,
    w_value,
    q_gain,
    k_gain,
    w_out,
    w_up,
    w_down,
):
    rows = latents.shape[0]
    x_id, yl_id = lax.axis_index("x"), lax.axis_index("yl")
    span_id = yl_id * 4 + x_id
    level = lax.dynamic_index_in_dim(noise_level, span_id, 0, keepdims=False)
    modulation = lax.dynamic_index_in_dim(mod_table, level, 0, keepdims=False).astype(jnp.float32)
    scale_one, gate_one, scale_two, gate_two = (modulation[i] for i in range(4))
    mask_row = lax.dynamic_index_in_dim(context_mask, span_id, 0, keepdims=False)

    from_y = (yl_id + jnp.array([0, 0, 0, 1, 0, 1, 1, 1], jnp.int32)) % 2
    from_x = (x_id + jnp.array([0, 1, 3, 0, 2, 1, 3, 2], jnp.int32)) % 4
    match = (from_y * 4 + from_x)[:, None] == jnp.arange(8, dtype=jnp.int32)[None, :]
    allowed = jnp.sum(jnp.where(match, mask_row[None, :], 0), axis=1)

    up = lax.all_gather(w_up.T, ("yl", "x"), axis=0, tiled=True)
    down = lax.all_gather(w_down, ("yl", "x"), axis=0, tiled=True)

    stream = latents.astype(jnp.float32)
    attn_own = (normed(stream) * (1.0 + scale_one)).astype(jnp.bfloat16)
    near, away = gather_rows(attn_own)
    done = project(near, 0, (), w_query, w_key, w_value, q_gain, k_gain)
    queries, own_kv = project(away, 1, done, w_query, w_key, w_value, q_gain, k_gain)
    first = gather_first(own_kv, "x", "yl")
    rest = gather_rest(*first, "x", "yl")
    carry = attend(queries, [own_kv, *first], allowed, None, False)
    attended = attend(queries, rest, allowed, carry, True)

    part_away = project_out(attended, 1, w_out)
    part_near = project_out(attended, 0, w_out)
    attn_sum = scatter_rows(part_near, part_away, rows)
    resid = stream + gate_one * attn_sum
    mlp_own = (normed(resid) * (1.0 + scale_two)).astype(jnp.bfloat16)
    near, away = gather_rows(mlp_own)
    part_near = feed_forward(near, up, down)
    part_away = feed_forward(away, up, down)
    mlp_sum = scatter_rows(part_near, part_away, rows)
    return (resid + gate_two * mlp_sum).astype(jnp.bfloat16)


def solution(mesh):
    fine = Mesh(mesh.devices.reshape([SIZES[a] for a in AXES]), AXES)
    head = ("z", "yh", "c")
    return jax.shard_map(
        on_device,
        mesh=fine,
        in_specs=(
            P(AXES, None),
            P(),
            P(),
            P(),
            P(None, head),
            P(None, head),
            P(None, head),
            P(),
            P(),
            P(head, None),
            P(None, AXES),
            P(AXES, None),
        ),
        out_specs=P(AXES, None),
        check_vma=False,
    )
```

```python
import functools

import jax
import jax.numpy as jnp
from jax import lax
from jax.experimental import pallas as pl
from jax.experimental.pallas import tpu as pltpu
from jax.sharding import Mesh, PartitionSpec as P

HD = 128
AXES = ("yl", "x", "z", "yh", "c")
SIZES = {"yl": 2, "x": 4, "z": 4, "yh": 2, "c": 2}
BLOCK = 1536
MIB = 1024 * 1024

epsilon = 1e-06


def normed(values):
    return values * lax.rsqrt(jnp.mean(values * values, axis=-1, keepdims=True) + epsilon)


def take_from(value, axis, offset):
    size = SIZES[axis]
    return lax.ppermute(value, axis, [((i + offset) % size, i) for i in range(size)])


def params():
    return pltpu.CompilerParams(vmem_limit_bytes=56 * MIB, dimension_semantics=("arbitrary",))


def stack(refs, pieces):
    return jnp.concatenate([refs[i][lo:hi, :] for i, lo, hi in pieces], axis=0)


def qkv_kernel(heads, pieces, count, *refs):
    x_refs, (wq, wk, wv, q_gain, k_gain), (q_ref, kv_ref, acc) = refs[:count], refs[count : count + 5], refs[-3:]
    k = pl.program_id(0)
    x = stack(x_refs, pieces)
    w = jnp.concatenate([wq[...], wk[...], wv[...]], axis=1)
    part = jnp.dot(x, w, preferred_element_type=jnp.float32)

    @pl.when(k == 0)
    def _():
        acc[...] = part

    @pl.when(k > 0)
    def _():
        acc[...] += part

    @pl.when(k == pl.num_programs(0) - 1)
    def _():
        width = heads * HD
        for h in range(heads):
            at = pl.ds(h * HD, HD)
            q_ref[:, at] = (normed(acc[:, at]) * q_gain[...]).astype(jnp.bfloat16)
            kv_ref[:, at] = (normed(acc[:, pl.ds(width + h * HD, HD)]) * k_gain[...]).astype(jnp.bfloat16)
        kv_ref[:, width:] = acc[:, 2 * width :].astype(jnp.bfloat16)


def project(chunk, place, earlier, wq, wk, wv, q_gain, k_gain):
    blocks, pieces = chunk
    depth, width = wq.shape
    rows = sum(hi - lo for _, lo, hi in pieces)
    heads = width // HD
    weight = pl.BlockSpec((BLOCK, width), lambda k: (k, 0))
    gain = pl.BlockSpec((1, HD), lambda k: (0, 0))
    ops = [*blocks, wq, wk, wv, q_gain.reshape(1, HD), k_gain.reshape(1, HD), *earlier]
    return pl.pallas_call(
        functools.partial(qkv_kernel, heads, pieces, len(blocks)),
        grid=(depth // BLOCK,),
        in_specs=[pl.BlockSpec((b.shape[0], BLOCK), lambda k: (0, k)) for b in blocks]
        + [weight] * 3
        + [gain] * 2
        + [pl.BlockSpec(memory_space=pl.ANY)] * len(earlier),
        out_specs=[
            pl.BlockSpec((rows, width), lambda k: (place, 0)),
            pl.BlockSpec((rows, 2 * width), lambda k: (place, 0)),
        ],
        out_shape=[
            jax.ShapeDtypeStruct((2 * rows, width), jnp.bfloat16),
            jax.ShapeDtypeStruct((2 * rows, 2 * width), jnp.bfloat16),
        ],
        input_output_aliases={len(ops) - 2 + i: i for i in range(len(earlier))},
        scratch_shapes=[pltpu.VMEM((rows, 3 * width), jnp.float32)],
        compiler_params=params(),
        cost_estimate=pl.CostEstimate(
            flops=6 * rows * depth * width, bytes_accessed=6 * depth * width + 2 * rows * depth, transcendentals=0
        ),
        name="project",
    )(*ops)


def attend_kernel(heads, count, first, last, *refs):
    allowed, q_ref, kv_refs, refs = refs[0], refs[1], refs[2 : 2 + count], refs[2 + count :]
    if not first:
        old_acc, old_sum, refs = refs[0], refs[1], refs[2:]
    if last:
        out_ref, acc, total = refs
    else:
        acc, total = refs
    rows = q_ref.shape[0]
    width = heads * HD
    if first:
        acc[...] = jnp.zeros_like(acc)
        total[...] = jnp.zeros_like(total)
    else:
        acc[...] = old_acc[...]
        total[...] = old_sum[...]
    factor = HD ** (-0.5) * 1.4426950408889634
    half = rows // 2
    for b in range(count):

        @pl.when(allowed[b + (0 if first else 4)] > 0)
        def _(b=b):
            for part in range(4):
                at = pl.ds(part // 2 * half, half)
                keys_at = pl.ds(part % 2 * half, half)
                for h in range(heads):
                    cols = pl.ds(h * HD, HD)
                    keys = kv_refs[b][keys_at, cols]
                    values = kv_refs[b][keys_at, pl.ds(width + h * HD, HD)]
                    scores = lax.dot_general(
                        q_ref[at, cols], keys, (((1,), (1,)), ((), ())), preferred_element_type=jnp.float32
                    )
                    probs = jnp.exp2(scores * factor)
                    lanes = probs[:, :HD]
                    for i in range(1, probs.shape[1] // HD):
                        lanes = lanes + probs[:, i * HD : (i + 1) * HD]
                    total[at, cols] += lanes
                    acc[at, cols] += jnp.dot(
                        probs.astype(jnp.bfloat16), values, preferred_element_type=jnp.float32
                    )

    if last:
        for h in range(heads):
            cols = pl.ds(h * HD, HD)
            denom = jnp.sum(total[:, cols], axis=-1, keepdims=True)
            out_ref[:, cols] = (acc[:, cols] / denom).astype(jnp.bfloat16)


def attend(queries, blocks, allowed, carry, last):
    rows, width = queries.shape
    heads = width // HD
    count = len(blocks)
    whole = pl.BlockSpec(memory_space=pltpu.VMEM)
    state = jax.ShapeDtypeStruct((rows, width), jnp.float32)
    ops = [allowed, queries, *blocks, *(carry or ())]
    if last:
        out_shape = jax.ShapeDtypeStruct((rows, width), jnp.bfloat16)
        scratch = [pltpu.VMEM(state.shape, jnp.float32)] * 2
        out_specs = whole
    else:
        out_shape, scratch, out_specs = [state, state], [], [whole, whole]
    return pl.pallas_call(
        functools.partial(attend_kernel, heads, count, carry is None, last),
        in_specs=[pl.BlockSpec(memory_space=pltpu.SMEM)] + [whole] * (len(ops) - 1),
        out_specs=out_specs,
        out_shape=out_shape,
        scratch_shapes=scratch,
        compiler_params=pltpu.CompilerParams(vmem_limit_bytes=32 * MIB),
        cost_estimate=pl.CostEstimate(
            flops=4 * count * rows * rows * width, bytes_accessed=4 * count * rows * width, transcendentals=0
        ),
        name="attend",
    )(*ops)


def out_kernel(a_ref, w_ref, keep_ref, send_ref):
    half = keep_ref.shape[0]
    r = jnp.dot(a_ref[...], w_ref[...], preferred_element_type=jnp.float32).astype(jnp.bfloat16)
    keep_ref[...] = r[:half]
    send_ref[...] = r[half:]


def project_out(attended, chunk, w_out):
    depth, width = w_out.shape
    rows = attended.shape[0] // 2
    return pl.pallas_call(
        out_kernel,
        grid=(width // BLOCK,),
        in_specs=[
            pl.BlockSpec((rows, depth), lambda n: (chunk, 0)),
            pl.BlockSpec((depth, BLOCK), lambda n: (0, n)),
        ],
        out_specs=[pl.BlockSpec((rows // 2, BLOCK), lambda n: (0, n))] * 2,
        out_shape=[jax.ShapeDtypeStruct((rows // 2, width), jnp.bfloat16)] * 2,
        compiler_params=params(),
        cost_estimate=pl.CostEstimate(
            flops=2 * rows * depth * width, bytes_accessed=2 * (depth + rows) * width, transcendentals=0
        ),
        name="project_out",
    )(attended, w_out)


def mlp_kernel(count, steps, *refs):
    x_refs, (up_ref, down_ref), refs = refs[:count], refs[count : count + 2], refs[count + 2 :]
    out_refs, (acc, hidden) = refs[:count], refs[count:]
    k = pl.program_id(0)

    @pl.when(k < steps)
    def _():
        x = jnp.concatenate([r[...] for r in x_refs], axis=0)
        part = lax.dot_general(x, up_ref[...], (((1,), (1,)), ((), ())), preferred_element_type=jnp.float32)

        @pl.when(k == 0)
        def _():
            acc[...] = part

        @pl.when(k > 0)
        def _():
            acc[...] += part

        @pl.when(k == steps - 1)
        def _():
            hidden[...] = jax.nn.gelu(acc[...], approximate=True).astype(jnp.bfloat16)

    @pl.when(k >= steps)
    def _():
        r = jnp.dot(hidden[...], down_ref[...], preferred_element_type=jnp.float32).astype(jnp.bfloat16)
        at = 0
        for out_ref in out_refs:
            n = out_ref.shape[0]
            out_ref[...] = r[at : at + n]
            at += n


def feed_forward(blocks, up, down):
    units, width = up.shape
    rows = sum(b.shape[0] for b in blocks)
    cut = width // 2
    steps = width // cut
    first = lambda k: (0, jnp.minimum(k, steps - 1))
    second = lambda k: (0, jnp.maximum(k - steps, 0))
    return pl.pallas_call(
        functools.partial(mlp_kernel, len(blocks), steps),
        grid=(2 * steps,),
        in_specs=[pl.BlockSpec((b.shape[0], cut), first) for b in blocks]
        + [pl.BlockSpec((units, cut), first), pl.BlockSpec((units, cut), second)],
        out_specs=[pl.BlockSpec((b.shape[0], cut), second) for b in blocks],
        out_shape=[jax.ShapeDtypeStruct(b.shape, jnp.bfloat16) for b in blocks],
        scratch_shapes=[pltpu.VMEM((rows, units), jnp.float32), pltpu.VMEM((rows, units), jnp.bfloat16)],
        compiler_params=params(),
        cost_estimate=pl.CostEstimate(
            flops=4 * rows * units * width, bytes_accessed=4 * units * width + 4 * rows * width, transcendentals=rows * units
        ),
        name="feed_forward",
    )(*blocks, up, down)


def tie_kernel(*refs):
    pass


def tie(values, token):
    anywhere = pl.BlockSpec(memory_space=pl.ANY)
    return pl.pallas_call(
        tie_kernel,
        in_specs=[anywhere] * (len(values) + 1),
        out_specs=[anywhere] * len(values),
        out_shape=[jax.ShapeDtypeStruct(v.shape, v.dtype) for v in values],
        input_output_aliases={i: i for i in range(len(values))},
        name="tie",
    )(*values, token)


def gather_first(own, ring, pair):
    return take_from(own, ring, 1), take_from(own, ring, -1), take_from(own, pair, 1)


def gather_rest(plus, minus, other, ring, pair):
    half = plus.shape[0] // 2
    first = take_from(plus[:half], ring, 1)
    second = take_from(minus[half:], ring, -1)
    other_plus = take_from(other, ring, 1)
    other_minus = take_from(other, ring, -1)
    far = jnp.concatenate([first, second])
    return far, other_plus, other_minus, take_from(far, pair, 1)


def gather_rows(own):
    n = own.shape[0]
    swap = lambda t: take_from(t, "c", 1)
    plus, minus, other = gather_first(own, "z", "yh")
    own_s = swap(own)
    far, other_plus, other_minus, other_far = gather_rest(plus, minus, other, "z", "yh")
    first_s = swap(jnp.concatenate([plus, minus, other]))
    far_s = swap(far)
    last_s = swap(jnp.concatenate([other_plus, other_minus, other_far]))
    whole = [(i, 0, n) for i in range(4)]
    near = [own, plus, minus, far, own_s, first_s, far_s]
    away = [other, other_plus, other_minus, other_far, first_s, last_s]
    return (near, [*whole, (4, 0, n), (5, 0, 2 * n), (6, 0, n)]), (away, [*whole, (4, 2 * n, 3 * n), (5, 0, 3 * n)])


def move(value, stage, offset):
    pairs = []
    at = lambda yl, z, yh, c: ((yl * 4 + z) * 2 + yh) * 2 + c
    for y in range(4):
        for z in range(4):
            for c in range(2):
                if (c + stage) % 2 == 0:
                    from_y, from_z = y, (z + offset) % 4
                else:
                    from_y, from_z = (y + offset) % 4, z
                pairs.append((at(from_y % 2, from_z, from_y // 2, c), at(y % 2, z, y // 2, c)))
    return lax.ppermute(value, ("yl", "z", "yh", "c"), pairs)


def gather_ring(own, get):
    half = own.shape[0] // 2
    plus = get(own, 1)
    minus = get(own, -1)
    return plus, minus, get(plus[:half], 1), get(minus[half:], -1)


def gather_wide(own):
    swap = lambda t: take_from(t, "c", 1)
    ring = jnp.concatenate([own, *gather_ring(own, lambda t, d: move(t, 0, d))])
    plus, minus, far_a, far_b = gather_ring(ring, lambda t, d: move(t, 1, d))
    return [ring, swap(ring)], [plus, minus, swap(plus), swap(minus)], [far_a, far_b, swap(far_a), swap(far_b)]


def scatter_wide(ring, near, far):
    swap = lambda t: take_from(t, "c", 1)
    far_a = add(far[0], swap(far[2]))
    far_b = add(far[1], swap(far[3]))
    got_a = move(far_a, 1, -1)
    got_b = move(far_b, 1, 1)
    plus_s, minus_s, ring_s = swap(near[2]), swap(near[3]), swap(ring[1])
    half = far_a.shape[0]
    plus = jnp.concatenate([add(near[0][:half], plus_s[:half], got_a), add(near[0][half:], plus_s[half:])])
    minus = jnp.concatenate([add(near[1][:half], minus_s[:half]), add(near[1][half:], minus_s[half:], got_b)])
    got_plus = move(plus, 1, -1)
    got_minus = move(minus, 1, 1)
    rows = ring[0].shape[0] // 4
    total = lambda lo, hi: functools.reduce(
        jnp.add, [wide(t[lo:hi]) for t in (ring[0], ring_s, got_plus, got_minus)]
    )
    narrow = lambda t: t.astype(jnp.bfloat16)
    half = rows // 2
    far_a = narrow(total(3 * rows, 3 * rows + half))
    far_b = narrow(total(3 * rows + half, 4 * rows))
    got_a = move(far_a, 0, -1)
    got_b = move(far_b, 0, 1)
    plus = narrow(
        jnp.concatenate([total(rows, rows + half) + wide(got_a), total(rows + half, 2 * rows)])
    )
    minus = narrow(
        jnp.concatenate([total(2 * rows, 2 * rows + half), total(2 * rows + half, 3 * rows) + wide(got_b)])
    )
    return total(0, rows) + wide(move(plus, 0, -1)) + wide(move(minus, 0, 1))


def wide(t):
    return t.astype(jnp.float32)


def add(*terms):
    return functools.reduce(jnp.add, map(wide, terms)).astype(jnp.bfloat16)


def scatter_rows(near, away, rows):
    half = rows // 2
    cut = lambda t, i: t[i * rows : (i + 1) * rows]
    away_got = take_from(away[1], "c", 1)
    near_got = take_from(near[1], "c", 1)
    away_sum = [add(cut(away[0], i), cut(away_got, i)) for i in (1, 2, 3)]
    from_minus = take_from(away_sum[0], "z", -1)
    from_plus = take_from(away_sum[1], "z", 1)
    from_pair = take_from(away_sum[2], "yh", 1)
    far = add(cut(near[0], 3), cut(near_got, 3), from_pair)
    first = take_from(far[:half], "z", -1)
    second = take_from(far[half:], "z", 1)
    away_own = add(cut(away[0], 0), cut(away_got, 0), from_plus, from_minus)
    plus = wide(cut(near[0], 1)) + wide(cut(near_got, 1))
    minus = wide(cut(near[0], 2)) + wide(cut(near_got, 2))
    plus = jnp.concatenate([plus[:half] + wide(first), plus[half:]]).astype(jnp.bfloat16)
    minus = jnp.concatenate([minus[:half], minus[half:] + wide(second)]).astype(jnp.bfloat16)
    total = wide(cut(near[0], 0)) + wide(cut(near_got, 0))
    total = total + wide(take_from(plus, "z", -1)) + wide(take_from(minus, "z", 1))
    return total + wide(take_from(away_own, "yh", 1)), from_pair


def on_device(
    latents,
    noise_level,
    context_mask,
    mod_table,
    w_query,
    w_key,
    w_value,
    q_gain,
    k_gain,
    w_out,
    w_up,
    w_down,
):
    rows = latents.shape[0]
    x_id, yl_id = lax.axis_index("x"), lax.axis_index("yl")
    span_id = yl_id * 4 + x_id
    level = lax.dynamic_index_in_dim(noise_level, span_id, 0, keepdims=False)
    modulation = lax.dynamic_index_in_dim(mod_table, level, 0, keepdims=False).astype(jnp.float32)
    scale_one, gate_one, scale_two, gate_two = (modulation[i] for i in range(4))
    mask_row = lax.dynamic_index_in_dim(context_mask, span_id, 0, keepdims=False)

    from_y = (yl_id + jnp.array([0, 0, 0, 1, 0, 1, 1, 1], jnp.int32)) % 2
    from_x = (x_id + jnp.array([0, 1, 3, 0, 2, 1, 3, 2], jnp.int32)) % 4
    match = (from_y * 4 + from_x)[:, None] == jnp.arange(8, dtype=jnp.int32)[None, :]
    allowed = jnp.sum(jnp.where(match, mask_row[None, :], 0), axis=1)

    units = w_up.shape[1]
    along = lambda t, d: take_from(t, "x", d)
    up_own = w_up.T
    up_plus, up_minus = along(up_own, 1), along(up_own, -1)

    stream = latents.astype(jnp.float32)
    attn_own = (normed(stream) * (1.0 + scale_one)).astype(jnp.bfloat16)
    near, away = gather_rows(attn_own)
    halves = tie([up_plus[: units // 2], up_minus[units // 2 :]], near[0][3])
    up = jnp.concatenate([up_own, up_plus, up_minus, along(halves[0], 1), along(halves[1], -1)])
    done = project(near, 0, (), w_query, w_key, w_value, q_gain, k_gain)
    queries, own_kv = project(away, 1, done, w_query, w_key, w_value, q_gain, k_gain)
    first = gather_first(own_kv, "x", "yl")
    rest = gather_rest(*first, "x", "yl")
    carry = attend(queries, [own_kv, *first], allowed, None, False)
    attended = attend(queries, rest, allowed, carry, True)

    down_own = tie([w_down], rest[3])[0]
    down_plus, down_minus = along(down_own, 1), along(down_own, -1)
    part_away = project_out(attended, 1, w_out)
    part_near = project_out(attended, 0, w_out)
    attn_sum, token = scatter_rows(part_near, part_away, rows)
    halves = tie([down_plus[: units // 2], down_minus[units // 2 :]], token)
    down = jnp.concatenate([down_own, down_plus, down_minus, along(halves[0], 1), along(halves[1], -1)])
    resid = stream + gate_one * attn_sum
    mlp_own = (normed(resid) * (1.0 + scale_two)).astype(jnp.bfloat16)
    parts = [feed_forward(blocks, up, down) for blocks in gather_wide(mlp_own)]
    mlp_sum = scatter_wide(*parts)
    return (resid + gate_two * mlp_sum).astype(jnp.bfloat16)


def solution(mesh):
    fine = Mesh(mesh.devices.reshape([SIZES[a] for a in AXES]), AXES)
    head = ("z", "yh", "c")
    return jax.shard_map(
        on_device,
        mesh=fine,
        in_specs=(
            P(AXES, None),
            P(),
            P(),
            P(),
            P(None, head),
            P(None, head),
            P(None, head),
            P(),
            P(),
            P(head, None),
            P(None, AXES),
            P(AXES, None),
        ),
        out_specs=P(AXES, None),
        check_vma=False,
    )
```

```python
import functools

import jax
import jax.numpy as jnp
from jax import lax
from jax.experimental import pallas as pl
from jax.experimental.pallas import tpu as pltpu
from jax.sharding import Mesh, PartitionSpec as P

HD = 128
AXES = ("yl", "x", "z", "yh", "c")
SIZES = {"yl": 2, "x": 4, "z": 4, "yh": 2, "c": 2}
MIB = 1024 * 1024

epsilon = 1e-06


def normed(values):
    return values * lax.rsqrt(jnp.mean(values * values, axis=-1, keepdims=True) + epsilon)


def take_from(value, axis, offset):
    size = SIZES[axis]
    return lax.ppermute(value, axis, [((i + offset) % size, i) for i in range(size)])


def params(mib=24):
    return pltpu.CompilerParams(vmem_limit_bytes=mib * MIB)


def cost(flops):
    return pl.CostEstimate(flops=flops // 5, bytes_accessed=0, transcendentals=0)


def in_vmem(value):
    return pltpu.with_memory_space_constraint(value, pltpu.VMEM)


ANYWHERE = pl.BlockSpec(memory_space=pl.ANY)
WHOLE = pl.BlockSpec(memory_space=pltpu.VMEM)


def stack(refs, pieces):
    return jnp.concatenate([refs[i][lo:hi, :] for i, lo, hi in pieces], axis=0)


def join_kernel(places, count, *refs):
    sources, (out_ref, _, sems) = refs[:count], refs[-3:]
    copies = [
        pltpu.make_async_copy(
            source.at[pl.ds(0, source.shape[0]), :],
            out_ref.at[pl.ds(row, source.shape[0]), pl.ds(col, source.shape[1])],
            sems.at[i],
        )
        for i, (source, (row, col)) in enumerate(zip(sources, places))
    ]
    for copy in copies:
        copy.start()
    for copy in copies:
        copy.wait()


def join(pieces, axis=0, vmem=False, tokens=()):
    places, at = [], 0
    for piece in pieces:
        places.append((0, at) if axis else (at, 0))
        at += piece.shape[axis]
    shape = (pieces[0].shape[0], at) if axis else (at, pieces[0].shape[1])
    make = pltpu.VMEM if vmem else jax.ShapeDtypeStruct
    return pl.pallas_call(
        functools.partial(join_kernel, places, len(pieces)),
        in_specs=[ANYWHERE] * (len(pieces) + len(tokens)),
        out_specs=[WHOLE if vmem else ANYWHERE, ANYWHERE],
        out_shape=[make(shape, jnp.bfloat16), jax.ShapeDtypeStruct((8, 128), jnp.float32)],
        scratch_shapes=[pltpu.SemaphoreType.DMA((len(pieces),))],
        compiler_params=params(),
        cost_estimate=cost(1),
        name="join",
    )(*pieces, *tokens)


def tie_kernel(*refs):
    pass


def tie(values, *tokens):
    return pl.pallas_call(
        tie_kernel,
        in_specs=[ANYWHERE] * (len(values) + len(tokens)),
        out_specs=[ANYWHERE] * len(values),
        out_shape=[jax.ShapeDtypeStruct(v.shape, v.dtype) for v in values],
        input_output_aliases={i: i for i in range(len(values))},
        cost_estimate=cost(1),
        name="tie",
    )(*values, *tokens)


def stack(refs, pieces):
    return jnp.concatenate([refs[i][lo:hi, :] for i, lo, hi in pieces], axis=0)


def qkv_kernel(heads, pieces, count, *refs):
    x_refs, (w_ref, q_gain, k_gain), (q_ref, kv_ref, acc) = refs[:count], refs[count : count + 3], refs[-3:]
    k = pl.program_id(0)
    x = stack(x_refs, pieces)
    at = pl.ds(pl.multiple_of(k * x.shape[1], x.shape[1]), x.shape[1])
    part = jnp.dot(x, w_ref[at, :], preferred_element_type=jnp.float32)

    @pl.when(k == 0)
    def _():
        acc[...] = part

    @pl.when(k > 0)
    def _():
        acc[...] += part

    @pl.when(k == pl.num_programs(0) - 1)
    def _():
        width = heads * HD
        for h in range(heads):
            at = pl.ds(h * HD, HD)
            q_ref[:, at] = (normed(acc[:, at]) * q_gain[...]).astype(jnp.bfloat16)
            kv_ref[:, at] = (normed(acc[:, pl.ds(width + h * HD, HD)]) * k_gain[...]).astype(jnp.bfloat16)
        kv_ref[:, width:] = acc[:, 2 * width :].astype(jnp.bfloat16)


def project(chunk, place, earlier, w, q_gain, k_gain):
    blocks, pieces = chunk
    depth, width = w.shape[0], w.shape[1] // 3
    rows = sum(hi - lo for _, lo, hi in pieces)
    heads = width // HD
    cut = depth // 2
    gain = pl.BlockSpec((1, HD), lambda k: (0, 0))
    ops = [*blocks, in_vmem(w), q_gain.reshape(1, HD), k_gain.reshape(1, HD), *earlier]
    return pl.pallas_call(
        functools.partial(qkv_kernel, heads, pieces, len(blocks)),
        grid=(depth // cut,),
        in_specs=[pl.BlockSpec((b.shape[0], cut), lambda k: (0, k)) for b in blocks]
        + [WHOLE, gain, gain]
        + [ANYWHERE] * len(earlier),
        out_specs=[
            pl.BlockSpec((rows, width), lambda k: (place, 0)),
            pl.BlockSpec((rows, 2 * width), lambda k: (place, 0)),
        ],
        out_shape=[
            jax.ShapeDtypeStruct((2 * rows, width), jnp.bfloat16),
            jax.ShapeDtypeStruct((2 * rows, 2 * width), jnp.bfloat16),
        ],
        input_output_aliases={len(ops) - 2 + i: i for i in range(len(earlier))},
        scratch_shapes=[pltpu.VMEM((rows, 3 * width), jnp.float32)],
        compiler_params=params(),
        cost_estimate=cost(6 * rows * depth * width),
        name="project",
    )(*ops)


def attend_kernel(heads, count, first, last, *refs):
    allowed, q_ref, kv_refs, refs = refs[0], refs[1], refs[2 : 2 + count], refs[2 + count :]
    if not first:
        old_acc, old_sum, refs = refs[0], refs[1], refs[2:]
    if last:
        out_ref, acc, total = refs
    else:
        acc, total = refs
    rows = q_ref.shape[0]
    width = heads * HD
    if first:
        acc[...] = jnp.zeros_like(acc)
        total[...] = jnp.zeros_like(total)
    else:
        acc[...] = old_acc[...]
        total[...] = old_sum[...]
    factor = HD ** (-0.5) * 1.4426950408889634
    half = rows // 2
    for b in range(count):

        @pl.when(allowed[b + (0 if first else 4)] > 0)
        def _(b=b):
            for part in range(4):
                at = pl.ds(part // 2 * half, half)
                keys_at = pl.ds(part % 2 * half, half)
                for h in range(heads):
                    cols = pl.ds(h * HD, HD)
                    keys = kv_refs[b][keys_at, cols]
                    values = kv_refs[b][keys_at, pl.ds(width + h * HD, HD)]
                    scores = lax.dot_general(
                        q_ref[at, cols], keys, (((1,), (1,)), ((), ())), preferred_element_type=jnp.float32
                    )
                    probs = jnp.exp2(scores * factor)
                    lanes = probs[:, :HD]
                    for i in range(1, probs.shape[1] // HD):
                        lanes = lanes + probs[:, i * HD : (i + 1) * HD]
                    total[at, cols] += lanes
                    acc[at, cols] += jnp.dot(
                        probs.astype(jnp.bfloat16), values, preferred_element_type=jnp.float32
                    )

    if last:
        for h in range(heads):
            cols = pl.ds(h * HD, HD)
            denom = jnp.sum(total[:, cols], axis=-1, keepdims=True)
            out_ref[:, cols] = (acc[:, cols] / denom).astype(jnp.bfloat16)


def attend(queries, blocks, allowed, carry, last):
    rows, width = queries.shape
    heads = width // HD
    count = len(blocks)
    whole = WHOLE
    state = jax.ShapeDtypeStruct((rows, width), jnp.float32)
    ops = [allowed, queries, *blocks, *(carry or ())]
    if last:
        out_shape = jax.ShapeDtypeStruct((rows, width), jnp.bfloat16)
        scratch = [pltpu.VMEM(state.shape, jnp.float32)] * 2
        out_specs = whole
    else:
        out_shape, scratch, out_specs = [state, state], [], [whole, whole]
    return pl.pallas_call(
        functools.partial(attend_kernel, heads, count, carry is None, last),
        in_specs=[pl.BlockSpec(memory_space=pltpu.SMEM)] + [whole] * (len(ops) - 1),
        out_specs=out_specs,
        out_shape=out_shape,
        scratch_shapes=scratch,
        compiler_params=params(),
        cost_estimate=cost(4 * count * rows * rows * width),
        name="attend",
    )(*ops)


def out_kernel(a_ref, w_ref, keep_ref, send_ref):
    half, cut = keep_ref.shape
    at = pl.ds(pl.multiple_of(pl.program_id(0) * cut, cut), cut)
    r = jnp.dot(a_ref[...], w_ref[:, at], preferred_element_type=jnp.float32).astype(jnp.bfloat16)
    keep_ref[...] = r[:half]
    send_ref[...] = r[half:]


def project_out(attended, chunk, w_out):
    depth, width = w_out.shape
    rows = attended.shape[0] // 2
    cut = width // 2
    return pl.pallas_call(
        out_kernel,
        grid=(width // cut,),
        in_specs=[pl.BlockSpec((rows, depth), lambda n: (chunk, 0)), WHOLE],
        out_specs=[pl.BlockSpec((rows // 2, cut), lambda n: (0, n))] * 2,
        out_shape=[jax.ShapeDtypeStruct((rows // 2, width), jnp.bfloat16)] * 2,
        compiler_params=params(),
        cost_estimate=cost(2 * rows * depth * width),
        name="project_out",
    )(attended, in_vmem(w_out))


def mlp_kernel(count, steps, *refs):
    x_refs, (up_ref, down_ref), refs = refs[:count], refs[count : count + 2], refs[count + 2 :]
    out_refs, (acc, hidden) = refs[:count], refs[count:]
    k = pl.program_id(0)
    cut = x_refs[0].shape[1]
    cols = pl.ds(pl.multiple_of(lax.rem(k, steps) * cut, cut), cut)

    @pl.when(k < steps)
    def _():
        x = jnp.concatenate([r[...] for r in x_refs], axis=0)
        part = lax.dot_general(x, up_ref[:, cols], (((1,), (1,)), ((), ())), preferred_element_type=jnp.float32)

        @pl.when(k == 0)
        def _():
            acc[...] = part

        @pl.when(k > 0)
        def _():
            acc[...] += part

        @pl.when(k == steps - 1)
        def _():
            hidden[...] = jax.nn.gelu(acc[...], approximate=True).astype(jnp.bfloat16)

    @pl.when(k >= steps)
    def _():
        r = jnp.dot(hidden[...], down_ref[:, cols], preferred_element_type=jnp.float32).astype(jnp.bfloat16)
        at = 0
        for out_ref in out_refs:
            n = out_ref.shape[0]
            out_ref[...] = r[at : at + n]
            at += n


def feed_forward(blocks, up, down):
    units, width = up.shape
    rows = sum(b.shape[0] for b in blocks)
    cut = width // 2
    steps = width // cut
    first = lambda k: (0, jnp.minimum(k, steps - 1))
    second = lambda k: (0, jnp.maximum(k - steps, 0))
    return pl.pallas_call(
        functools.partial(mlp_kernel, len(blocks), steps),
        grid=(2 * steps,),
        in_specs=[pl.BlockSpec((b.shape[0], cut), first) for b in blocks] + [WHOLE, WHOLE],
        out_specs=[pl.BlockSpec((b.shape[0], cut), second) for b in blocks],
        out_shape=[jax.ShapeDtypeStruct(b.shape, jnp.bfloat16) for b in blocks],
        scratch_shapes=[pltpu.VMEM((rows, units), jnp.float32), pltpu.VMEM((rows, units), jnp.bfloat16)],
        compiler_params=params(),
        cost_estimate=cost(4 * rows * units * width),
        name="feed_forward",
    )(*blocks, in_vmem(up), in_vmem(down))


def swap(value):
    return take_from(value, "c", 1)


def gather_first(own, ring, pair):
    return take_from(own, ring, 1), take_from(own, ring, -1), take_from(own, pair, 1)


def gather_rest(plus, minus, other, ring, pair, *tokens):
    half = plus.shape[0] // 2
    halves = tie([plus[:half], minus[half:]], *tokens)
    first = take_from(halves[0], ring, 1)
    second = take_from(halves[1], ring, -1)
    other_plus = take_from(other, ring, 1)
    other_minus = take_from(other, ring, -1)
    far, _ = join([first, second])
    return far, other_plus, other_minus, take_from(far, pair, 1)


def move(value, stage, offset):
    pairs = []
    at = lambda yl, z, yh, c: ((yl * 4 + z) * 2 + yh) * 2 + c
    for y in range(4):
        for z in range(4):
            for c in range(2):
                if (c + stage) % 2 == 0:
                    from_y, from_z = y, (z + offset) % 4
                else:
                    from_y, from_z = (y + offset) % 4, z
                pairs.append((at(from_y % 2, from_z, from_y // 2, c), at(y % 2, z, y // 2, c)))
    return lax.ppermute(value, ("yl", "z", "yh", "c"), pairs)


def wide(t):
    return t.astype(jnp.float32)


def add(*terms):
    return functools.reduce(jnp.add, map(wide, terms)).astype(jnp.bfloat16)


def scatter_rows(near, away, rows, tokens):
    half = rows // 2
    cut = lambda t, i: t[i * rows : (i + 1) * rows]
    away_got = take_from(away[1], "c", 1)
    near_got = take_from(near[1], "c", 1)
    away_sum = [add(cut(away[0], i), cut(away_got, i)) for i in (1, 2, 3)]
    from_minus = take_from(away_sum[0], "z", -1)
    from_plus = take_from(away_sum[1], "z", 1)
    from_pair = take_from(away_sum[2], "yh", 1)
    far = add(cut(near[0], 3), cut(near_got, 3), from_pair)
    halves = tie([far[:half], far[half:]], *tokens)
    first = take_from(halves[0], "z", -1)
    second = take_from(halves[1], "z", 1)
    away_own = add(cut(away[0], 0), cut(away_got, 0), from_plus, from_minus)
    plus = wide(cut(near[0], 1)) + wide(cut(near_got, 1))
    minus = wide(cut(near[0], 2)) + wide(cut(near_got, 2))
    plus = jnp.concatenate([plus[:half] + wide(first), plus[half:]]).astype(jnp.bfloat16)
    minus = jnp.concatenate([minus[:half], minus[half:] + wide(second)]).astype(jnp.bfloat16)
    total = wide(cut(near[0], 0)) + wide(cut(near_got, 0))
    total = total + wide(take_from(plus, "z", -1)) + wide(take_from(minus, "z", 1))
    return total + wide(take_from(away_own, "yh", 1)), first


def scatter_wide(ring_a, ring_b, plus, minus, far):
    far_a = add(far[0], swap(far[2]))
    far_b = add(far[1], swap(far[3]))
    got_a = move(far_a, 1, -1)
    got_b = move(far_b, 1, 1)
    plus_b = add(plus[1], swap(plus[3]))
    minus_a = add(minus[0], swap(minus[2]))
    got_plus_b = move(plus_b, 1, -1)
    got_minus_a = move(minus_a, 1, 1)
    plus_a = add(plus[0], swap(plus[2]), got_a)
    minus_b = add(minus[1], swap(minus[3]), got_b)
    ring_a_s, ring_b_s = swap(ring_a[1]), swap(ring_b[1])
    got_minus_b = move(minus_b, 1, 1)
    got_plus_a = move(plus_a, 1, -1)
    rows = ring_a[0].shape[0] // 2
    total = lambda terms, lo, hi: functools.reduce(jnp.add, [wide(t[lo:hi]) for t in terms])
    narrow = lambda t: t.astype(jnp.bfloat16)
    top = ring_a[0], ring_a_s, got_plus_a, got_minus_a
    low = ring_b[0], ring_b_s, got_plus_b, got_minus_b
    half = rows // 2
    got_a = move(narrow(total(low, rows, rows + half)), 0, -1)
    got_b = move(narrow(total(low, rows + half, 2 * rows)), 0, 1)
    plus = jnp.concatenate([total(top, rows, rows + half) + wide(got_a), total(top, rows + half, 2 * rows)])
    minus = jnp.concatenate([total(low, 0, half), total(low, half, rows) + wide(got_b)])
    own = total(top, 0, rows)
    return own + wide(move(narrow(plus), 0, -1)) + wide(move(narrow(minus), 0, 1))


def on_device(
    latents,
    noise_level,
    context_mask,
    mod_table,
    w_query,
    w_key,
    w_value,
    q_gain,
    k_gain,
    w_out,
    w_up,
    w_down,
):
    rows = latents.shape[0]
    x_id, yl_id = lax.axis_index("x"), lax.axis_index("yl")
    span_id = yl_id * 4 + x_id
    level = lax.dynamic_index_in_dim(noise_level, span_id, 0, keepdims=False)
    modulation = lax.dynamic_index_in_dim(mod_table, level, 0, keepdims=False).astype(jnp.float32)
    scale_one, gate_one, scale_two, gate_two = (modulation[i] for i in range(4))
    mask_row = lax.dynamic_index_in_dim(context_mask, span_id, 0, keepdims=False)

    from_y = (yl_id + jnp.array([0, 0, 0, 1, 0, 1, 1, 1], jnp.int32)) % 2
    from_x = (x_id + jnp.array([0, 1, 3, 0, 2, 1, 3, 2], jnp.int32)) % 4
    match = (from_y * 4 + from_x)[:, None] == jnp.arange(8, dtype=jnp.int32)[None, :]
    allowed = jnp.sum(jnp.where(match, mask_row[None, :], 0), axis=1)

    units = w_up.shape[1]
    along = lambda t, d: take_from(t, "x", d)
    up_own = w_up.T
    up_plus, up_minus = along(up_own, 1), along(up_own, -1)

    stream = latents.astype(jnp.float32)
    own = (normed(stream) * (1.0 + scale_one)).astype(jnp.bfloat16)
    plus, minus, other = gather_first(own, "z", "yh")
    own_s = swap(own)
    w_qkv, token = join([w_query, w_key, w_value], axis=1, vmem=True)
    far, other_plus, other_minus, other_far = gather_rest(plus, minus, other, "z", "yh", token)
    first_s = swap(join([plus, minus, other])[0])
    n = rows
    whole = [(i, 0, n) for i in range(4)]
    near = [own, plus, minus, far, own_s, first_s, swap(far)], [*whole, (4, 0, n), (5, 0, 2 * n), (6, 0, n)]
    done = project(near, 0, (), w_qkv, q_gain, k_gain)
    last_s = swap(join([other_plus, other_minus, other_far], tokens=done[:1])[0])
    away = [other, other_plus, other_minus, other_far, first_s, last_s], [*whole, (4, 2 * n, 3 * n), (5, 0, 3 * n)]
    queries, own_kv = project(away, 1, done, w_qkv, q_gain, k_gain)

    own_kv = tie([own_kv], up_plus, up_minus)[0]
    first = gather_first(own_kv, "x", "yl")
    w_o, token = join([w_out], vmem=True)
    rest = gather_rest(*first, "x", "yl", token)
    carry = attend(queries, [own_kv, *first], allowed, None, False)
    attended = attend(queries, rest, allowed, carry, True)

    down_own, _ = join([w_down], tokens=[attended])
    down_plus, down_minus = along(down_own, 1), along(down_own, -1)
    part_away = project_out(attended, 1, w_o)
    part_near = project_out(attended, 0, w_o)
    attn_sum, token = scatter_rows(part_near, part_away, rows, [down_plus, down_minus])
    halves = tie([up_plus[: units // 2], up_minus[units // 2 :]], attended)
    up, up_token = join([up_own, up_plus, up_minus, along(halves[0], 1), along(halves[1], -1)], vmem=True)
    halves = tie([down_plus[: units // 2], down_minus[units // 2 :]], token)
    down, down_token = join([down_own, down_plus, down_minus, along(halves[0], 1), along(halves[1], -1)], vmem=True)

    resid = stream + gate_one * attn_sum
    own = (normed(resid) * (1.0 + scale_two)).astype(jnp.bfloat16)
    half = n // 2
    plus, minus = move(own, 0, 1), move(own, 0, -1)
    far_a, far_b = move(plus[:half], 0, 1), move(minus[half:], 0, -1)
    ring_a, _ = join([own, plus])
    plus_a, minus_a = move(ring_a, 1, 1), move(ring_a, 1, -1)
    ring_b, _ = join([minus, far_a, far_b])
    plus_b, minus_b = move(ring_b, 1, 1), move(ring_b, 1, -1)
    part = feed_forward([ring_a, ring_b, swap(ring_a), swap(ring_b)], up, down)
    parts = [(part[0], part[2]), (part[1], part[3])]
    sends = tie([plus_a, minus_b], part[0])
    far_a, far_b = move(sends[0], 1, 1), move(sends[1], 1, -1)
    part = feed_forward([sends[0], plus_b, swap(sends[0]), swap(plus_b)], up, down)
    parts.append(part)
    far_s = tie([far_a, far_b], part[0])
    part_far = feed_forward([*far_s, swap(far_s[0]), swap(far_s[1])], up, down)
    minus_s = tie([minus_a, sends[1]], part_far[0])
    parts.append(feed_forward([*minus_s, swap(minus_s[0]), swap(minus_s[1])], up, down))
    mlp_sum = scatter_wide(*parts, part_far)
    return (resid + gate_two * mlp_sum).astype(jnp.bfloat16)


def solution(mesh):
    fine = Mesh(mesh.devices.reshape([SIZES[a] for a in AXES]), AXES)
    head = ("z", "yh", "c")
    return jax.shard_map(
        on_device,
        mesh=fine,
        in_specs=(
            P(AXES, None),
            P(),
            P(),
            P(),
            P(None, head),
            P(None, head),
            P(None, head),
            P(),
            P(),
            P(head, None),
            P(None, AXES),
            P(AXES, None),
        ),
        out_specs=P(AXES, None),
        check_vma=False,
    )
```

```python
import functools

import jax
import jax.numpy as jnp
from jax import lax
from jax.experimental import pallas as pl
from jax.experimental.pallas import tpu as pltpu
from jax.sharding import Mesh, PartitionSpec as P

HD = 128
AXES = ("yl", "x", "z", "yh", "c")
SIZES = {"yl": 2, "x": 4, "z": 4, "yh": 2, "c": 2}
MIB = 1024 * 1024

epsilon = 1e-06


def normed(values):
    return values * lax.rsqrt(jnp.mean(values * values, axis=-1, keepdims=True) + epsilon)


def take_from(value, axis, offset):
    size = SIZES[axis]
    return lax.ppermute(value, axis, [((i + offset) % size, i) for i in range(size)])


def params(mib=24):
    return pltpu.CompilerParams(vmem_limit_bytes=mib * MIB)


def cost(flops):
    return pl.CostEstimate(flops=flops // 5, bytes_accessed=0, transcendentals=0)


def in_hbm(value):
    return pltpu.with_memory_space_constraint(value, pltpu.HBM)


ANYWHERE = pl.BlockSpec(memory_space=pl.ANY)
WHOLE = pl.BlockSpec(memory_space=pltpu.VMEM)


def stack(refs, pieces):
    return jnp.concatenate([refs[i][lo:hi, :] for i, lo, hi in pieces], axis=0)


def join_kernel(count, *refs):
    out_ref, at = refs[-1], 0
    for source in refs[:count]:
        out_ref[pl.ds(at, source.shape[0]), :] = source[...]
        at += source.shape[0]


def join(pieces, tokens=()):
    rows, width = sum(p.shape[0] for p in pieces), pieces[0].shape[1]
    return pl.pallas_call(
        functools.partial(join_kernel, len(pieces)),
        in_specs=[WHOLE] * len(pieces) + [ANYWHERE] * len(tokens),
        out_specs=WHOLE,
        out_shape=jax.ShapeDtypeStruct((rows, width), jnp.bfloat16),
        compiler_params=params(),
        cost_estimate=cost(1),
        name="join",
    )(*pieces, *tokens)


def tie_kernel(*refs):
    pass


def tie(values, *tokens):
    return pl.pallas_call(
        tie_kernel,
        in_specs=[ANYWHERE] * (len(values) + len(tokens)),
        out_specs=[ANYWHERE] * len(values),
        out_shape=[jax.ShapeDtypeStruct(v.shape, v.dtype) for v in values],
        input_output_aliases={i: i for i in range(len(values))},
        cost_estimate=cost(1),
        name="tie",
    )(*values, *tokens)


def stack(refs, pieces):
    return jnp.concatenate([refs[i][lo:hi, :] for i, lo, hi in pieces], axis=0)


def qkv_kernel(heads, pieces, count, steps, *refs):
    x_refs, w_refs, (q_gain, k_gain) = refs[:count], refs[count : count + 3], refs[count + 3 : count + 5]
    q_ref, kv_ref, acc, w, sems = refs[-5:]
    width = heads * HD
    cut = w.shape[0] // steps
    copies = [
        [
            pltpu.make_async_copy(
                w_refs[i].at[pl.ds(k * cut, cut), :], w.at[pl.ds(k * cut, cut), pl.ds(i * width, width)], sems.at[k, i]
            )
            for i in range(3)
        ]
        for k in range(steps)
    ]
    for row in copies:
        for copy in row:
            copy.start()
    for k, row in enumerate(copies):
        for copy in row:
            copy.wait()
        cols = slice(k * cut, (k + 1) * cut)
        x = jnp.concatenate([x_refs[i][lo:hi, cols] for i, lo, hi in pieces], axis=0)
        part = jnp.dot(x, w[cols, :], preferred_element_type=jnp.float32)
        if k == 0:
            acc[...] = part
        else:
            acc[...] += part
    for h in range(heads):
        at = pl.ds(h * HD, HD)
        q_ref[:, at] = (normed(acc[:, at]) * q_gain[...]).astype(jnp.bfloat16)
        kv_ref[:, at] = (normed(acc[:, pl.ds(width + h * HD, HD)]) * k_gain[...]).astype(jnp.bfloat16)
    kv_ref[:, width:] = acc[:, 2 * width :].astype(jnp.bfloat16)


def project(chunk, place, earlier, weights, q_gain, k_gain):
    blocks, pieces = chunk
    depth, width = weights[0].shape
    rows = sum(hi - lo for _, lo, hi in pieces)
    heads = width // HD
    steps = 4
    same = lambda i: (0, 0)
    ops = [*blocks, *map(in_hbm, weights), q_gain.reshape(1, HD), k_gain.reshape(1, HD), *earlier]
    return pl.pallas_call(
        functools.partial(qkv_kernel, heads, pieces, len(blocks), steps),
        grid=(1,),
        in_specs=[pl.BlockSpec(b.shape, same) for b in blocks]
        + [ANYWHERE] * 3
        + [pl.BlockSpec((1, HD), same)] * 2
        + [ANYWHERE] * len(earlier),
        out_specs=[
            pl.BlockSpec((rows, width), lambda i: (place, 0)),
            pl.BlockSpec((rows, 2 * width), lambda i: (place, 0)),
        ],
        out_shape=[
            jax.ShapeDtypeStruct((2 * rows, width), jnp.bfloat16),
            jax.ShapeDtypeStruct((2 * rows, 2 * width), jnp.bfloat16),
        ],
        input_output_aliases={len(ops) - 2 + i: i for i in range(len(earlier))},
        scratch_shapes=[
            pltpu.VMEM((rows, 3 * width), jnp.float32),
            pltpu.VMEM((depth, 3 * width), jnp.bfloat16),
            pltpu.SemaphoreType.DMA((steps, 3)),
        ],
        compiler_params=params(36),
        cost_estimate=cost(6 * rows * depth * width),
        name="project",
    )(*ops)


def attend_kernel(heads, count, first, last, *refs):
    allowed, q_ref, kv_refs, refs = refs[0], refs[1], refs[2 : 2 + count], refs[2 + count :]
    if not first:
        old_acc, old_sum, refs = refs[0], refs[1], refs[2:]
    if last:
        out_ref, acc, total = refs
    else:
        acc, total = refs
    rows = q_ref.shape[0]
    width = heads * HD
    if first:
        acc[...] = jnp.zeros_like(acc)
        total[...] = jnp.zeros_like(total)
    else:
        acc[...] = old_acc[...]
        total[...] = old_sum[...]
    factor = HD ** (-0.5) * 1.4426950408889634
    half = rows // 2
    for b in range(count):

        @pl.when(allowed[b + (0 if first else 4)] > 0)
        def _(b=b):
            for part in range(4):
                at = pl.ds(part // 2 * half, half)
                keys_at = pl.ds(part % 2 * half, half)
                for h in range(heads):
                    cols = pl.ds(h * HD, HD)
                    keys = kv_refs[b][keys_at, cols]
                    values = kv_refs[b][keys_at, pl.ds(width + h * HD, HD)]
                    scores = lax.dot_general(
                        q_ref[at, cols], keys, (((1,), (1,)), ((), ())), preferred_element_type=jnp.float32
                    )
                    probs = jnp.exp2(scores * factor)
                    lanes = probs[:, :HD]
                    for i in range(1, probs.shape[1] // HD):
                        lanes = lanes + probs[:, i * HD : (i + 1) * HD]
                    total[at, cols] += lanes
                    acc[at, cols] += jnp.dot(
                        probs.astype(jnp.bfloat16), values, preferred_element_type=jnp.float32
                    )

    if last:
        for h in range(heads):
            cols = pl.ds(h * HD, HD)
            denom = jnp.sum(total[:, cols], axis=-1, keepdims=True)
            out_ref[:, cols] = (acc[:, cols] / denom).astype(jnp.bfloat16)


def attend(queries, blocks, allowed, carry, last):
    rows, width = queries.shape
    heads = width // HD
    count = len(blocks)
    whole = WHOLE
    state = jax.ShapeDtypeStruct((rows, width), jnp.float32)
    ops = [allowed, queries, *blocks, *(carry or ())]
    if last:
        out_shape = jax.ShapeDtypeStruct((rows, width), jnp.bfloat16)
        scratch = [pltpu.VMEM(state.shape, jnp.float32)] * 2
        out_specs = whole
    else:
        out_shape, scratch, out_specs = [state, state], [], [whole, whole]
    return pl.pallas_call(
        functools.partial(attend_kernel, heads, count, carry is None, last),
        in_specs=[pl.BlockSpec(memory_space=pltpu.SMEM)] + [whole] * (len(ops) - 1),
        out_specs=out_specs,
        out_shape=out_shape,
        scratch_shapes=scratch,
        compiler_params=params(),
        cost_estimate=cost(4 * count * rows * rows * width),
        name="attend",
    )(*ops)


def out_kernel(steps, a_ref, w_ref, keep_ref, send_ref, w, sems):
    half = keep_ref.shape[0]
    cut = w.shape[1] // steps
    copies = [
        pltpu.make_async_copy(w_ref.at[:, pl.ds(k * cut, cut)], w.at[:, pl.ds(k * cut, cut)], sems.at[k])
        for k in range(steps)
    ]
    for copy in copies:
        copy.start()
    for k, copy in enumerate(copies):
        copy.wait()
        cols = slice(k * cut, (k + 1) * cut)
        r = jnp.dot(a_ref[...], w[:, cols], preferred_element_type=jnp.float32).astype(jnp.bfloat16)
        keep_ref[:, cols] = r[:half]
        send_ref[:, cols] = r[half:]


def project_out(attended, chunk, w_out):
    depth, width = w_out.shape
    rows = attended.shape[0] // 2
    steps = 4
    same = lambda i: (0, 0)
    return pl.pallas_call(
        functools.partial(out_kernel, steps),
        grid=(1,),
        in_specs=[pl.BlockSpec((rows, depth), lambda i: (chunk, 0)), ANYWHERE],
        out_specs=[pl.BlockSpec((rows // 2, width), same)] * 2,
        out_shape=[jax.ShapeDtypeStruct((rows // 2, width), jnp.bfloat16)] * 2,
        scratch_shapes=[pltpu.VMEM((depth, width), jnp.bfloat16), pltpu.SemaphoreType.DMA((steps,))],
        compiler_params=params(),
        cost_estimate=cost(2 * rows * depth * width),
        name="project_out",
    )(attended, w_out)


def mlp_kernel(count, steps, *refs):
    x_refs, w_refs = refs[:count], refs[count : count + 2]
    out_refs, (acc, hidden, up, down, sems) = refs[-count - 5 : -5], refs[-5:]
    cut = up.shape[1] // steps
    k = pl.program_id(0)
    copies = [
        pltpu.make_async_copy(source.at[:, pl.ds(i * cut, cut)], w.at[:, pl.ds(i * cut, cut)], sems.at[j, i])
        for j, (source, w) in enumerate(zip(w_refs, (up, down)))
        for i in range(steps)
    ]

    @pl.when(k == 0)
    def _():
        for copy in copies:
            copy.start()

    for step in range(steps):

        @pl.when(k == step)
        def _(step=step):
            copies[step].wait()
            x = jnp.concatenate([r[...] for r in x_refs], axis=0)
            w = up[:, step * cut : (step + 1) * cut]
            total = lax.dot_general(x, w, (((1,), (1,)), ((), ())), preferred_element_type=jnp.float32)
            if step > 0:
                total = acc[...] + total
            if step < steps - 1:
                acc[...] = total
            else:
                hidden[...] = jax.nn.gelu(total, approximate=True).astype(jnp.bfloat16)

        @pl.when(k == steps + step)
        def _(step=step):
            copies[steps + step].wait()
            w = down[:, step * cut : (step + 1) * cut]
            r = jnp.dot(hidden[...], w, preferred_element_type=jnp.float32).astype(jnp.bfloat16)
            at = 0
            for out_ref in out_refs:
                n = out_ref.shape[0]
                out_ref[...] = r[at : at + n]
                at += n


def feed_forward(blocks, up, down, *tokens):
    units, width = up.shape
    rows = sum(b.shape[0] for b in blocks)
    steps = 4
    cut = width // steps
    first = lambda k: (0, jnp.minimum(k, steps - 1))
    second = lambda k: (0, jnp.maximum(k - steps, 0))
    return pl.pallas_call(
        functools.partial(mlp_kernel, len(blocks), steps),
        grid=(2 * steps,),
        in_specs=[pl.BlockSpec((b.shape[0], cut), first) for b in blocks] + [ANYWHERE] * (2 + len(tokens)),
        out_specs=[pl.BlockSpec((b.shape[0], cut), second) for b in blocks],
        out_shape=[jax.ShapeDtypeStruct(b.shape, jnp.bfloat16) for b in blocks],
        scratch_shapes=[
            pltpu.VMEM((rows, units), jnp.float32),
            pltpu.VMEM((rows, units), jnp.bfloat16),
            pltpu.VMEM((units, width), jnp.bfloat16),
            pltpu.VMEM((units, width), jnp.bfloat16),
            pltpu.SemaphoreType.DMA((2, steps)),
        ],
        compiler_params=params(60),
        cost_estimate=cost(4 * rows * units * width),
        name="feed_forward",
    )(*blocks, in_hbm(up), in_hbm(down), *tokens)


def swap(value):
    return take_from(value, "c", 1)


def gather_first(own, ring, pair):
    return take_from(own, ring, 1), take_from(own, ring, -1), take_from(own, pair, 1)


def gather_rest(plus, minus, other, ring, pair):
    half = plus.shape[0] // 2
    first = take_from(plus[:half], ring, 1)
    second = take_from(minus[half:], ring, -1)
    other_plus = take_from(other, ring, 1)
    other_minus = take_from(other, ring, -1)
    far = join([first, second])
    return far, other_plus, other_minus, take_from(far, pair, 1)


def move(value, stage, offset):
    pairs = []
    at = lambda yl, z, yh, c: ((yl * 4 + z) * 2 + yh) * 2 + c
    for y in range(4):
        for z in range(4):
            for c in range(2):
                if (c + stage) % 2 == 0:
                    from_y, from_z = y, (z + offset) % 4
                else:
                    from_y, from_z = (y + offset) % 4, z
                pairs.append((at(from_y % 2, from_z, from_y // 2, c), at(y % 2, z, y // 2, c)))
    return lax.ppermute(value, ("yl", "z", "yh", "c"), pairs)


def wide(t):
    return t.astype(jnp.float32)


def add(*terms):
    return functools.reduce(jnp.add, map(wide, terms)).astype(jnp.bfloat16)


def scatter_rows(near, away, rows):
    half = rows // 2
    cut = lambda t, i: t[i * rows : (i + 1) * rows]
    away_got = take_from(away[1], "c", 1)
    near_got = take_from(near[1], "c", 1)
    away_sum = [add(cut(away[0], i), cut(away_got, i)) for i in (1, 2, 3)]
    from_minus = take_from(away_sum[0], "z", -1)
    from_plus = take_from(away_sum[1], "z", 1)
    from_pair = take_from(away_sum[2], "yh", 1)
    far = add(cut(near[0], 3), cut(near_got, 3), from_pair)
    first = take_from(far[:half], "z", -1)
    second = take_from(far[half:], "z", 1)
    away_own = add(cut(away[0], 0), cut(away_got, 0), from_plus, from_minus)
    plus = wide(cut(near[0], 1)) + wide(cut(near_got, 1))
    minus = wide(cut(near[0], 2)) + wide(cut(near_got, 2))
    plus = jnp.concatenate([plus[:half] + wide(first), plus[half:]]).astype(jnp.bfloat16)
    minus = jnp.concatenate([minus[:half], minus[half:] + wide(second)]).astype(jnp.bfloat16)
    total = wide(cut(near[0], 0)) + wide(cut(near_got, 0))
    total = total + wide(take_from(plus, "z", -1)) + wide(take_from(minus, "z", 1))
    return total + wide(take_from(away_own, "yh", 1))


def sums_kernel(plan, count, *refs):
    for out_ref, terms in zip(refs[count:], plan):
        total = None
        for i, lo, at in terms:
            n = refs[i].shape[0] if at is None else at[1] - at[0]
            part = wide(refs[i][lo : lo + n, :])
            if at is not None and n < out_ref.shape[0]:
                pads = [jnp.zeros((k, part.shape[1]), jnp.float32) for k in (at[0], out_ref.shape[0] - at[1])]
                part = jnp.concatenate([p for p in (pads[0], part, pads[1]) if p.shape[0]], axis=0)
            total = part if total is None else total + part
        out_ref[...] = total.astype(out_ref.dtype)


def sums(*wanted):
    arrays, plan = [], []
    for _, rows, terms in wanted:
        row = []
        for array, lo, at in terms:
            spots = [i for i, a in enumerate(arrays) if a is array]
            if not spots:
                arrays.append(array)
            row.append((spots[0] if spots else len(arrays) - 1, lo, at or (0, rows)))
        plan.append(row)
    width = arrays[0].shape[1]
    return pl.pallas_call(
        functools.partial(sums_kernel, plan, len(arrays)),
        grid=(4,),
        in_specs=[pl.BlockSpec((a.shape[0], width // 4), lambda i: (0, i)) for a in arrays],
        out_specs=[pl.BlockSpec((rows, width // 4), lambda i: (0, i)) for _, rows, _ in wanted],
        out_shape=[jax.ShapeDtypeStruct((rows, width), kind) for kind, rows, _ in wanted],
        compiler_params=params(),
        cost_estimate=cost(1),
        name="sums",
    )(*arrays)


def whole_sum(*terms):
    return jnp.bfloat16, terms[0].shape[0], [(t, 0, None) for t in terms]


def scatter_ring(top, low, rows):
    half = rows // 2
    cut = lambda terms, lo: [(t, lo, None) for t in terms]
    far = sums((jnp.bfloat16, half, cut(low, rows)), (jnp.bfloat16, half, cut(low, rows + half)))
    got_a, got_b = move(far[0], 0, -1), move(far[1], 0, 1)
    plus, minus, own = sums(
        (jnp.bfloat16, rows, cut(top, rows) + [(got_a, 0, (0, half))]),
        (jnp.bfloat16, rows, cut(low, 0) + [(got_b, 0, (half, rows))]),
        (jnp.float32, rows, cut(top, 0)),
    )
    return own + wide(move(plus, 0, -1)) + wide(move(minus, 0, 1))


def on_device(
    latents,
    noise_level,
    context_mask,
    mod_table,
    w_query,
    w_key,
    w_value,
    q_gain,
    k_gain,
    w_out,
    w_up,
    w_down,
):
    rows = latents.shape[0]
    x_id, yl_id = lax.axis_index("x"), lax.axis_index("yl")
    span_id = yl_id * 4 + x_id
    level = lax.dynamic_index_in_dim(noise_level, span_id, 0, keepdims=False)
    modulation = lax.dynamic_index_in_dim(mod_table, level, 0, keepdims=False).astype(jnp.float32)
    scale_one, gate_one, scale_two, gate_two = (modulation[i] for i in range(4))
    mask_row = lax.dynamic_index_in_dim(context_mask, span_id, 0, keepdims=False)

    from_y = (yl_id + jnp.array([0, 0, 0, 1, 0, 1, 1, 1], jnp.int32)) % 2
    from_x = (x_id + jnp.array([0, 1, 3, 0, 2, 1, 3, 2], jnp.int32)) % 4
    match = (from_y * 4 + from_x)[:, None] == jnp.arange(8, dtype=jnp.int32)[None, :]
    allowed = jnp.sum(jnp.where(match, mask_row[None, :], 0), axis=1)

    up = lax.all_gather(w_up.T, ("x", "c"), axis=0, tiled=True)

    stream = latents.astype(jnp.float32)
    own = (normed(stream) * (1.0 + scale_one)).astype(jnp.bfloat16)
    plus, minus, other = gather_first(own, "z", "yh")
    own_s = swap(own)
    weights = w_query, w_key, w_value
    far, other_plus, other_minus, other_far = gather_rest(plus, minus, other, "z", "yh")
    first_s = swap(join([plus, minus, other]))
    n = rows
    whole = [(i, 0, n) for i in range(4)]
    near = [own, plus, minus, far, own_s, first_s, swap(far)], [*whole, (4, 0, n), (5, 0, 2 * n), (6, 0, n)]
    done = project(near, 0, (), weights, q_gain, k_gain)
    last_s = swap(join([other_plus, other_minus, other_far], tokens=done[:1]))
    away = [other, other_plus, other_minus, other_far, first_s, last_s], [*whole, (4, 2 * n, 3 * n), (5, 0, 3 * n)]
    queries, own_kv = project(away, 1, done, weights, q_gain, k_gain)

    own_kv = tie([own_kv], up)[0]
    first = gather_first(own_kv, "x", "yl")
    rest = gather_rest(*first, "x", "yl")
    carry = attend(queries, [own_kv, *first], allowed, None, False)
    attended = attend(queries, rest, allowed, carry, True)

    down = lax.all_gather(join([w_down], tokens=[attended]), ("x", "c"), axis=0, tiled=True)
    part_away = project_out(attended, 1, w_out)
    part_near = project_out(attended, 0, w_out)
    attn_sum = scatter_rows(part_near, part_away, rows)

    resid = stream + gate_one * attn_sum
    own = (normed(resid) * (1.0 + scale_two)).astype(jnp.bfloat16)
    half = n // 2
    plus, minus = move(own, 0, 1), move(own, 0, -1)
    ring_a = join([own, plus])
    ring_b = join([minus, move(plus[:half], 0, 1), move(minus[half:], 0, -1)])
    plus_a, minus_a = move(ring_a, 1, 1), move(ring_a, 1, -1)
    plus_b, minus_b = move(ring_b, 1, 1), move(ring_b, 1, -1)
    far_a, far_b = move(plus_a, 1, 1), move(minus_b, 1, -1)
    blocks = [far_a, far_b, plus_a, minus_b, plus_b, minus_a, ring_a, ring_b]
    far_a, far_b, plus_a, minus_b, plus_b, minus_a, ring_a, ring_b = feed_forward(blocks, up, down)
    got_a, got_b = move(far_a, 1, -1), move(far_b, 1, 1)
    got_plus_b, got_minus_a = move(plus_b, 1, -1), move(minus_a, 1, 1)
    out = sums(whole_sum(plus_a, got_a), whole_sum(minus_b, got_b))
    got_plus_a, got_minus_b = move(out[0], 1, -1), move(out[1], 1, 1)
    mlp_sum = scatter_ring((ring_a, got_plus_a, got_minus_a), (ring_b, got_plus_b, got_minus_b), rows)
    return (resid + gate_two * mlp_sum).astype(jnp.bfloat16)


def solution(mesh):
    fine = Mesh(mesh.devices.reshape([SIZES[a] for a in AXES]), AXES)
    head = ("z", "yh", "c")
    return jax.shard_map(
        on_device,
        mesh=fine,
        in_specs=(
            P(AXES, None),
            P(),
            P(),
            P(),
            P(None, head),
            P(None, head),
            P(None, head),
            P(),
            P(),
            P(head, None),
            P(None, AXES),
            P(AXES, None),
        ),
        out_specs=P(AXES, None),
        check_vma=False,
    )
```

```python
import functools

import jax
import jax.numpy as jnp
from jax import lax
from jax.experimental import pallas as pl
from jax.experimental.pallas import tpu as pltpu
from jax.sharding import Mesh, PartitionSpec as P

HD = 128
AXES = ("yl", "x", "z", "yh", "c")
SIZES = {"yl": 2, "x": 4, "z": 4, "yh": 2, "c": 2}
MIB = 1024 * 1024

epsilon = 1e-06


def normed(values):
    return values * lax.rsqrt(jnp.mean(values * values, axis=-1, keepdims=True) + epsilon)


def take_from(value, axis, offset):
    size = SIZES[axis]
    return lax.ppermute(value, axis, [((i + offset) % size, i) for i in range(size)])


def params(mib=24):
    return pltpu.CompilerParams(vmem_limit_bytes=mib * MIB)


def cost(flops):
    return pl.CostEstimate(flops=flops // 5, bytes_accessed=0, transcendentals=0)


def in_hbm(value):
    return pltpu.with_memory_space_constraint(value, pltpu.HBM)


ANYWHERE = pl.BlockSpec(memory_space=pl.ANY)
WHOLE = pl.BlockSpec(memory_space=pltpu.VMEM)


def join_kernel(count, *refs):
    out_ref, at = refs[-1], 0
    for source in refs[:count]:
        out_ref[pl.ds(at, source.shape[0]), :] = source[...]
        at += source.shape[0]


def join(pieces, tokens=()):
    rows, width = sum(p.shape[0] for p in pieces), pieces[0].shape[1]
    return pl.pallas_call(
        functools.partial(join_kernel, len(pieces)),
        in_specs=[WHOLE] * len(pieces) + [ANYWHERE] * len(tokens),
        out_specs=WHOLE,
        out_shape=jax.ShapeDtypeStruct((rows, width), jnp.bfloat16),
        compiler_params=params(),
        cost_estimate=cost(1),
        name="join",
    )(*pieces, *tokens)


def tie_kernel(*refs):
    pass


def tie(values, *tokens):
    return pl.pallas_call(
        tie_kernel,
        in_specs=[ANYWHERE] * (len(values) + len(tokens)),
        out_specs=[ANYWHERE] * len(values),
        out_shape=[jax.ShapeDtypeStruct(v.shape, v.dtype) for v in values],
        input_output_aliases={i: i for i in range(len(values))},
        cost_estimate=cost(1),
        name="tie",
    )(*values, *tokens)


def enter_kernel(span, levels, x_ref, mod_ref, out_ref, table_ref):
    table = mod_ref[...].astype(jnp.float32)
    table_ref[...] = table
    out_ref[...] = (normed(wide(x_ref[...])) * (1.0 + table[0:1])).astype(jnp.bfloat16)


def enter(latents, span_id, noise_level, mod_table):
    rows, width = latents.shape
    spec = pltpu.PrefetchScalarGridSpec(
        num_scalar_prefetch=2,
        grid=(1,),
        in_specs=[
            pl.BlockSpec((rows, width), lambda i, span, levels: (0, 0)),
            pl.BlockSpec((None, 4, width), lambda i, span, levels: (levels[span[0]], 0, 0)),
        ],
        out_specs=[
            pl.BlockSpec((rows, width), lambda i, span, levels: (0, 0)),
            pl.BlockSpec((4, width), lambda i, span, levels: (0, 0)),
        ],
    )
    return pl.pallas_call(
        enter_kernel,
        grid_spec=spec,
        out_shape=[
            jax.ShapeDtypeStruct((rows, width), jnp.bfloat16),
            jax.ShapeDtypeStruct((4, width), jnp.float32),
        ],
        compiler_params=params(),
        cost_estimate=cost(1),
        name="enter",
    )(span_id.reshape(1).astype(jnp.int32), noise_level, in_hbm(latents), in_hbm(mod_table))


def stack(refs, pieces):
    return jnp.concatenate([refs[i][lo:hi, :] for i, lo, hi in pieces], axis=0)


def qkv_kernel(heads, pieces, count, steps, *refs):
    x_refs, w_refs, (q_gain, k_gain) = refs[:count], refs[count : count + 3], refs[count + 3 : count + 5]
    q_ref, kv_ref, acc, w, sems = refs[-5:]
    width = heads * HD
    cut = w.shape[0] // steps
    copies = [
        [
            pltpu.make_async_copy(
                w_refs[i].at[pl.ds(k * cut, cut), :], w.at[pl.ds(k * cut, cut), pl.ds(i * width, width)], sems.at[k, i]
            )
            for i in range(3)
        ]
        for k in range(steps)
    ]
    for row in copies:
        for copy in row:
            copy.start()
    for k, row in enumerate(copies):
        for copy in row:
            copy.wait()
        cols = slice(k * cut, (k + 1) * cut)
        x = jnp.concatenate([x_refs[i][lo:hi, cols] for i, lo, hi in pieces], axis=0)
        part = jnp.dot(x, w[cols, :], preferred_element_type=jnp.float32)
        if k == 0:
            acc[...] = part
        else:
            acc[...] += part
    for h in range(heads):
        at = pl.ds(h * HD, HD)
        q_ref[:, at] = (normed(acc[:, at]) * q_gain[...]).astype(jnp.bfloat16)
        kv_ref[:, at] = (normed(acc[:, pl.ds(width + h * HD, HD)]) * k_gain[...]).astype(jnp.bfloat16)
    kv_ref[:, width:] = acc[:, 2 * width :].astype(jnp.bfloat16)


def project(chunk, place, earlier, weights, q_gain, k_gain):
    blocks, pieces = chunk
    depth, width = weights[0].shape
    rows = sum(hi - lo for _, lo, hi in pieces)
    heads = width // HD
    steps = 4
    same = lambda i: (0, 0)
    ops = [*blocks, *map(in_hbm, weights), q_gain.reshape(1, HD), k_gain.reshape(1, HD), *earlier]
    return pl.pallas_call(
        functools.partial(qkv_kernel, heads, pieces, len(blocks), steps),
        grid=(1,),
        in_specs=[pl.BlockSpec(b.shape, same) for b in blocks]
        + [ANYWHERE] * 3
        + [pl.BlockSpec((1, HD), same)] * 2
        + [ANYWHERE] * len(earlier),
        out_specs=[
            pl.BlockSpec((rows, width), lambda i: (place, 0)),
            pl.BlockSpec((rows, 2 * width), lambda i: (place, 0)),
        ],
        out_shape=[
            jax.ShapeDtypeStruct((2 * rows, width), jnp.bfloat16),
            jax.ShapeDtypeStruct((2 * rows, 2 * width), jnp.bfloat16),
        ],
        input_output_aliases={len(ops) - 2 + i: i for i in range(len(earlier))},
        scratch_shapes=[
            pltpu.VMEM((rows, 3 * width), jnp.float32),
            pltpu.VMEM((depth, 3 * width), jnp.bfloat16),
            pltpu.SemaphoreType.DMA((steps, 3)),
        ],
        compiler_params=params(36),
        cost_estimate=cost(6 * rows * depth * width),
        name="project",
    )(*ops)


def attend_kernel(heads, count, first, last, spare, *refs):
    allowed, q_ref, kv_refs, refs = refs[0], refs[1], refs[2 : 2 + count], refs[2 + count :]
    if not first:
        old_acc, old_sum, refs = refs[0], refs[1], refs[2:]
    refs = refs[spare:]
    if last:
        out_ref, acc, total = refs
    else:
        acc, total = refs
    rows = q_ref.shape[0]
    width = heads * HD
    if first:
        acc[...] = jnp.zeros_like(acc)
        total[...] = jnp.zeros_like(total)
    else:
        acc[...] = old_acc[...]
        total[...] = old_sum[...]
    factor = HD ** (-0.5) * 1.4426950408889634
    half = rows // 2
    for b in range(count):

        @pl.when(allowed[b + (0 if first else 4)] > 0)
        def _(b=b):
            for part in range(4):
                at = pl.ds(part // 2 * half, half)
                keys_at = pl.ds(part % 2 * half, half)
                for h in range(heads):
                    cols = pl.ds(h * HD, HD)
                    keys = kv_refs[b][keys_at, cols]
                    values = kv_refs[b][keys_at, pl.ds(width + h * HD, HD)]
                    scores = lax.dot_general(
                        q_ref[at, cols], keys, (((1,), (1,)), ((), ())), preferred_element_type=jnp.float32
                    )
                    probs = jnp.exp2(scores * factor)
                    lanes = probs[:, :HD]
                    for i in range(1, probs.shape[1] // HD):
                        lanes = lanes + probs[:, i * HD : (i + 1) * HD]
                    total[at, cols] += lanes
                    acc[at, cols] += jnp.dot(
                        probs.astype(jnp.bfloat16), values, preferred_element_type=jnp.float32
                    )

    if last:
        for h in range(heads):
            cols = pl.ds(h * HD, HD)
            denom = jnp.sum(total[:, cols], axis=-1, keepdims=True)
            out_ref[:, cols] = (acc[:, cols] / denom).astype(jnp.bfloat16)


def attend(queries, blocks, allowed, carry, last, *tokens):
    rows, width = queries.shape
    heads = width // HD
    count = len(blocks)
    whole = WHOLE
    state = jax.ShapeDtypeStruct((rows, width), jnp.float32)
    ops = [allowed, queries, *blocks, *(carry or ())]
    if last:
        out_shape = jax.ShapeDtypeStruct((rows, width), jnp.bfloat16)
        scratch = [pltpu.VMEM(state.shape, jnp.float32)] * 2
        out_specs = whole
    else:
        out_shape, scratch, out_specs = [state, state], [], [whole, whole]
    return pl.pallas_call(
        functools.partial(attend_kernel, heads, count, carry is None, last, len(tokens)),
        in_specs=[pl.BlockSpec(memory_space=pltpu.SMEM)] + [whole] * (len(ops) - 1) + [ANYWHERE] * len(tokens),
        out_specs=out_specs,
        out_shape=out_shape,
        scratch_shapes=scratch,
        compiler_params=params(),
        cost_estimate=cost(4 * count * rows * rows * width),
        name="attend",
    )(*ops, *tokens)


def out_kernel(steps, a_ref, w_ref, keep_ref, send_ref, w, sems):
    half = keep_ref.shape[0]
    cut = w.shape[1] // steps
    copies = [
        pltpu.make_async_copy(w_ref.at[:, pl.ds(k * cut, cut)], w.at[:, pl.ds(k * cut, cut)], sems.at[k])
        for k in range(steps)
    ]
    for copy in copies:
        copy.start()
    for k, copy in enumerate(copies):
        copy.wait()
        cols = slice(k * cut, (k + 1) * cut)
        r = jnp.dot(a_ref[...], w[:, cols], preferred_element_type=jnp.float32).astype(jnp.bfloat16)
        keep_ref[:, cols] = r[:half]
        send_ref[:, cols] = r[half:]


def project_out(attended, chunk, w_out):
    depth, width = w_out.shape
    rows = attended.shape[0] // 2
    steps = 4
    same = lambda i: (0, 0)
    return pl.pallas_call(
        functools.partial(out_kernel, steps),
        grid=(1,),
        in_specs=[pl.BlockSpec((rows, depth), lambda i: (chunk, 0)), ANYWHERE],
        out_specs=[pl.BlockSpec((rows // 2, width), same)] * 2,
        out_shape=[jax.ShapeDtypeStruct((rows // 2, width), jnp.bfloat16)] * 2,
        scratch_shapes=[pltpu.VMEM((depth, width), jnp.bfloat16), pltpu.SemaphoreType.DMA((steps,))],
        compiler_params=params(),
        cost_estimate=cost(2 * rows * depth * width),
        name="project_out",
    )(attended, in_hbm(w_out))


def mlp_kernel(count, steps, *refs):
    x_refs, w_refs = refs[:count], refs[count : count + 2]
    out_refs, (acc, hidden, up, down, sems) = refs[-count - 5 : -5], refs[-5:]
    cut = up.shape[1] // steps
    k = pl.program_id(0)
    copies = [
        pltpu.make_async_copy(source.at[:, pl.ds(i * cut, cut)], w.at[:, pl.ds(i * cut, cut)], sems.at[j, i])
        for j, (source, w) in enumerate(zip(w_refs, (up, down)))
        for i in range(steps)
    ]

    @pl.when(k == 0)
    def _():
        for copy in copies:
            copy.start()

    for step in range(steps):

        @pl.when(k == step)
        def _(step=step):
            copies[step].wait()
            x = jnp.concatenate([r[...] for r in x_refs], axis=0)
            w = up[:, step * cut : (step + 1) * cut]
            total = lax.dot_general(x, w, (((1,), (1,)), ((), ())), preferred_element_type=jnp.float32)
            if step > 0:
                total = acc[...] + total
            if step < steps - 1:
                acc[...] = total
            else:
                hidden[...] = jax.nn.gelu(total, approximate=True).astype(jnp.bfloat16)

        @pl.when(k == steps + step)
        def _(step=step):
            copies[steps + step].wait()
            w = down[:, step * cut : (step + 1) * cut]
            r = jnp.dot(hidden[...], w, preferred_element_type=jnp.float32).astype(jnp.bfloat16)
            at = 0
            for out_ref in out_refs:
                n = out_ref.shape[0]
                out_ref[...] = r[at : at + n]
                at += n


def feed_forward(blocks, up, down, *tokens):
    units, width = up.shape
    rows = sum(b.shape[0] for b in blocks)
    steps = 2
    cut = width // steps
    first = lambda k: (0, jnp.minimum(k, steps - 1))
    second = lambda k: (0, jnp.maximum(k - steps, 0))
    return pl.pallas_call(
        functools.partial(mlp_kernel, len(blocks), steps),
        grid=(2 * steps,),
        in_specs=[pl.BlockSpec((b.shape[0], cut), first) for b in blocks] + [ANYWHERE] * (2 + len(tokens)),
        out_specs=[pl.BlockSpec((b.shape[0], cut), second) for b in blocks],
        out_shape=[jax.ShapeDtypeStruct(b.shape, jnp.bfloat16) for b in blocks],
        scratch_shapes=[
            pltpu.VMEM((rows, units), jnp.float32),
            pltpu.VMEM((rows, units), jnp.bfloat16),
            pltpu.VMEM((units, width), jnp.bfloat16),
            pltpu.VMEM((units, width), jnp.bfloat16),
            pltpu.SemaphoreType.DMA((2, steps)),
        ],
        compiler_params=params(60),
        cost_estimate=cost(4 * rows * units * width),
        name="feed_forward",
    )(*blocks, in_hbm(up), in_hbm(down), *tokens)


def swap(value):
    return take_from(value, "c", 1)


def gather_first(own, ring, pair):
    return take_from(own, ring, 1), take_from(own, ring, -1), take_from(own, pair, 1)


def gather_rest(plus, minus, other, ring, pair):
    half = plus.shape[0] // 2
    first = take_from(plus[:half], ring, 1)
    second = take_from(minus[half:], ring, -1)
    other_plus = take_from(other, ring, 1)
    other_minus = take_from(other, ring, -1)
    far = join([first, second])
    return far, other_plus, other_minus, take_from(far, pair, 1)


def move(value, stage, offset):
    pairs = []
    at = lambda yl, z, yh, c: ((yl * 4 + z) * 2 + yh) * 2 + c
    for y in range(4):
        for z in range(4):
            for c in range(2):
                if (c + stage) % 2 == 0:
                    from_y, from_z = y, (z + offset) % 4
                else:
                    from_y, from_z = (y + offset) % 4, z
                pairs.append((at(from_y % 2, from_z, from_y // 2, c), at(y % 2, z, y // 2, c)))
    return lax.ppermute(value, ("yl", "z", "yh", "c"), pairs)


def wide(t):
    return t.astype(jnp.float32)


def add(*terms):
    return functools.reduce(jnp.add, map(wide, terms)).astype(jnp.bfloat16)


def scatter_rows(near, away, rows):
    half = rows // 2
    cut = lambda t, i: t[i * rows : (i + 1) * rows]
    away_got = take_from(away[1], "c", 1)
    near_got = take_from(near[1], "c", 1)
    away_sum = [add(cut(away[0], i), cut(away_got, i)) for i in (1, 2, 3)]
    from_minus = take_from(away_sum[0], "z", -1)
    from_plus = take_from(away_sum[1], "z", 1)
    from_pair = take_from(away_sum[2], "yh", 1)
    far = add(cut(near[0], 3), cut(near_got, 3), from_pair)
    first = take_from(far[:half], "z", -1)
    second = take_from(far[half:], "z", 1)
    away_own = add(cut(away[0], 0), cut(away_got, 0), from_plus, from_minus)
    plus = wide(cut(near[0], 1)) + wide(cut(near_got, 1))
    minus = wide(cut(near[0], 2)) + wide(cut(near_got, 2))
    plus = jnp.concatenate([plus[:half] + wide(first), plus[half:]]).astype(jnp.bfloat16)
    minus = jnp.concatenate([minus[:half], minus[half:] + wide(second)]).astype(jnp.bfloat16)
    total = wide(cut(near[0], 0)) + wide(cut(near_got, 0))
    total = total + wide(take_from(plus, "z", -1)) + wide(take_from(minus, "z", 1))
    return total + wide(take_from(away_own, "yh", 1))


def sums_kernel(plan, count, *refs):
    for out_ref, terms in zip(refs[count:], plan):
        total = None
        for i, lo, at in terms:
            n = refs[i].shape[0] if at is None else at[1] - at[0]
            part = wide(refs[i][lo : lo + n, :])
            if at is not None and n < out_ref.shape[0]:
                pads = [jnp.zeros((k, part.shape[1]), jnp.float32) for k in (at[0], out_ref.shape[0] - at[1])]
                part = jnp.concatenate([p for p in (pads[0], part, pads[1]) if p.shape[0]], axis=0)
            total = part if total is None else total + part
        out_ref[...] = total.astype(out_ref.dtype)


def sums(*wanted):
    arrays, plan = [], []
    for _, rows, terms in wanted:
        row = []
        for array, lo, at in terms:
            spots = [i for i, a in enumerate(arrays) if a is array]
            if not spots:
                arrays.append(array)
            row.append((spots[0] if spots else len(arrays) - 1, lo, at or (0, rows)))
        plan.append(row)
    width = arrays[0].shape[1]
    return pl.pallas_call(
        functools.partial(sums_kernel, plan, len(arrays)),
        grid=(4,),
        in_specs=[pl.BlockSpec((a.shape[0], width // 4), lambda i: (0, i)) for a in arrays],
        out_specs=[pl.BlockSpec((rows, width // 4), lambda i: (0, i)) for _, rows, _ in wanted],
        out_shape=[jax.ShapeDtypeStruct((rows, width), kind) for kind, rows, _ in wanted],
        compiler_params=params(),
        cost_estimate=cost(1),
        name="sums",
    )(*arrays)


def whole_sum(*terms):
    return jnp.bfloat16, terms[0].shape[0], [(t, 0, None) for t in terms]


def scatter_ring(top, low, rows):
    half = rows // 2
    cut = lambda terms, lo: [(t, lo, None) for t in terms]
    far = sums((jnp.bfloat16, half, cut(low, rows)), (jnp.bfloat16, half, cut(low, rows + half)))
    got_a, got_b = move(far[0], 0, -1), move(far[1], 0, 1)
    plus, minus, own = sums(
        (jnp.bfloat16, rows, cut(top, rows) + [(got_a, 0, (0, half))]),
        (jnp.bfloat16, rows, cut(low, 0) + [(got_b, 0, (half, rows))]),
        (jnp.float32, rows, cut(top, 0)),
    )
    return own + wide(move(plus, 0, -1)) + wide(move(minus, 0, 1))


def on_device(
    latents,
    noise_level,
    context_mask,
    mod_table,
    w_query,
    w_key,
    w_value,
    q_gain,
    k_gain,
    w_out,
    w_up,
    w_down,
):
    rows = latents.shape[0]
    x_id, yl_id = lax.axis_index("x"), lax.axis_index("yl")
    span_id = yl_id * 4 + x_id
    mask_row = lax.dynamic_index_in_dim(context_mask, span_id, 0, keepdims=False)

    from_y = (yl_id + jnp.array([0, 0, 0, 1, 0, 1, 1, 1], jnp.int32)) % 2
    from_x = (x_id + jnp.array([0, 1, 3, 0, 2, 1, 3, 2], jnp.int32)) % 4
    match = (from_y * 4 + from_x)[:, None] == jnp.arange(8, dtype=jnp.int32)[None, :]
    allowed = jnp.sum(jnp.where(match, mask_row[None, :], 0), axis=1)

    up = lax.all_gather(w_up.T, ("x", "c"), axis=0, tiled=True)

    own, table = enter(latents, span_id, noise_level, mod_table)
    plus, minus, other = gather_first(own, "z", "yh")
    own_s = swap(own)
    weights = w_query, w_key, w_value
    far, other_plus, other_minus, other_far = gather_rest(plus, minus, other, "z", "yh")
    first_s = swap(join([plus, minus, other]))
    n = rows
    whole = [(i, 0, n) for i in range(4)]
    near = [own, plus, minus, far, own_s, first_s, swap(far)], [*whole, (4, 0, n), (5, 0, 2 * n), (6, 0, n)]
    done = project(near, 0, (), weights, q_gain, k_gain)
    last_s = swap(join([other_plus, other_minus, other_far], tokens=done[:1]))
    away = [other, other_plus, other_minus, other_far, first_s, last_s], [*whole, (4, 2 * n, 3 * n), (5, 0, 3 * n)]
    queries, own_kv = project(away, 1, done, weights, q_gain, k_gain)

    first = gather_first(own_kv, "x", "yl")
    rest = gather_rest(*first, "x", "yl")
    carry = attend(queries, [own_kv, *first], allowed, None, False, in_hbm(up))
    attended = attend(queries, rest, allowed, carry, True)

    down = lax.all_gather(join([w_down], tokens=[attended]), ("x", "c"), axis=0, tiled=True)
    part_away = project_out(attended, 1, w_out)
    part_near = project_out(attended, 0, w_out)
    attn_sum = scatter_rows(part_near, part_away, rows)

    resid = wide(latents) + table[1] * attn_sum
    own = (normed(resid) * (1.0 + table[2])).astype(jnp.bfloat16)
    half = n // 2
    plus, minus = move(own, 0, 1), move(own, 0, -1)
    ring_a = join([own, plus])
    ring_b = join([minus, move(plus[:half], 0, 1), move(minus[half:], 0, -1)])
    plus_a, minus_a = move(ring_a, 1, 1), move(ring_a, 1, -1)
    plus_b, minus_b = move(ring_b, 1, 1), move(ring_b, 1, -1)
    far_a, far_b = move(plus_a, 1, 1), move(minus_b, 1, -1)
    blocks = [far_a, far_b, plus_a, minus_b, plus_b, minus_a, ring_a, ring_b]
    far_a, far_b, plus_a, minus_b, plus_b, minus_a, ring_a, ring_b = feed_forward(blocks, up, down)
    got_a, got_b = move(far_a, 1, -1), move(far_b, 1, 1)
    got_plus_b, got_minus_a = move(plus_b, 1, -1), move(minus_a, 1, 1)
    out = sums(whole_sum(plus_a, got_a), whole_sum(minus_b, got_b))
    got_plus_a, got_minus_b = move(out[0], 1, -1), move(out[1], 1, 1)
    mlp_sum = scatter_ring((ring_a, got_plus_a, got_minus_a), (ring_b, got_plus_b, got_minus_b), rows)
    return (resid + table[3] * mlp_sum).astype(jnp.bfloat16)


def solution(mesh):
    fine = Mesh(mesh.devices.reshape([SIZES[a] for a in AXES]), AXES)
    head = ("z", "yh", "c")
    return jax.shard_map(
        on_device,
        mesh=fine,
        in_specs=(
            P(AXES, None),
            P(),
            P(),
            P(),
            P(None, head),
            P(None, head),
            P(None, head),
            P(),
            P(),
            P(head, None),
            P(None, AXES),
            P(AXES, None),
        ),
        out_specs=P(AXES, None),
        check_vma=False,
    )
```

```python
import functools

import jax
import jax.numpy as jnp
from jax import lax
from jax.experimental import pallas as pl
from jax.experimental.pallas import tpu as pltpu
from jax.sharding import Mesh, PartitionSpec as P

HD = 128
AXES = ("yl", "x", "z", "yh", "c")
SIZES = {"yl": 2, "x": 4, "z": 4, "yh": 2, "c": 2}
MIB = 1024 * 1024

epsilon = 1e-06


def normed(values):
    return values * lax.rsqrt(jnp.mean(values * values, axis=-1, keepdims=True) + epsilon)


def take_from(value, axis, offset):
    size = SIZES[axis]
    return lax.ppermute(value, axis, [((i + offset) % size, i) for i in range(size)])


def params(mib=24):
    return pltpu.CompilerParams(vmem_limit_bytes=mib * MIB)


def cost(flops):
    return pl.CostEstimate(flops=flops // 5, bytes_accessed=0, transcendentals=0)


def in_hbm(value):
    return pltpu.with_memory_space_constraint(value, pltpu.HBM)


ANYWHERE = pl.BlockSpec(memory_space=pl.ANY)
WHOLE = pl.BlockSpec(memory_space=pltpu.VMEM)


def join_kernel(count, *refs):
    out_ref, at = refs[-1], 0
    for source in refs[:count]:
        out_ref[pl.ds(at, source.shape[0]), :] = source[...]
        at += source.shape[0]


def join(pieces, tokens=()):
    rows, width = sum(p.shape[0] for p in pieces), pieces[0].shape[1]
    return pl.pallas_call(
        functools.partial(join_kernel, len(pieces)),
        in_specs=[WHOLE] * len(pieces) + [ANYWHERE] * len(tokens),
        out_specs=WHOLE,
        out_shape=jax.ShapeDtypeStruct((rows, width), jnp.bfloat16),
        compiler_params=params(),
        cost_estimate=cost(1),
        name="join",
    )(*pieces, *tokens)


def tie_kernel(*refs):
    pass


def tie(values, *tokens):
    return pl.pallas_call(
        tie_kernel,
        in_specs=[ANYWHERE] * (len(values) + len(tokens)),
        out_specs=[ANYWHERE] * len(values),
        out_shape=[jax.ShapeDtypeStruct(v.shape, v.dtype) for v in values],
        input_output_aliases={i: i for i in range(len(values))},
        cost_estimate=cost(1),
        name="tie",
    )(*values, *tokens)


def enter_kernel(span, levels, x_ref, mod_ref, out_ref, table_ref):
    table = mod_ref[...].astype(jnp.float32)
    table_ref[...] = table
    out_ref[...] = (normed(wide(x_ref[...])) * (1.0 + table[0:1])).astype(jnp.bfloat16)


def enter(latents, span_id, noise_level, mod_table):
    rows, width = latents.shape
    spec = pltpu.PrefetchScalarGridSpec(
        num_scalar_prefetch=2,
        grid=(1,),
        in_specs=[
            pl.BlockSpec((rows, width), lambda i, span, levels: (0, 0)),
            pl.BlockSpec((None, 4, width), lambda i, span, levels: (levels[span[0]], 0, 0)),
        ],
        out_specs=[
            pl.BlockSpec((rows, width), lambda i, span, levels: (0, 0)),
            pl.BlockSpec((4, width), lambda i, span, levels: (0, 0)),
        ],
    )
    return pl.pallas_call(
        enter_kernel,
        grid_spec=spec,
        out_shape=[
            jax.ShapeDtypeStruct((rows, width), jnp.bfloat16),
            jax.ShapeDtypeStruct((4, width), jnp.float32),
        ],
        compiler_params=params(),
        cost_estimate=cost(1),
        name="enter",
    )(span_id.reshape(1).astype(jnp.int32), noise_level, in_hbm(latents), in_hbm(mod_table))


def stack(refs, pieces):
    return jnp.concatenate([refs[i][lo:hi, :] for i, lo, hi in pieces], axis=0)


def qkv_kernel(heads, pieces, count, steps, *refs):
    x_refs, w_refs, (q_gain, k_gain) = refs[:count], refs[count : count + 3], refs[count + 3 : count + 5]
    q_ref, kv_ref, acc, w, sems = refs[-5:]
    width = heads * HD
    cut = w.shape[0] // steps
    copies = [
        [
            pltpu.make_async_copy(
                w_refs[i].at[pl.ds(k * cut, cut), :], w.at[pl.ds(k * cut, cut), pl.ds(i * width, width)], sems.at[k, i]
            )
            for i in range(3)
        ]
        for k in range(steps)
    ]
    for row in copies:
        for copy in row:
            copy.start()
    for k, row in enumerate(copies):
        for copy in row:
            copy.wait()
        cols = slice(k * cut, (k + 1) * cut)
        x = jnp.concatenate([x_refs[i][lo:hi, cols] for i, lo, hi in pieces], axis=0)
        part = jnp.dot(x, w[cols, :], preferred_element_type=jnp.float32)
        if k == 0:
            acc[...] = part
        else:
            acc[...] += part
    for h in range(heads):
        at = pl.ds(h * HD, HD)
        q_ref[:, at] = (normed(acc[:, at]) * q_gain[...]).astype(jnp.bfloat16)
        kv_ref[:, at] = (normed(acc[:, pl.ds(width + h * HD, HD)]) * k_gain[...]).astype(jnp.bfloat16)
    kv_ref[:, width:] = acc[:, 2 * width :].astype(jnp.bfloat16)


def project(chunk, place, earlier, weights, q_gain, k_gain):
    blocks, pieces = chunk
    depth, width = weights[0].shape
    rows = sum(hi - lo for _, lo, hi in pieces)
    heads = width // HD
    steps = 4
    same = lambda i: (0, 0)
    ops = [*blocks, *map(in_hbm, weights), q_gain.reshape(1, HD), k_gain.reshape(1, HD), *earlier]
    return pl.pallas_call(
        functools.partial(qkv_kernel, heads, pieces, len(blocks), steps),
        grid=(1,),
        in_specs=[pl.BlockSpec(b.shape, same) for b in blocks]
        + [ANYWHERE] * 3
        + [pl.BlockSpec((1, HD), same)] * 2
        + [ANYWHERE] * len(earlier),
        out_specs=[
            pl.BlockSpec((rows, width), lambda i: (place, 0)),
            pl.BlockSpec((rows, 2 * width), lambda i: (place, 0)),
        ],
        out_shape=[
            jax.ShapeDtypeStruct((2 * rows, width), jnp.bfloat16),
            jax.ShapeDtypeStruct((2 * rows, 2 * width), jnp.bfloat16),
        ],
        input_output_aliases={len(ops) - 2 + i: i for i in range(len(earlier))},
        scratch_shapes=[
            pltpu.VMEM((rows, 3 * width), jnp.float32),
            pltpu.VMEM((depth, 3 * width), jnp.bfloat16),
            pltpu.SemaphoreType.DMA((steps, 3)),
        ],
        compiler_params=params(36),
        cost_estimate=cost(6 * rows * depth * width),
        name="project",
    )(*ops)


def attend_kernel(heads, count, first, last, spare, *refs):
    allowed, q_ref, kv_refs, refs = refs[0], refs[1], refs[2 : 2 + count], refs[2 + count :]
    if not first:
        old_acc, old_sum, refs = refs[0], refs[1], refs[2:]
    refs = refs[spare:]
    if last:
        keep_ref, send_ref, acc, total = refs
    else:
        acc, total = refs
    rows = q_ref.shape[0]
    width = heads * HD
    if first:
        acc[...] = jnp.zeros_like(acc)
        total[...] = jnp.zeros_like(total)
    else:
        acc[...] = old_acc[...]
        total[...] = old_sum[...]
    factor = HD ** (-0.5) * 1.4426950408889634
    half = rows // 2
    for b in range(count):

        @pl.when(allowed[b + (0 if first else 4)] > 0)
        def _(b=b):
            for part in range(4):
                at = pl.ds(part // 2 * half, half)
                keys_at = pl.ds(part % 2 * half, half)
                for h in range(heads):
                    cols = pl.ds(h * HD, HD)
                    keys = kv_refs[b][keys_at, cols]
                    values = kv_refs[b][keys_at, pl.ds(width + h * HD, HD)]
                    scores = lax.dot_general(
                        q_ref[at, cols], keys, (((1,), (1,)), ((), ())), preferred_element_type=jnp.float32
                    )
                    probs = jnp.exp2(scores * factor)
                    lanes = probs[:, :HD]
                    for i in range(1, probs.shape[1] // HD):
                        lanes = lanes + probs[:, i * HD : (i + 1) * HD]
                    total[at, cols] += lanes
                    acc[at, cols] += jnp.dot(
                        probs.astype(jnp.bfloat16), values, preferred_element_type=jnp.float32
                    )

    if last:
        for h in range(heads):
            cols = pl.ds(h * HD, HD)
            denom = jnp.sum(total[:, cols], axis=-1, keepdims=True)
            out = (acc[:, cols] / denom).astype(jnp.bfloat16)
            n = rows // 4
            for i, ref in enumerate((keep_ref, send_ref)):
                ref[:n, cols] = out[i * n : (i + 1) * n]
                ref[n:, cols] = out[(2 + i) * n : (3 + i) * n]


def attend(queries, blocks, allowed, carry, last, *tokens):
    rows, width = queries.shape
    heads = width // HD
    count = len(blocks)
    whole = WHOLE
    state = jax.ShapeDtypeStruct((rows, width), jnp.float32)
    ops = [allowed, queries, *blocks, *(carry or ())]
    if last:
        out_shape = [jax.ShapeDtypeStruct((rows // 2, width), jnp.bfloat16)] * 2
        scratch = [pltpu.VMEM(state.shape, jnp.float32)] * 2
        out_specs = [whole, whole]
    else:
        out_shape, scratch, out_specs = [state, state], [], [whole, whole]
    return pl.pallas_call(
        functools.partial(attend_kernel, heads, count, carry is None, last, len(tokens)),
        in_specs=[pl.BlockSpec(memory_space=pltpu.SMEM)] + [whole] * (len(ops) - 1) + [ANYWHERE] * len(tokens),
        out_specs=out_specs,
        out_shape=out_shape,
        scratch_shapes=scratch,
        compiler_params=params(),
        cost_estimate=cost(4 * count * rows * rows * width),
        name="attend",
    )(*ops, *tokens)


def out_kernel(steps, a_ref, b_ref, own_ref, other_ref, *refs):
    out_refs, (w, sems) = refs[:-2], refs[-2:]
    depth = own_ref.shape[0]
    cut = w.shape[1] // steps
    copies = [
        [
            pltpu.make_async_copy(
                source.at[:, pl.ds(k * cut, cut)], w.at[pl.ds(i * depth, depth), pl.ds(k * cut, cut)], sems.at[k, i]
            )
            for i, source in enumerate((own_ref, other_ref))
        ]
        for k in range(steps)
    ]
    for row in copies:
        for copy in row:
            copy.start()
    x = jnp.concatenate([a_ref[...], b_ref[...]], axis=1)
    for k, row in enumerate(copies):
        for copy in row:
            copy.wait()
        cols = slice(k * cut, (k + 1) * cut)
        r = jnp.dot(x, w[:, cols], preferred_element_type=jnp.float32).astype(jnp.bfloat16)
        n = out_refs[0].shape[0]
        for i, out_ref in enumerate(out_refs):
            out_ref[:, cols] = r[i * n : (i + 1) * n]


def project_out(own_cols, other_cols, own_w, other_w, count):
    depth, width = own_w.shape
    rows = own_cols.shape[0]
    steps = 4
    return pl.pallas_call(
        functools.partial(out_kernel, steps),
        in_specs=[WHOLE, WHOLE, ANYWHERE, ANYWHERE],
        out_specs=[WHOLE] * count,
        out_shape=[jax.ShapeDtypeStruct((rows // count, width), jnp.bfloat16)] * count,
        scratch_shapes=[pltpu.VMEM((2 * depth, width), jnp.bfloat16), pltpu.SemaphoreType.DMA((steps, 2))],
        compiler_params=params(28),
        cost_estimate=cost(4 * rows * depth * width),
        name="project_out",
    )(own_cols, other_cols, in_hbm(own_w), other_w)


def mlp_kernel(count, steps, *refs):
    x_refs, w_refs = refs[:count], refs[count : count + 2]
    out_refs, (acc, hidden, up, down, sems) = refs[-count - 5 : -5], refs[-5:]
    cut = up.shape[1] // steps
    k = pl.program_id(0)
    copies = [
        pltpu.make_async_copy(source.at[:, pl.ds(i * cut, cut)], w.at[:, pl.ds(i * cut, cut)], sems.at[j, i])
        for j, (source, w) in enumerate(zip(w_refs, (up, down)))
        for i in range(steps)
    ]

    @pl.when(k == 0)
    def _():
        for copy in copies:
            copy.start()

    for step in range(steps):

        @pl.when(k == step)
        def _(step=step):
            copies[step].wait()
            x = jnp.concatenate([r[...] for r in x_refs], axis=0)
            w = up[:, step * cut : (step + 1) * cut]
            total = lax.dot_general(x, w, (((1,), (1,)), ((), ())), preferred_element_type=jnp.float32)
            if step > 0:
                total = acc[...] + total
            if step < steps - 1:
                acc[...] = total
            else:
                hidden[...] = jax.nn.gelu(total, approximate=True).astype(jnp.bfloat16)

        @pl.when(k == steps + step)
        def _(step=step):
            copies[steps + step].wait()
            w = down[:, step * cut : (step + 1) * cut]
            r = jnp.dot(hidden[...], w, preferred_element_type=jnp.float32).astype(jnp.bfloat16)
            at = 0
            for out_ref in out_refs:
                n = out_ref.shape[0]
                out_ref[...] = r[at : at + n]
                at += n


def feed_forward(blocks, up, down, *tokens):
    units, width = up.shape
    rows = sum(b.shape[0] for b in blocks)
    steps = 2
    cut = width // steps
    first = lambda k: (0, jnp.minimum(k, steps - 1))
    second = lambda k: (0, jnp.maximum(k - steps, 0))
    return pl.pallas_call(
        functools.partial(mlp_kernel, len(blocks), steps),
        grid=(2 * steps,),
        in_specs=[pl.BlockSpec((b.shape[0], cut), first) for b in blocks] + [ANYWHERE] * (2 + len(tokens)),
        out_specs=[pl.BlockSpec((b.shape[0], cut), second) for b in blocks],
        out_shape=[jax.ShapeDtypeStruct(b.shape, jnp.bfloat16) for b in blocks],
        scratch_shapes=[
            pltpu.VMEM((rows, units), jnp.float32),
            pltpu.VMEM((rows, units), jnp.bfloat16),
            pltpu.VMEM((units, width), jnp.bfloat16),
            pltpu.VMEM((units, width), jnp.bfloat16),
            pltpu.SemaphoreType.DMA((2, steps)),
        ],
        compiler_params=params(60),
        cost_estimate=cost(4 * rows * units * width),
        name="feed_forward",
    )(*blocks, in_hbm(up), in_hbm(down), *tokens)


def swap(value):
    return take_from(value, "c", 1)


def gather_first(own, ring, pair):
    return take_from(own, ring, 1), take_from(own, ring, -1), take_from(own, pair, 1)


def gather_rest(plus, minus, other, ring, pair):
    half = plus.shape[0] // 2
    first = take_from(plus[:half], ring, 1)
    second = take_from(minus[half:], ring, -1)
    other_plus = take_from(other, ring, 1)
    other_minus = take_from(other, ring, -1)
    far = join([first, second])
    return far, other_plus, other_minus, take_from(far, pair, 1)


def move(value, stage, offset):
    pairs = []
    at = lambda yl, z, yh, c: ((yl * 4 + z) * 2 + yh) * 2 + c
    for y in range(4):
        for z in range(4):
            for c in range(2):
                if (c + stage) % 2 == 0:
                    from_y, from_z = y, (z + offset) % 4
                else:
                    from_y, from_z = (y + offset) % 4, z
                pairs.append((at(from_y % 2, from_z, from_y // 2, c), at(y % 2, z, y // 2, c)))
    return lax.ppermute(value, ("yl", "z", "yh", "c"), pairs)


def wide(t):
    return t.astype(jnp.float32)


def sums_kernel(plan, count, *refs):
    for out_ref, terms in zip(refs[count:], plan):
        total = None
        for i, lo, at in terms:
            n = refs[i].shape[0] if at is None else at[1] - at[0]
            part = wide(refs[i][lo : lo + n, :])
            if at is not None and n < out_ref.shape[0]:
                pads = [jnp.zeros((k, part.shape[1]), jnp.float32) for k in (at[0], out_ref.shape[0] - at[1])]
                part = jnp.concatenate([p for p in (pads[0], part, pads[1]) if p.shape[0]], axis=0)
            total = part if total is None else total + part
        out_ref[...] = total.astype(out_ref.dtype)


def sums(*wanted):
    arrays, plan = [], []
    for _, rows, terms in wanted:
        row = []
        for array, lo, at in terms:
            spots = [i for i, a in enumerate(arrays) if a is array]
            if not spots:
                arrays.append(array)
            row.append((spots[0] if spots else len(arrays) - 1, lo, at or (0, rows)))
        plan.append(row)
    width = arrays[0].shape[1]
    return pl.pallas_call(
        functools.partial(sums_kernel, plan, len(arrays)),
        grid=(4,),
        in_specs=[pl.BlockSpec((a.shape[0], width // 4), lambda i: (0, i)) for a in arrays],
        out_specs=[pl.BlockSpec((rows, width // 4), lambda i: (0, i)) for _, rows, _ in wanted],
        out_shape=[jax.ShapeDtypeStruct((rows, width), kind) for kind, rows, _ in wanted],
        compiler_params=params(),
        cost_estimate=cost(1),
        name="sums",
    )(*arrays)


def whole_sum(*terms):
    return jnp.bfloat16, terms[0].shape[0], [(t, 0, None) for t in terms]


def scatter_rows(near, away):
    rows = near[0].shape[0]
    half = rows // 2
    from_minus = take_from(away[1], "z", -1)
    from_plus = take_from(away[2], "z", 1)
    from_pair = take_from(away[3], "yh", 1)
    far_a, far_b, other = sums(
        (jnp.bfloat16, half, [(near[3], 0, None), (from_pair, 0, None)]),
        (jnp.bfloat16, half, [(near[3], half, None), (from_pair, half, None)]),
        whole_sum(away[0], from_plus, from_minus),
    )
    got_a, got_b = take_from(far_a, "z", -1), take_from(far_b, "z", 1)
    got_other = take_from(other, "yh", 1)
    plus, minus = sums(
        (jnp.bfloat16, rows, [(near[1], 0, None), (got_a, 0, (0, half))]),
        (jnp.bfloat16, rows, [(near[2], 0, None), (got_b, 0, (half, rows))]),
    )
    return near[0], take_from(plus, "z", -1), take_from(minus, "z", 1), got_other


def scatter_ring(top, low, rows):
    half = rows // 2
    cut = lambda terms, lo: [(t, lo, None) for t in terms]
    far = sums((jnp.bfloat16, half, cut(low, rows)), (jnp.bfloat16, half, cut(low, rows + half)))
    got_a, got_b = move(far[0], 0, -1), move(far[1], 0, 1)
    plus, minus, own = sums(
        (jnp.bfloat16, rows, cut(top, rows) + [(got_a, 0, (0, half))]),
        (jnp.bfloat16, rows, cut(low, 0) + [(got_b, 0, (half, rows))]),
        (jnp.float32, rows, cut(top, 0)),
    )
    return own, move(plus, 0, -1), move(minus, 0, 1)


def on_device(
    latents,
    noise_level,
    context_mask,
    mod_table,
    w_query,
    w_key,
    w_value,
    q_gain,
    k_gain,
    w_out,
    w_up,
    w_down,
):
    rows = latents.shape[0]
    x_id, yl_id = lax.axis_index("x"), lax.axis_index("yl")
    span_id = yl_id * 4 + x_id
    mask_row = lax.dynamic_index_in_dim(context_mask, span_id, 0, keepdims=False)

    from_y = (yl_id + jnp.array([0, 0, 0, 1, 0, 1, 1, 1], jnp.int32)) % 2
    from_x = (x_id + jnp.array([0, 1, 3, 0, 2, 1, 3, 2], jnp.int32)) % 4
    match = (from_y * 4 + from_x)[:, None] == jnp.arange(8, dtype=jnp.int32)[None, :]
    allowed = jnp.sum(jnp.where(match, mask_row[None, :], 0), axis=1)

    up = lax.all_gather(w_up.T, ("x", "c"), axis=0, tiled=True)

    own, table = enter(latents, span_id, noise_level, mod_table)
    plus, minus, other = gather_first(own, "z", "yh")
    own_s = swap(own)
    weights = w_query, w_key, w_value
    far, other_plus, other_minus, other_far = gather_rest(plus, minus, other, "z", "yh")
    first_s = swap(join([plus, minus, other]))
    n = rows
    whole = [(i, 0, n) for i in range(4)]
    near = [own, plus, minus, far, own_s, first_s, swap(far)], [*whole, (4, 0, n), (5, 0, 2 * n), (6, 0, n)]
    done = project(near, 0, (), weights, q_gain, k_gain)
    last_s = swap(join([other_plus, other_minus, other_far], tokens=done[:1]))
    away = [other, other_plus, other_minus, other_far, first_s, last_s], [*whole, (4, 2 * n, 3 * n), (5, 0, 3 * n)]
    queries, own_kv = project(away, 1, done, weights, q_gain, k_gain)

    first = gather_first(own_kv, "x", "yl")
    rest = gather_rest(*first, "x", "yl")
    other_w = swap(w_out)
    carry = attend(queries, [own_kv, *first], allowed, None, False, in_hbm(up), other_w[:8, :HD])
    kept, sent = attend(queries, rest, allowed, carry, True)

    down = lax.all_gather(join([w_down], tokens=[kept]), ("x", "c"), axis=0, tiled=True)
    parts = project_out(kept, swap(sent), w_out, other_w, 8)
    attn_sum = functools.reduce(jnp.add, map(wide, scatter_rows(parts[:4], parts[4:])))
    resid = wide(latents) + table[1] * attn_sum
    own = (normed(resid) * (1.0 + table[2])).astype(jnp.bfloat16)
    half = n // 2
    plus, minus = move(own, 0, 1), move(own, 0, -1)
    ring_a = join([own, plus])
    ring_b = join([minus, move(plus[:half], 0, 1), move(minus[half:], 0, -1)])
    plus_a, minus_a = move(ring_a, 1, 1), move(ring_a, 1, -1)
    plus_b, minus_b = move(ring_b, 1, 1), move(ring_b, 1, -1)
    far_a, far_b = move(plus_a, 1, 1), move(minus_b, 1, -1)
    blocks = [far_a, far_b, plus_a, minus_b, plus_b, minus_a, ring_a, ring_b]
    far_a, far_b, plus_a, minus_b, plus_b, minus_a, ring_a, ring_b = feed_forward(blocks, up, down)
    got_a, got_b = move(far_a, 1, -1), move(far_b, 1, 1)
    got_plus_b, got_minus_a = move(plus_b, 1, -1), move(minus_a, 1, 1)
    out = sums(whole_sum(plus_a, got_a), whole_sum(minus_b, got_b))
    got_plus_a, got_minus_b = move(out[0], 1, -1), move(out[1], 1, 1)
    terms = scatter_ring((ring_a, got_plus_a, got_minus_a), (ring_b, got_plus_b, got_minus_b), rows)
    mlp_sum = functools.reduce(jnp.add, map(wide, terms))
    return (resid + table[3] * mlp_sum).astype(jnp.bfloat16)


def solution(mesh):
    fine = Mesh(mesh.devices.reshape([SIZES[a] for a in AXES]), AXES)
    head = ("z", "yh", "c")
    return jax.shard_map(
        on_device,
        mesh=fine,
        in_specs=(
            P(AXES, None),
            P(),
            P(),
            P(),
            P(None, head),
            P(None, head),
            P(None, head),
            P(),
            P(),
            P(head, None),
            P(None, AXES),
            P(AXES, None),
        ),
        out_specs=P(AXES, None),
        check_vma=False,
    )
```

```python
import functools

import jax
import jax.numpy as jnp
from jax import lax
from jax.experimental import pallas as pl
from jax.experimental.pallas import tpu as pltpu
from jax.sharding import Mesh, PartitionSpec as P

HD = 128
AXES = ("yl", "x", "z", "yh", "c")
SIZES = {"yl": 2, "x": 4, "z": 4, "yh": 2, "c": 2}
MIB = 1024 * 1024

epsilon = 1e-06


def normed(values):
    return values * lax.rsqrt(jnp.mean(values * values, axis=-1, keepdims=True) + epsilon)


def take_from(value, axis, offset):
    size = SIZES[axis]
    return lax.ppermute(value, axis, [((i + offset) % size, i) for i in range(size)])


def params(mib=24):
    return pltpu.CompilerParams(vmem_limit_bytes=mib * MIB)


def cost(flops):
    return pl.CostEstimate(flops=flops // 5, bytes_accessed=0, transcendentals=0)


def in_hbm(value):
    return pltpu.with_memory_space_constraint(value, pltpu.HBM)


ANYWHERE = pl.BlockSpec(memory_space=pl.ANY)
WHOLE = pl.BlockSpec(memory_space=pltpu.VMEM)


def join_kernel(count, *refs):
    out_ref, at = refs[-1], 0
    for source in refs[:count]:
        out_ref[pl.ds(at, source.shape[0]), :] = source[...]
        at += source.shape[0]


def join(pieces, tokens=()):
    rows, width = sum(p.shape[0] for p in pieces), pieces[0].shape[1]
    return pl.pallas_call(
        functools.partial(join_kernel, len(pieces)),
        in_specs=[WHOLE] * len(pieces) + [ANYWHERE] * len(tokens),
        out_specs=WHOLE,
        out_shape=jax.ShapeDtypeStruct((rows, width), jnp.bfloat16),
        compiler_params=params(),
        cost_estimate=cost(1),
        name="join",
    )(*pieces, *tokens)


def tie_kernel(*refs):
    pass


def tie(values, *tokens):
    return pl.pallas_call(
        tie_kernel,
        in_specs=[ANYWHERE] * (len(values) + len(tokens)),
        out_specs=[ANYWHERE] * len(values),
        out_shape=[jax.ShapeDtypeStruct(v.shape, v.dtype) for v in values],
        input_output_aliases={i: i for i in range(len(values))},
        cost_estimate=cost(1),
        name="tie",
    )(*values, *tokens)


def enter_kernel(span, levels, x_ref, mod_ref, out_ref, table_ref):
    table = mod_ref[...].astype(jnp.float32)
    table_ref[...] = table
    out_ref[...] = (normed(wide(x_ref[...])) * (1.0 + table[0:1])).astype(jnp.bfloat16)


def enter(latents, span_id, noise_level, mod_table):
    rows, width = latents.shape
    spec = pltpu.PrefetchScalarGridSpec(
        num_scalar_prefetch=2,
        grid=(1,),
        in_specs=[
            pl.BlockSpec((rows, width), lambda i, span, levels: (0, 0)),
            pl.BlockSpec((None, 4, width), lambda i, span, levels: (levels[span[0]], 0, 0)),
        ],
        out_specs=[
            pl.BlockSpec((rows, width), lambda i, span, levels: (0, 0)),
            pl.BlockSpec((4, width), lambda i, span, levels: (0, 0)),
        ],
    )
    return pl.pallas_call(
        enter_kernel,
        grid_spec=spec,
        out_shape=[
            jax.ShapeDtypeStruct((rows, width), jnp.bfloat16),
            jax.ShapeDtypeStruct((4, width), jnp.float32),
        ],
        compiler_params=params(),
        cost_estimate=cost(1),
        name="enter",
    )(span_id.reshape(1).astype(jnp.int32), noise_level, in_hbm(latents), in_hbm(mod_table))


def stack(refs, pieces):
    return jnp.concatenate([refs[i][lo:hi, :] for i, lo, hi in pieces], axis=0)


def qkv_kernel(heads, pieces, count, steps, *refs):
    x_refs, w_refs, (q_gain, k_gain) = refs[:count], refs[count : count + 3], refs[count + 3 : count + 5]
    q_ref, kv_ref, acc, w, sems = refs[-5:]
    width = heads * HD
    cut = w.shape[0] // steps
    copies = [
        [
            pltpu.make_async_copy(
                w_refs[i].at[pl.ds(k * cut, cut), :], w.at[pl.ds(k * cut, cut), pl.ds(i * width, width)], sems.at[k, i]
            )
            for i in range(3)
        ]
        for k in range(steps)
    ]
    for row in copies:
        for copy in row:
            copy.start()
    for k, row in enumerate(copies):
        for copy in row:
            copy.wait()
        cols = slice(k * cut, (k + 1) * cut)
        x = jnp.concatenate([x_refs[i][lo:hi, cols] for i, lo, hi in pieces], axis=0)
        part = jnp.dot(x, w[cols, :], preferred_element_type=jnp.float32)
        if k == 0:
            acc[...] = part
        else:
            acc[...] += part
    for h in range(heads):
        at = pl.ds(h * HD, HD)
        q_ref[:, at] = (normed(acc[:, at]) * q_gain[...]).astype(jnp.bfloat16)
        kv_ref[:, at] = (normed(acc[:, pl.ds(width + h * HD, HD)]) * k_gain[...]).astype(jnp.bfloat16)
    kv_ref[:, width:] = acc[:, 2 * width :].astype(jnp.bfloat16)


def project(chunk, place, earlier, weights, q_gain, k_gain):
    blocks, pieces = chunk
    depth, width = weights[0].shape
    rows = sum(hi - lo for _, lo, hi in pieces)
    heads = width // HD
    steps = 4
    same = lambda i: (0, 0)
    ops = [*blocks, *map(in_hbm, weights), q_gain.reshape(1, HD), k_gain.reshape(1, HD), *earlier]
    return pl.pallas_call(
        functools.partial(qkv_kernel, heads, pieces, len(blocks), steps),
        grid=(1,),
        in_specs=[pl.BlockSpec(b.shape, same) for b in blocks]
        + [ANYWHERE] * 3
        + [pl.BlockSpec((1, HD), same)] * 2
        + [ANYWHERE] * len(earlier),
        out_specs=[
            pl.BlockSpec((rows, width), lambda i: (place, 0)),
            pl.BlockSpec((rows, 2 * width), lambda i: (place, 0)),
        ],
        out_shape=[
            jax.ShapeDtypeStruct((2 * rows, width), jnp.bfloat16),
            jax.ShapeDtypeStruct((2 * rows, 2 * width), jnp.bfloat16),
        ],
        input_output_aliases={len(ops) - 2 + i: i for i in range(len(earlier))},
        scratch_shapes=[
            pltpu.VMEM((rows, 3 * width), jnp.float32),
            pltpu.VMEM((depth, 3 * width), jnp.bfloat16),
            pltpu.SemaphoreType.DMA((steps, 3)),
        ],
        compiler_params=params(36),
        cost_estimate=cost(6 * rows * depth * width),
        name="project",
    )(*ops)


def attend_kernel(heads, count, first, last, spare, *refs):
    allowed, q_ref, kv_refs, refs = refs[0], refs[1], refs[2 : 2 + count], refs[2 + count :]
    if not first:
        old_acc, old_sum, refs = refs[0], refs[1], refs[2:]
    refs = refs[spare:]
    if last:
        keep_ref, send_ref, acc, total = refs
    else:
        acc, total = refs
    rows = q_ref.shape[0]
    width = heads * HD
    if first:
        acc[...] = jnp.zeros_like(acc)
        total[...] = jnp.zeros_like(total)
    else:
        acc[...] = old_acc[...]
        total[...] = old_sum[...]
    factor = HD ** (-0.5) * 1.4426950408889634
    half = rows // 2
    for b in range(count):

        @pl.when(allowed[b + (0 if first else 4)] > 0)
        def _(b=b):
            for part in range(4):
                at = pl.ds(part // 2 * half, half)
                keys_at = pl.ds(part % 2 * half, half)
                for h in range(heads):
                    cols = pl.ds(h * HD, HD)
                    keys = kv_refs[b][keys_at, cols]
                    values = kv_refs[b][keys_at, pl.ds(width + h * HD, HD)]
                    scores = lax.dot_general(
                        q_ref[at, cols], keys, (((1,), (1,)), ((), ())), preferred_element_type=jnp.float32
                    )
                    probs = jnp.exp2(scores * factor)
                    lanes = probs[:, :HD]
                    for i in range(1, probs.shape[1] // HD):
                        lanes = lanes + probs[:, i * HD : (i + 1) * HD]
                    total[at, cols] += lanes
                    acc[at, cols] += jnp.dot(
                        probs.astype(jnp.bfloat16), values, preferred_element_type=jnp.float32
                    )

    if last:
        for h in range(heads):
            cols = pl.ds(h * HD, HD)
            denom = jnp.sum(total[:, cols], axis=-1, keepdims=True)
            out = (acc[:, cols] / denom).astype(jnp.bfloat16)
            n = rows // 4
            for i, ref in enumerate((keep_ref, send_ref)):
                ref[:n, cols] = out[i * n : (i + 1) * n]
                ref[n:, cols] = out[(2 + i) * n : (3 + i) * n]


def attend(queries, blocks, allowed, carry, last, *tokens):
    rows, width = queries.shape
    heads = width // HD
    count = len(blocks)
    whole = WHOLE
    state = jax.ShapeDtypeStruct((rows, width), jnp.float32)
    ops = [allowed, queries, *blocks, *(carry or ())]
    if last:
        out_shape = [jax.ShapeDtypeStruct((rows // 2, width), jnp.bfloat16)] * 2
        scratch = [pltpu.VMEM(state.shape, jnp.float32)] * 2
        out_specs = [whole, whole]
    else:
        out_shape, scratch, out_specs = [state, state], [], [whole, whole]
    return pl.pallas_call(
        functools.partial(attend_kernel, heads, count, carry is None, last, len(tokens)),
        in_specs=[pl.BlockSpec(memory_space=pltpu.SMEM)] + [whole] * (len(ops) - 1) + [ANYWHERE] * len(tokens),
        out_specs=out_specs,
        out_shape=out_shape,
        scratch_shapes=scratch,
        compiler_params=params(),
        cost_estimate=cost(4 * count * rows * rows * width),
        name="attend",
    )(*ops, *tokens)


def out_kernel(steps, a_ref, b_ref, own_ref, other_ref, *refs):
    out_refs, (w, sems) = refs[:-2], refs[-2:]
    depth = own_ref.shape[0]
    cut = w.shape[1] // steps
    copies = [
        [
            pltpu.make_async_copy(
                source.at[:, pl.ds(k * cut, cut)], w.at[pl.ds(i * depth, depth), pl.ds(k * cut, cut)], sems.at[k, i]
            )
            for i, source in enumerate((own_ref, other_ref))
        ]
        for k in range(steps)
    ]
    for row in copies:
        for copy in row:
            copy.start()
    x = jnp.concatenate([a_ref[...], b_ref[...]], axis=1)
    for k, row in enumerate(copies):
        for copy in row:
            copy.wait()
        cols = slice(k * cut, (k + 1) * cut)
        r = jnp.dot(x, w[:, cols], preferred_element_type=jnp.float32).astype(jnp.bfloat16)
        n = out_refs[0].shape[0]
        for i, out_ref in enumerate(out_refs):
            out_ref[:, cols] = r[i * n : (i + 1) * n]


def project_out(own_cols, other_cols, own_w, other_w, count):
    depth, width = own_w.shape
    rows = own_cols.shape[0]
    steps = 4
    return pl.pallas_call(
        functools.partial(out_kernel, steps),
        in_specs=[WHOLE, WHOLE, ANYWHERE, ANYWHERE],
        out_specs=[WHOLE] * count,
        out_shape=[jax.ShapeDtypeStruct((rows // count, width), jnp.bfloat16)] * count,
        scratch_shapes=[pltpu.VMEM((2 * depth, width), jnp.bfloat16), pltpu.SemaphoreType.DMA((steps, 2))],
        compiler_params=params(28),
        cost_estimate=cost(4 * rows * depth * width),
        name="project_out",
    )(own_cols, other_cols, in_hbm(own_w), other_w)


def mlp_kernel(count, steps, *refs):
    x_refs, w_refs = refs[:count], refs[count : count + 2]
    out_refs, (acc, hidden, up, down, sems) = refs[-count - 5 : -5], refs[-5:]
    cut = up.shape[1] // steps
    k = pl.program_id(0)
    copies = [
        pltpu.make_async_copy(source.at[:, pl.ds(i * cut, cut)], w.at[:, pl.ds(i * cut, cut)], sems.at[j, i])
        for j, (source, w) in enumerate(zip(w_refs, (up, down)))
        for i in range(steps)
    ]

    @pl.when(k == 0)
    def _():
        for copy in copies:
            copy.start()

    for step in range(steps):

        @pl.when(k == step)
        def _(step=step):
            copies[step].wait()
            x = jnp.concatenate([r[...] for r in x_refs], axis=0)
            w = up[:, step * cut : (step + 1) * cut]
            total = lax.dot_general(x, w, (((1,), (1,)), ((), ())), preferred_element_type=jnp.float32)
            if step > 0:
                total = acc[...] + total
            if step < steps - 1:
                acc[...] = total
            else:
                hidden[...] = jax.nn.gelu(total, approximate=True).astype(jnp.bfloat16)

        @pl.when(k == steps + step)
        def _(step=step):
            copies[steps + step].wait()
            w = down[:, step * cut : (step + 1) * cut]
            r = jnp.dot(hidden[...], w, preferred_element_type=jnp.float32).astype(jnp.bfloat16)
            at = 0
            for out_ref in out_refs:
                n = out_ref.shape[0]
                out_ref[...] = r[at : at + n]
                at += n


def feed_forward(blocks, up, down, *tokens):
    units, width = up.shape
    rows = sum(b.shape[0] for b in blocks)
    steps = 2
    cut = width // steps
    first = lambda k: (0, jnp.minimum(k, steps - 1))
    second = lambda k: (0, jnp.maximum(k - steps, 0))
    return pl.pallas_call(
        functools.partial(mlp_kernel, len(blocks), steps),
        grid=(2 * steps,),
        in_specs=[pl.BlockSpec((b.shape[0], cut), first) for b in blocks] + [ANYWHERE] * (2 + len(tokens)),
        out_specs=[pl.BlockSpec((b.shape[0], cut), second) for b in blocks],
        out_shape=[jax.ShapeDtypeStruct(b.shape, jnp.bfloat16) for b in blocks],
        scratch_shapes=[
            pltpu.VMEM((rows, units), jnp.float32),
            pltpu.VMEM((rows, units), jnp.bfloat16),
            pltpu.VMEM((units, width), jnp.bfloat16),
            pltpu.VMEM((units, width), jnp.bfloat16),
            pltpu.SemaphoreType.DMA((2, steps)),
        ],
        compiler_params=params(60),
        cost_estimate=cost(4 * rows * units * width),
        name="feed_forward",
    )(*blocks, in_hbm(up), in_hbm(down), *tokens)


def swap(value):
    return take_from(value, "c", 1)


def gather_first(own, ring, pair):
    return take_from(own, ring, 1), take_from(own, ring, -1), take_from(own, pair, 1)


def gather_rest(plus, minus, other, ring, pair):
    half = plus.shape[0] // 2
    first = take_from(plus[:half], ring, 1)
    second = take_from(minus[half:], ring, -1)
    other_plus = take_from(other, ring, 1)
    other_minus = take_from(other, ring, -1)
    far = join([first, second])
    return far, other_plus, other_minus, take_from(far, pair, 1)


def move(value, stage, offset):
    pairs = []
    at = lambda yl, z, yh, c: ((yl * 4 + z) * 2 + yh) * 2 + c
    for y in range(4):
        for z in range(4):
            for c in range(2):
                if (c + stage) % 2 == 0:
                    from_y, from_z = y, (z + offset) % 4
                else:
                    from_y, from_z = (y + offset) % 4, z
                pairs.append((at(from_y % 2, from_z, from_y // 2, c), at(y % 2, z, y // 2, c)))
    return lax.ppermute(value, ("yl", "z", "yh", "c"), pairs)


def wide(t):
    return t.astype(jnp.float32)


def sums_kernel(plan, count, *refs):
    for out_ref, terms in zip(refs[count:], plan):
        total = None
        for i, lo, at in terms:
            n = refs[i].shape[0] if at is None else at[1] - at[0]
            part = wide(refs[i][lo : lo + n, :])
            if at is not None and n < out_ref.shape[0]:
                pads = [jnp.zeros((k, part.shape[1]), jnp.float32) for k in (at[0], out_ref.shape[0] - at[1])]
                part = jnp.concatenate([p for p in (pads[0], part, pads[1]) if p.shape[0]], axis=0)
            total = part if total is None else total + part
        out_ref[...] = total.astype(out_ref.dtype)


def sums(*wanted):
    arrays, plan = [], []
    for _, rows, terms in wanted:
        row = []
        for array, lo, at in terms:
            spots = [i for i, a in enumerate(arrays) if a is array]
            if not spots:
                arrays.append(array)
            row.append((spots[0] if spots else len(arrays) - 1, lo, at or (0, rows)))
        plan.append(row)
    width = arrays[0].shape[1]
    return pl.pallas_call(
        functools.partial(sums_kernel, plan, len(arrays)),
        grid=(4,),
        in_specs=[pl.BlockSpec((a.shape[0], width // 4), lambda i: (0, i)) for a in arrays],
        out_specs=[pl.BlockSpec((rows, width // 4), lambda i: (0, i)) for _, rows, _ in wanted],
        out_shape=[jax.ShapeDtypeStruct((rows, width), kind) for kind, rows, _ in wanted],
        compiler_params=params(),
        cost_estimate=cost(1),
        name="sums",
    )(*arrays)


def whole_sum(*terms):
    return jnp.bfloat16, terms[0].shape[0], [(t, 0, None) for t in terms]


def scatter_rows(near, away):
    rows = near[0].shape[0]
    half = rows // 2
    from_minus = take_from(away[1], "z", -1)
    from_plus = take_from(away[2], "z", 1)
    from_pair = take_from(away[3], "yh", 1)
    far_a, far_b, other = sums(
        (jnp.bfloat16, half, [(near[3], 0, None), (from_pair, 0, None)]),
        (jnp.bfloat16, half, [(near[3], half, None), (from_pair, half, None)]),
        whole_sum(away[0], from_plus, from_minus),
    )
    got_a, got_b = take_from(far_a, "z", -1), take_from(far_b, "z", 1)
    got_other = take_from(other, "yh", 1)
    plus, minus = sums(
        (jnp.bfloat16, rows, [(near[1], 0, None), (got_a, 0, (0, half))]),
        (jnp.bfloat16, rows, [(near[2], 0, None), (got_b, 0, (half, rows))]),
    )
    return near[0], take_from(plus, "z", -1), take_from(minus, "z", 1), got_other


def scatter_ring(top, low, rows):
    cut = lambda terms, lo: [(t, lo, None) for t in terms]
    plus, minus, far, own = sums(
        (jnp.bfloat16, rows, cut(top, rows)),
        (jnp.bfloat16, rows, cut(low, 0)),
        (jnp.bfloat16, rows, cut(low, rows)),
        (jnp.float32, rows, cut(top, 0)),
    )
    return own, move(plus, 0, -1), move(minus, 0, 1), move(far, 0, 2)


def on_device(
    latents,
    noise_level,
    context_mask,
    mod_table,
    w_query,
    w_key,
    w_value,
    q_gain,
    k_gain,
    w_out,
    w_up,
    w_down,
):
    rows = latents.shape[0]
    x_id, yl_id = lax.axis_index("x"), lax.axis_index("yl")
    span_id = yl_id * 4 + x_id
    mask_row = lax.dynamic_index_in_dim(context_mask, span_id, 0, keepdims=False)

    from_y = (yl_id + jnp.array([0, 0, 0, 1, 0, 1, 1, 1], jnp.int32)) % 2
    from_x = (x_id + jnp.array([0, 1, 3, 0, 2, 1, 3, 2], jnp.int32)) % 4
    match = (from_y * 4 + from_x)[:, None] == jnp.arange(8, dtype=jnp.int32)[None, :]
    allowed = jnp.sum(jnp.where(match, mask_row[None, :], 0), axis=1)

    up = lax.all_gather(w_up.T, ("x", "c"), axis=0, tiled=True)

    own, table = enter(latents, span_id, noise_level, mod_table)
    plus, minus, other = gather_first(own, "z", "yh")
    own_s = swap(own)
    weights = w_query, w_key, w_value
    far, other_plus, other_minus, other_far = gather_rest(plus, minus, other, "z", "yh")
    first_s = swap(join([plus, minus, other]))
    n = rows
    whole = [(i, 0, n) for i in range(4)]
    near = [own, plus, minus, far, own_s, first_s, swap(far)], [*whole, (4, 0, n), (5, 0, 2 * n), (6, 0, n)]
    done = project(near, 0, (), weights, q_gain, k_gain)
    last_s = swap(join([other_plus, other_minus, other_far], tokens=done[:1]))
    away = [other, other_plus, other_minus, other_far, first_s, last_s], [*whole, (4, 2 * n, 3 * n), (5, 0, 3 * n)]
    queries, own_kv = project(away, 1, done, weights, q_gain, k_gain)

    first = gather_first(own_kv, "x", "yl")
    rest = gather_rest(*first, "x", "yl")
    other_w = swap(w_out)
    carry = attend(queries, [own_kv, *first], allowed, None, False, in_hbm(up), other_w[:8, :HD])
    kept, sent = attend(queries, rest, allowed, carry, True)

    down = lax.all_gather(join([w_down], tokens=[kept]), ("x", "c"), axis=0, tiled=True)
    parts = project_out(kept, swap(sent), w_out, other_w, 8)
    attn_sum = functools.reduce(jnp.add, map(wide, scatter_rows(parts[:4], parts[4:])))
    resid = wide(latents) + table[1] * attn_sum
    own = (normed(resid) * (1.0 + table[2])).astype(jnp.bfloat16)
    plus, minus, far = move(own, 0, 1), move(own, 0, -1), move(own, 0, 2)
    ring_a = join([own, plus])
    ring_b = join([minus, far])
    plus_a, minus_a = move(ring_a, 1, 1), move(ring_a, 1, -1)
    plus_b, minus_b = move(ring_b, 1, 1), move(ring_b, 1, -1)
    far_a, far_b = move(plus_a, 1, 1), move(minus_b, 1, -1)
    blocks = [far_a, far_b, plus_a, minus_b, plus_b, minus_a, ring_a, ring_b]
    far_a, far_b, plus_a, minus_b, plus_b, minus_a, ring_a, ring_b = feed_forward(blocks, up, down)
    got_a, got_b = move(far_a, 1, -1), move(far_b, 1, 1)
    got_plus_b, got_minus_a = move(plus_b, 1, -1), move(minus_a, 1, 1)
    out = sums(whole_sum(plus_a, got_a), whole_sum(minus_b, got_b))
    got_plus_a, got_minus_b = move(out[0], 1, -1), move(out[1], 1, 1)
    terms = scatter_ring((ring_a, got_plus_a, got_minus_a), (ring_b, got_plus_b, got_minus_b), rows)
    mlp_sum = functools.reduce(jnp.add, map(wide, terms))
    return (resid + table[3] * mlp_sum).astype(jnp.bfloat16)


def solution(mesh):
    fine = Mesh(mesh.devices.reshape([SIZES[a] for a in AXES]), AXES)
    head = ("z", "yh", "c")
    return jax.shard_map(
        on_device,
        mesh=fine,
        in_specs=(
            P(AXES, None),
            P(),
            P(),
            P(),
            P(None, head),
            P(None, head),
            P(None, head),
            P(),
            P(),
            P(head, None),
            P(None, AXES),
            P(AXES, None),
        ),
        out_specs=P(AXES, None),
        check_vma=False,
    )
```

```python
import functools

import jax
import jax.numpy as jnp
from jax import lax
from jax.experimental import pallas as pl
from jax.experimental.pallas import tpu as pltpu
from jax.sharding import Mesh, PartitionSpec as P

HD = 128
AXES = ("yl", "x", "z", "yh", "c")
SIZES = {"yl": 2, "x": 4, "z": 4, "yh": 2, "c": 2}
MIB = 1024 * 1024

epsilon = 1e-06


def normed(values):
    return values * lax.rsqrt(jnp.mean(values * values, axis=-1, keepdims=True) + epsilon)


def take_from(value, axis, offset):
    size = SIZES[axis]
    return lax.ppermute(value, axis, [((i + offset) % size, i) for i in range(size)])


def params(mib=24):
    return pltpu.CompilerParams(vmem_limit_bytes=mib * MIB)


def cost(flops):
    return pl.CostEstimate(flops=flops // 5, bytes_accessed=0, transcendentals=0)


def in_hbm(value):
    return pltpu.with_memory_space_constraint(value, pltpu.HBM)


ANYWHERE = pl.BlockSpec(memory_space=pl.ANY)
WHOLE = pl.BlockSpec(memory_space=pltpu.VMEM)


def join_kernel(count, *refs):
    out_ref, at = refs[-1], 0
    for source in refs[:count]:
        out_ref[pl.ds(at, source.shape[0]), :] = source[...]
        at += source.shape[0]


def join(pieces, tokens=()):
    rows, width = sum(p.shape[0] for p in pieces), pieces[0].shape[1]
    return pl.pallas_call(
        functools.partial(join_kernel, len(pieces)),
        in_specs=[WHOLE] * len(pieces) + [ANYWHERE] * len(tokens),
        out_specs=WHOLE,
        out_shape=jax.ShapeDtypeStruct((rows, width), jnp.bfloat16),
        compiler_params=params(),
        cost_estimate=cost(1),
        name="join",
    )(*pieces, *tokens)


def tie_kernel(*refs):
    pass


def tie(values, *tokens):
    return pl.pallas_call(
        tie_kernel,
        in_specs=[ANYWHERE] * (len(values) + len(tokens)),
        out_specs=[ANYWHERE] * len(values),
        out_shape=[jax.ShapeDtypeStruct(v.shape, v.dtype) for v in values],
        input_output_aliases={i: i for i in range(len(values))},
        cost_estimate=cost(1),
        name="tie",
    )(*values, *tokens)


def enter_kernel(span, levels, x_ref, mod_ref, out_ref, table_ref):
    table = mod_ref[...].astype(jnp.float32)
    table_ref[...] = table
    out_ref[...] = (normed(wide(x_ref[...])) * (1.0 + table[0:1])).astype(jnp.bfloat16)


def enter(latents, span_id, noise_level, mod_table):
    rows, width = latents.shape
    spec = pltpu.PrefetchScalarGridSpec(
        num_scalar_prefetch=2,
        grid=(1,),
        in_specs=[
            pl.BlockSpec((rows, width), lambda i, span, levels: (0, 0)),
            pl.BlockSpec((None, 4, width), lambda i, span, levels: (levels[span[0]], 0, 0)),
        ],
        out_specs=[
            pl.BlockSpec((rows, width), lambda i, span, levels: (0, 0)),
            pl.BlockSpec((4, width), lambda i, span, levels: (0, 0)),
        ],
    )
    return pl.pallas_call(
        enter_kernel,
        grid_spec=spec,
        out_shape=[
            jax.ShapeDtypeStruct((rows, width), jnp.bfloat16),
            jax.ShapeDtypeStruct((4, width), jnp.float32),
        ],
        compiler_params=params(),
        cost_estimate=cost(1),
        name="enter",
    )(span_id.reshape(1).astype(jnp.int32), noise_level, in_hbm(latents), in_hbm(mod_table))


def stack(refs, pieces):
    return jnp.concatenate([refs[i][lo:hi, :] for i, lo, hi in pieces], axis=0)


def qkv_kernel(heads, pieces, count, steps, *refs):
    x_refs, w_refs, (q_gain, k_gain) = refs[:count], refs[count : count + 3], refs[count + 3 : count + 5]
    q_ref, kv_ref, acc, w, sems = refs[-5:]
    width = heads * HD
    cut = w.shape[0] // steps
    copies = [
        [
            pltpu.make_async_copy(
                w_refs[i].at[pl.ds(k * cut, cut), :], w.at[pl.ds(k * cut, cut), pl.ds(i * width, width)], sems.at[k, i]
            )
            for i in range(3)
        ]
        for k in range(steps)
    ]
    for row in copies:
        for copy in row:
            copy.start()
    for k, row in enumerate(copies):
        for copy in row:
            copy.wait()
        cols = slice(k * cut, (k + 1) * cut)
        x = jnp.concatenate([x_refs[i][lo:hi, cols] for i, lo, hi in pieces], axis=0)
        part = jnp.dot(x, w[cols, :], preferred_element_type=jnp.float32)
        if k == 0:
            acc[...] = part
        else:
            acc[...] += part
    for h in range(heads):
        at = pl.ds(h * HD, HD)
        q_ref[:, at] = (normed(acc[:, at]) * q_gain[...]).astype(jnp.bfloat16)
        kv_ref[:, at] = (normed(acc[:, pl.ds(width + h * HD, HD)]) * k_gain[...]).astype(jnp.bfloat16)
    kv_ref[:, width:] = acc[:, 2 * width :].astype(jnp.bfloat16)


def project(chunk, place, earlier, weights, q_gain, k_gain):
    blocks, pieces = chunk
    depth, width = weights[0].shape
    rows = sum(hi - lo for _, lo, hi in pieces)
    heads = width // HD
    steps = 4
    same = lambda i: (0, 0)
    ops = [*blocks, *map(in_hbm, weights), q_gain.reshape(1, HD), k_gain.reshape(1, HD), *earlier]
    return pl.pallas_call(
        functools.partial(qkv_kernel, heads, pieces, len(blocks), steps),
        grid=(1,),
        in_specs=[pl.BlockSpec(b.shape, same) for b in blocks]
        + [ANYWHERE] * 3
        + [pl.BlockSpec((1, HD), same)] * 2
        + [ANYWHERE] * len(earlier),
        out_specs=[
            pl.BlockSpec((rows, width), lambda i: (place, 0)),
            pl.BlockSpec((rows, 2 * width), lambda i: (place, 0)),
        ],
        out_shape=[
            jax.ShapeDtypeStruct((2 * rows, width), jnp.bfloat16),
            jax.ShapeDtypeStruct((2 * rows, 2 * width), jnp.bfloat16),
        ],
        input_output_aliases={len(ops) - 2 + i: i for i in range(len(earlier))},
        scratch_shapes=[
            pltpu.VMEM((rows, 3 * width), jnp.float32),
            pltpu.VMEM((depth, 3 * width), jnp.bfloat16),
            pltpu.SemaphoreType.DMA((steps, 3)),
        ],
        compiler_params=params(36),
        cost_estimate=cost(6 * rows * depth * width),
        name="project",
    )(*ops)


def attend_kernel(heads, count, first, last, spare, *refs):
    allowed, q_ref, kv_refs, refs = refs[0], refs[1], refs[2 : 2 + count], refs[2 + count :]
    if not first:
        old_acc, old_sum, refs = refs[0], refs[1], refs[2:]
    refs = refs[spare:]
    if last:
        keep_ref, send_ref, acc, total = refs
    else:
        acc, total = refs
    rows = q_ref.shape[0]
    width = heads * HD
    if first:
        acc[...] = jnp.zeros_like(acc)
        total[...] = jnp.zeros_like(total)
    else:
        acc[...] = old_acc[...]
        total[...] = old_sum[...]
    factor = HD ** (-0.5) * 1.4426950408889634
    half = rows // 2
    for b in range(count):

        @pl.when(allowed[b + (0 if first else 4)] > 0)
        def _(b=b):
            for part in range(4):
                at = pl.ds(part // 2 * half, half)
                keys_at = pl.ds(part % 2 * half, half)
                for h in range(heads):
                    cols = pl.ds(h * HD, HD)
                    keys = kv_refs[b][keys_at, cols]
                    values = kv_refs[b][keys_at, pl.ds(width + h * HD, HD)]
                    scores = lax.dot_general(
                        q_ref[at, cols], keys, (((1,), (1,)), ((), ())), preferred_element_type=jnp.float32
                    )
                    probs = jnp.exp2(scores * factor)
                    lanes = probs[:, :HD]
                    for i in range(1, probs.shape[1] // HD):
                        lanes = lanes + probs[:, i * HD : (i + 1) * HD]
                    total[at, cols] += lanes
                    acc[at, cols] += jnp.dot(
                        probs.astype(jnp.bfloat16), values, preferred_element_type=jnp.float32
                    )

    if last:
        for h in range(heads):
            cols = pl.ds(h * HD, HD)
            denom = jnp.sum(total[:, cols], axis=-1, keepdims=True)
            out = (acc[:, cols] / denom).astype(jnp.bfloat16)
            n = rows // 4
            for i, ref in enumerate((keep_ref, send_ref)):
                ref[:n, cols] = out[i * n : (i + 1) * n]
                ref[n:, cols] = out[(2 + i) * n : (3 + i) * n]


def attend(queries, blocks, allowed, carry, last, *tokens):
    rows, width = queries.shape
    heads = width // HD
    count = len(blocks)
    whole = WHOLE
    state = jax.ShapeDtypeStruct((rows, width), jnp.float32)
    ops = [allowed, queries, *blocks, *(carry or ())]
    if last:
        out_shape = [jax.ShapeDtypeStruct((rows // 2, width), jnp.bfloat16)] * 2
        scratch = [pltpu.VMEM(state.shape, jnp.float32)] * 2
        out_specs = [whole, whole]
    else:
        out_shape, scratch, out_specs = [state, state], [], [whole, whole]
    return pl.pallas_call(
        functools.partial(attend_kernel, heads, count, carry is None, last, len(tokens)),
        in_specs=[pl.BlockSpec(memory_space=pltpu.SMEM)] + [whole] * (len(ops) - 1) + [ANYWHERE] * len(tokens),
        out_specs=out_specs,
        out_shape=out_shape,
        scratch_shapes=scratch,
        compiler_params=params(),
        cost_estimate=cost(4 * count * rows * rows * width),
        name="attend",
    )(*ops, *tokens)


def out_kernel(steps, a_ref, b_ref, own_ref, other_ref, *refs):
    out_refs, (w, sems) = refs[:-2], refs[-2:]
    depth = own_ref.shape[0]
    cut = w.shape[1] // steps
    copies = [
        [
            pltpu.make_async_copy(
                source.at[:, pl.ds(k * cut, cut)], w.at[pl.ds(i * depth, depth), pl.ds(k * cut, cut)], sems.at[k, i]
            )
            for i, source in enumerate((own_ref, other_ref))
        ]
        for k in range(steps)
    ]
    for row in copies:
        for copy in row:
            copy.start()
    x = jnp.concatenate([a_ref[...], b_ref[...]], axis=1)
    for k, row in enumerate(copies):
        for copy in row:
            copy.wait()
        cols = slice(k * cut, (k + 1) * cut)
        r = jnp.dot(x, w[:, cols], preferred_element_type=jnp.float32).astype(jnp.bfloat16)
        n = out_refs[0].shape[0]
        for i, out_ref in enumerate(out_refs):
            out_ref[:, cols] = r[i * n : (i + 1) * n]


def project_out(own_cols, other_cols, own_w, other_w, count):
    depth, width = own_w.shape
    rows = own_cols.shape[0]
    steps = 4
    return pl.pallas_call(
        functools.partial(out_kernel, steps),
        in_specs=[WHOLE, WHOLE, ANYWHERE, ANYWHERE],
        out_specs=[WHOLE] * count,
        out_shape=[jax.ShapeDtypeStruct((rows // count, width), jnp.bfloat16)] * count,
        scratch_shapes=[pltpu.VMEM((2 * depth, width), jnp.bfloat16), pltpu.SemaphoreType.DMA((steps, 2))],
        compiler_params=params(28),
        cost_estimate=cost(4 * rows * depth * width),
        name="project_out",
    )(own_cols, other_cols, in_hbm(own_w), other_w)


def mlp_kernel(count, steps, *refs):
    x_refs, w_refs = refs[:count], refs[count : count + 2]
    out_refs, (acc, hidden, up, down, sems) = refs[-count - 5 : -5], refs[-5:]
    cut = up.shape[1] // steps
    k = pl.program_id(0)
    copies = [
        pltpu.make_async_copy(source.at[:, pl.ds(i * cut, cut)], w.at[:, pl.ds(i * cut, cut)], sems.at[j, i])
        for j, (source, w) in enumerate(zip(w_refs, (up, down)))
        for i in range(steps)
    ]

    @pl.when(k == 0)
    def _():
        for copy in copies:
            copy.start()

    for step in range(steps):

        @pl.when(k == step)
        def _(step=step):
            copies[step].wait()
            x = jnp.concatenate([r[...] for r in x_refs], axis=0)
            w = up[:, step * cut : (step + 1) * cut]
            total = lax.dot_general(x, w, (((1,), (1,)), ((), ())), preferred_element_type=jnp.float32)
            if step > 0:
                total = acc[...] + total
            if step < steps - 1:
                acc[...] = total
            else:
                hidden[...] = jax.nn.gelu(total, approximate=True).astype(jnp.bfloat16)

        @pl.when(k == steps + step)
        def _(step=step):
            copies[steps + step].wait()
            w = down[:, step * cut : (step + 1) * cut]
            r = jnp.dot(hidden[...], w, preferred_element_type=jnp.float32).astype(jnp.bfloat16)
            at = 0
            for out_ref in out_refs:
                n = out_ref.shape[0]
                out_ref[...] = r[at : at + n]
                at += n


def feed_forward(blocks, up, down, *tokens):
    units, width = up.shape
    rows = sum(b.shape[0] for b in blocks)
    steps = 2
    cut = width // steps
    first = lambda k: (0, jnp.minimum(k, steps - 1))
    second = lambda k: (0, jnp.maximum(k - steps, 0))
    return pl.pallas_call(
        functools.partial(mlp_kernel, len(blocks), steps),
        grid=(2 * steps,),
        in_specs=[pl.BlockSpec((b.shape[0], cut), first) for b in blocks] + [ANYWHERE] * (2 + len(tokens)),
        out_specs=[pl.BlockSpec((b.shape[0], cut), second) for b in blocks],
        out_shape=[jax.ShapeDtypeStruct(b.shape, jnp.bfloat16) for b in blocks],
        scratch_shapes=[
            pltpu.VMEM((rows, units), jnp.float32),
            pltpu.VMEM((rows, units), jnp.bfloat16),
            pltpu.VMEM((units, width), jnp.bfloat16),
            pltpu.VMEM((units, width), jnp.bfloat16),
            pltpu.SemaphoreType.DMA((2, steps)),
        ],
        compiler_params=params(60),
        cost_estimate=cost(4 * rows * units * width),
        name="feed_forward",
    )(*blocks, in_hbm(up), in_hbm(down), *tokens)


def swap(value):
    return take_from(value, "c", 1)


def gather_first(own, ring, pair):
    return take_from(own, ring, 1), take_from(own, ring, -1), take_from(own, pair, 1)


def gather_rest(plus, minus, other, ring, pair):
    half = plus.shape[0] // 2
    first = take_from(plus[:half], ring, 1)
    second = take_from(minus[half:], ring, -1)
    other_plus = take_from(other, ring, 1)
    other_minus = take_from(other, ring, -1)
    far = join([first, second])
    return far, other_plus, other_minus, take_from(far, pair, 1)


def move(value, stage, offset):
    pairs = []
    at = lambda yl, z, yh, c: ((yl * 4 + z) * 2 + yh) * 2 + c
    for y in range(4):
        for z in range(4):
            for c in range(2):
                if (c + stage) % 2 == 0:
                    from_y, from_z = y, (z + offset) % 4
                else:
                    from_y, from_z = (y + offset) % 4, z
                pairs.append((at(from_y % 2, from_z, from_y // 2, c), at(y % 2, z, y // 2, c)))
    return lax.ppermute(value, ("yl", "z", "yh", "c"), pairs)


def wide(t):
    return t.astype(jnp.float32)


def sums_kernel(plan, count, *refs):
    for out_ref, terms in zip(refs[count:], plan):
        total = None
        for i, lo, at in terms:
            n = refs[i].shape[0] if at is None else at[1] - at[0]
            part = wide(refs[i][lo : lo + n, :])
            if at is not None and n < out_ref.shape[0]:
                pads = [jnp.zeros((k, part.shape[1]), jnp.float32) for k in (at[0], out_ref.shape[0] - at[1])]
                part = jnp.concatenate([p for p in (pads[0], part, pads[1]) if p.shape[0]], axis=0)
            total = part if total is None else total + part
        out_ref[...] = total.astype(out_ref.dtype)


def sums(*wanted):
    arrays, plan = [], []
    for _, rows, terms in wanted:
        row = []
        for array, lo, at in terms:
            spots = [i for i, a in enumerate(arrays) if a is array]
            if not spots:
                arrays.append(array)
            row.append((spots[0] if spots else len(arrays) - 1, lo, at or (0, rows)))
        plan.append(row)
    width = arrays[0].shape[1]
    return pl.pallas_call(
        functools.partial(sums_kernel, plan, len(arrays)),
        grid=(2,),
        in_specs=[pl.BlockSpec((a.shape[0], width // 2), lambda i: (0, i)) for a in arrays],
        out_specs=[pl.BlockSpec((rows, width // 2), lambda i: (0, i)) for _, rows, _ in wanted],
        out_shape=[jax.ShapeDtypeStruct((rows, width), kind) for kind, rows, _ in wanted],
        compiler_params=params(),
        cost_estimate=cost(1),
        name="sums",
    )(*arrays)


def whole_sum(*terms):
    return jnp.bfloat16, terms[0].shape[0], [(t, 0, None) for t in terms]


def scatter_rows(near, away):
    rows = near[0].shape[0]
    half = rows // 2
    from_minus = take_from(away[1], "z", -1)
    from_plus = take_from(away[2], "z", 1)
    from_pair = take_from(away[3], "yh", 1)
    far_a, far_b, other = sums(
        (jnp.bfloat16, half, [(near[3], 0, None), (from_pair, 0, None)]),
        (jnp.bfloat16, half, [(near[3], half, None), (from_pair, half, None)]),
        whole_sum(away[0], from_plus, from_minus),
    )
    got_a, got_b = take_from(far_a, "z", -1), take_from(far_b, "z", 1)
    got_other = take_from(other, "yh", 1)
    plus, minus = sums(
        (jnp.bfloat16, rows, [(near[1], 0, None), (got_a, 0, (0, half))]),
        (jnp.bfloat16, rows, [(near[2], 0, None), (got_b, 0, (half, rows))]),
    )
    return near[0], take_from(plus, "z", -1), take_from(minus, "z", 1), got_other


def scatter_ring(top, low, rows):
    cut = lambda terms, lo: [(t, lo, None) for t in terms]
    plus, minus, far, own = sums(
        (jnp.bfloat16, rows, cut(top, rows)),
        (jnp.bfloat16, rows, cut(low, 0)),
        (jnp.bfloat16, rows, cut(low, rows)),
        (jnp.float32, rows, cut(top, 0)),
    )
    return own, move(plus, 0, -1), move(minus, 0, 1), move(far, 0, 2)


def on_device(
    latents,
    noise_level,
    context_mask,
    mod_table,
    w_query,
    w_key,
    w_value,
    q_gain,
    k_gain,
    w_out,
    w_up,
    w_down,
):
    rows = latents.shape[0]
    x_id, yl_id = lax.axis_index("x"), lax.axis_index("yl")
    span_id = yl_id * 4 + x_id
    mask_row = lax.dynamic_index_in_dim(context_mask, span_id, 0, keepdims=False)

    from_y = (yl_id + jnp.array([0, 0, 0, 1, 0, 1, 1, 1], jnp.int32)) % 2
    from_x = (x_id + jnp.array([0, 1, 3, 0, 2, 1, 3, 2], jnp.int32)) % 4
    match = (from_y * 4 + from_x)[:, None] == jnp.arange(8, dtype=jnp.int32)[None, :]
    allowed = jnp.sum(jnp.where(match, mask_row[None, :], 0), axis=1)

    up = lax.all_gather(w_up.T, ("x", "c"), axis=0, tiled=True)

    own, table = enter(latents, span_id, noise_level, mod_table)
    plus, minus, other = gather_first(own, "z", "yh")
    own_s = swap(own)
    weights = w_query, w_key, w_value
    far = take_from(own, "z", 2)
    other_plus, other_minus = take_from(other, "z", 1), take_from(other, "z", -1)
    other_far = take_from(far, "yh", 1)
    first_s = swap(join([plus, minus, other], tokens=[far]))
    n = rows
    whole = [(i, 0, n) for i in range(4)]
    near = [own, plus, minus, far, own_s, first_s, swap(far)], [*whole, (4, 0, n), (5, 0, 2 * n), (6, 0, n)]
    done = project(near, 0, (), weights, q_gain, k_gain)
    last_s = swap(join([other_plus, other_minus, other_far], tokens=done[:1]))
    away = [other, other_plus, other_minus, other_far, first_s, last_s], [*whole, (4, 2 * n, 3 * n), (5, 0, 3 * n)]
    queries, own_kv = project(away, 1, done, weights, q_gain, k_gain)

    first = gather_first(own_kv, "x", "yl")
    rest = gather_rest(*first, "x", "yl")
    other_w = swap(w_out)
    carry = attend(queries, [own_kv, *first], allowed, None, False, in_hbm(up), other_w[:8, :HD])
    kept, sent = attend(queries, rest, allowed, carry, True)

    down = lax.all_gather(join([w_down], tokens=[kept]), ("x", "c"), axis=0, tiled=True)
    parts = project_out(kept, swap(sent), w_out, other_w, 8)
    attn_sum = functools.reduce(jnp.add, map(wide, scatter_rows(parts[:4], parts[4:])))
    resid = wide(latents) + table[1] * attn_sum
    own = (normed(resid) * (1.0 + table[2])).astype(jnp.bfloat16)
    plus, minus, far = move(own, 0, 1), move(own, 0, -1), move(own, 0, 2)
    ring_a = join([own, plus])
    ring_b = join([minus, far])
    plus_a, minus_a = move(ring_a, 1, 1), move(ring_a, 1, -1)
    plus_b, minus_b = move(ring_b, 1, 1), move(ring_b, 1, -1)
    far_a, far_b = move(plus_a, 1, 1), move(minus_b, 1, -1)
    blocks = [far_a, far_b, plus_a, minus_b, plus_b, minus_a, ring_a, ring_b]
    far_a, far_b, plus_a, minus_b, plus_b, minus_a, ring_a, ring_b = feed_forward(blocks, up, down)
    got_a, got_b = move(far_a, 1, -1), move(far_b, 1, 1)
    got_plus_b, got_minus_a = move(plus_b, 1, -1), move(minus_a, 1, 1)
    out = sums(whole_sum(plus_a, got_a), whole_sum(minus_b, got_b))
    got_plus_a, got_minus_b = move(out[0], 1, -1), move(out[1], 1, 1)
    terms = scatter_ring((ring_a, got_plus_a, got_minus_a), (ring_b, got_plus_b, got_minus_b), rows)
    mlp_sum = functools.reduce(jnp.add, map(wide, terms))
    return (resid + table[3] * mlp_sum).astype(jnp.bfloat16)


def solution(mesh):
    fine = Mesh(mesh.devices.reshape([SIZES[a] for a in AXES]), AXES)
    head = ("z", "yh", "c")
    return jax.shard_map(
        on_device,
        mesh=fine,
        in_specs=(
            P(AXES, None),
            P(),
            P(),
            P(),
            P(None, head),
            P(None, head),
            P(None, head),
            P(),
            P(),
            P(head, None),
            P(None, AXES),
            P(AXES, None),
        ),
        out_specs=P(AXES, None),
        check_vma=False,
    )
```

```python
import functools

import jax
import jax.numpy as jnp
from jax import lax
from jax.experimental import pallas as pl
from jax.experimental.pallas import tpu as pltpu
from jax.sharding import Mesh, PartitionSpec as P

HD = 128
AXES = ("yl", "x", "z", "yh", "c")
SIZES = {"yl": 2, "x": 4, "z": 4, "yh": 2, "c": 2}
MIB = 1024 * 1024

epsilon = 1e-06


def normed(values):
    return values * lax.rsqrt(jnp.mean(values * values, axis=-1, keepdims=True) + epsilon)


def take_from(value, axis, offset):
    size = SIZES[axis]
    return lax.ppermute(value, axis, [((i + offset) % size, i) for i in range(size)])


def params(mib=24):
    return pltpu.CompilerParams(vmem_limit_bytes=mib * MIB)


def cost(flops):
    return pl.CostEstimate(flops=flops // 5, bytes_accessed=0, transcendentals=0)


def in_hbm(value):
    return pltpu.with_memory_space_constraint(value, pltpu.HBM)


ANYWHERE = pl.BlockSpec(memory_space=pl.ANY)
WHOLE = pl.BlockSpec(memory_space=pltpu.VMEM)


def join_kernel(count, *refs):
    out_ref, at = refs[-1], 0
    for source in refs[:count]:
        out_ref[pl.ds(at, source.shape[0]), :] = source[...]
        at += source.shape[0]


def join(pieces, tokens=()):
    rows, width = sum(p.shape[0] for p in pieces), pieces[0].shape[1]
    return pl.pallas_call(
        functools.partial(join_kernel, len(pieces)),
        in_specs=[WHOLE] * len(pieces) + [ANYWHERE] * len(tokens),
        out_specs=WHOLE,
        out_shape=jax.ShapeDtypeStruct((rows, width), jnp.bfloat16),
        compiler_params=params(),
        cost_estimate=cost(1),
        name="join",
    )(*pieces, *tokens)


def tie_kernel(*refs):
    pass


def tie(values, *tokens):
    return pl.pallas_call(
        tie_kernel,
        in_specs=[ANYWHERE] * (len(values) + len(tokens)),
        out_specs=[ANYWHERE] * len(values),
        out_shape=[jax.ShapeDtypeStruct(v.shape, v.dtype) for v in values],
        input_output_aliases={i: i for i in range(len(values))},
        cost_estimate=cost(1),
        name="tie",
    )(*values, *tokens)


def enter_kernel(span, levels, x_ref, mod_ref, out_ref, table_ref):
    table = mod_ref[...].astype(jnp.float32)
    table_ref[...] = table
    out_ref[...] = (normed(wide(x_ref[...])) * (1.0 + table[0:1])).astype(jnp.bfloat16)


def enter(latents, span_id, noise_level, mod_table):
    rows, width = latents.shape
    spec = pltpu.PrefetchScalarGridSpec(
        num_scalar_prefetch=2,
        grid=(1,),
        in_specs=[
            pl.BlockSpec((rows, width), lambda i, span, levels: (0, 0)),
            pl.BlockSpec((None, 4, width), lambda i, span, levels: (levels[span[0]], 0, 0)),
        ],
        out_specs=[
            pl.BlockSpec((rows, width), lambda i, span, levels: (0, 0)),
            pl.BlockSpec((4, width), lambda i, span, levels: (0, 0)),
        ],
    )
    return pl.pallas_call(
        enter_kernel,
        grid_spec=spec,
        out_shape=[
            jax.ShapeDtypeStruct((rows, width), jnp.bfloat16),
            jax.ShapeDtypeStruct((4, width), jnp.float32),
        ],
        compiler_params=params(),
        cost_estimate=cost(1),
        name="enter",
    )(span_id.reshape(1).astype(jnp.int32), noise_level, in_hbm(latents), in_hbm(mod_table))


def stack(refs, pieces):
    return jnp.concatenate([refs[i][lo:hi, :] for i, lo, hi in pieces], axis=0)


def qkv_kernel(heads, pieces, count, steps, *refs):
    x_refs, w_refs, (q_gain, k_gain) = refs[:count], refs[count : count + 3], refs[count + 3 : count + 5]
    q_ref, kv_ref, acc, w, sems = refs[-5:]
    width = heads * HD
    cut = w.shape[0] // steps
    copies = [
        [
            pltpu.make_async_copy(
                w_refs[i].at[pl.ds(k * cut, cut), :], w.at[pl.ds(k * cut, cut), pl.ds(i * width, width)], sems.at[k, i]
            )
            for i in range(3)
        ]
        for k in range(steps)
    ]
    for row in copies:
        for copy in row:
            copy.start()
    for k, row in enumerate(copies):
        for copy in row:
            copy.wait()
        cols = slice(k * cut, (k + 1) * cut)
        x = jnp.concatenate([x_refs[i][lo:hi, cols] for i, lo, hi in pieces], axis=0)
        part = jnp.dot(x, w[cols, :], preferred_element_type=jnp.float32)
        if k == 0:
            acc[...] = part
        else:
            acc[...] += part
    for h in range(heads):
        at = pl.ds(h * HD, HD)
        q_ref[:, at] = (normed(acc[:, at]) * q_gain[...]).astype(jnp.bfloat16)
        kv_ref[:, at] = (normed(acc[:, pl.ds(width + h * HD, HD)]) * k_gain[...]).astype(jnp.bfloat16)
    kv_ref[:, width:] = acc[:, 2 * width :].astype(jnp.bfloat16)


def project(chunk, place, earlier, weights, q_gain, k_gain):
    blocks, pieces = chunk
    depth, width = weights[0].shape
    rows = sum(hi - lo for _, lo, hi in pieces)
    heads = width // HD
    steps = 4
    same = lambda i: (0, 0)
    ops = [*blocks, *map(in_hbm, weights), q_gain.reshape(1, HD), k_gain.reshape(1, HD), *earlier]
    return pl.pallas_call(
        functools.partial(qkv_kernel, heads, pieces, len(blocks), steps),
        grid=(1,),
        in_specs=[pl.BlockSpec(b.shape, same) for b in blocks]
        + [ANYWHERE] * 3
        + [pl.BlockSpec((1, HD), same)] * 2
        + [ANYWHERE] * len(earlier),
        out_specs=[
            pl.BlockSpec((rows, width), lambda i: (place, 0)),
            pl.BlockSpec((rows, 2 * width), lambda i: (place, 0)),
        ],
        out_shape=[
            jax.ShapeDtypeStruct((2 * rows, width), jnp.bfloat16),
            jax.ShapeDtypeStruct((2 * rows, 2 * width), jnp.bfloat16),
        ],
        input_output_aliases={len(ops) - 2 + i: i for i in range(len(earlier))},
        scratch_shapes=[
            pltpu.VMEM((rows, 3 * width), jnp.float32),
            pltpu.VMEM((depth, 3 * width), jnp.bfloat16),
            pltpu.SemaphoreType.DMA((steps, 3)),
        ],
        compiler_params=params(36),
        cost_estimate=cost(6 * rows * depth * width),
        name="project",
    )(*ops)


def attend_kernel(heads, count, first, last, spare, *refs):
    allowed, q_ref, kv_refs, refs = refs[0], refs[1], refs[2 : 2 + count], refs[2 + count :]
    if not first:
        old_acc, old_sum, refs = refs[0], refs[1], refs[2:]
    refs = refs[spare:]
    if last:
        keep_ref, send_ref, acc, total = refs
    else:
        acc, total = refs
    rows = q_ref.shape[0]
    width = heads * HD
    if first:
        acc[...] = jnp.zeros_like(acc)
        total[...] = jnp.zeros_like(total)
    else:
        acc[...] = old_acc[...]
        total[...] = old_sum[...]
    factor = HD ** (-0.5) * 1.4426950408889634
    half = rows // 2
    for b in range(count):

        @pl.when(allowed[b + (0 if first else 4)] > 0)
        def _(b=b):
            for part in range(4):
                at = pl.ds(part // 2 * half, half)
                keys_at = pl.ds(part % 2 * half, half)
                for h in range(heads):
                    cols = pl.ds(h * HD, HD)
                    keys = kv_refs[b][keys_at, cols]
                    values = kv_refs[b][keys_at, pl.ds(width + h * HD, HD)]
                    scores = lax.dot_general(
                        q_ref[at, cols], keys, (((1,), (1,)), ((), ())), preferred_element_type=jnp.float32
                    )
                    probs = jnp.exp2(scores * factor)
                    lanes = probs[:, :HD]
                    for i in range(1, probs.shape[1] // HD):
                        lanes = lanes + probs[:, i * HD : (i + 1) * HD]
                    total[at, cols] += lanes
                    acc[at, cols] += jnp.dot(
                        probs.astype(jnp.bfloat16), values, preferred_element_type=jnp.float32
                    )

    if last:
        for h in range(heads):
            cols = pl.ds(h * HD, HD)
            denom = jnp.sum(total[:, cols], axis=-1, keepdims=True)
            out = (acc[:, cols] / denom).astype(jnp.bfloat16)
            n = rows // 4
            for i, ref in enumerate((keep_ref, send_ref)):
                ref[:n, cols] = out[i * n : (i + 1) * n]
                ref[n:, cols] = out[(2 + i) * n : (3 + i) * n]


def attend(queries, blocks, allowed, carry, last, *tokens):
    rows, width = queries.shape
    heads = width // HD
    count = len(blocks)
    whole = WHOLE
    state = jax.ShapeDtypeStruct((rows, width), jnp.float32)
    ops = [allowed, queries, *blocks, *(carry or ())]
    if last:
        out_shape = [jax.ShapeDtypeStruct((rows // 2, width), jnp.bfloat16)] * 2
        scratch = [pltpu.VMEM(state.shape, jnp.float32)] * 2
        out_specs = [whole, whole]
    else:
        out_shape, scratch, out_specs = [state, state], [], [whole, whole]
    return pl.pallas_call(
        functools.partial(attend_kernel, heads, count, carry is None, last, len(tokens)),
        in_specs=[pl.BlockSpec(memory_space=pltpu.SMEM)] + [whole] * (len(ops) - 1) + [ANYWHERE] * len(tokens),
        out_specs=out_specs,
        out_shape=out_shape,
        scratch_shapes=scratch,
        compiler_params=params(),
        cost_estimate=cost(4 * count * rows * rows * width),
        name="attend",
    )(*ops, *tokens)


def out_kernel(steps, a_ref, b_ref, own_ref, other_ref, *refs):
    out_refs, (w, sems) = refs[:-2], refs[-2:]
    depth = own_ref.shape[0]
    cut = w.shape[1] // steps
    copies = [
        [
            pltpu.make_async_copy(
                source.at[:, pl.ds(k * cut, cut)], w.at[pl.ds(i * depth, depth), pl.ds(k * cut, cut)], sems.at[k, i]
            )
            for i, source in enumerate((own_ref, other_ref))
        ]
        for k in range(steps)
    ]
    for row in copies:
        for copy in row:
            copy.start()
    x = jnp.concatenate([a_ref[...], b_ref[...]], axis=1)
    for k, row in enumerate(copies):
        for copy in row:
            copy.wait()
        cols = slice(k * cut, (k + 1) * cut)
        r = jnp.dot(x, w[:, cols], preferred_element_type=jnp.float32).astype(jnp.bfloat16)
        n = out_refs[0].shape[0]
        for i, out_ref in enumerate(out_refs):
            out_ref[:, cols] = r[i * n : (i + 1) * n]


def project_out(own_cols, other_cols, own_w, other_w, count):
    depth, width = own_w.shape
    rows = own_cols.shape[0]
    steps = 4
    return pl.pallas_call(
        functools.partial(out_kernel, steps),
        in_specs=[WHOLE, WHOLE, ANYWHERE, ANYWHERE],
        out_specs=[WHOLE] * count,
        out_shape=[jax.ShapeDtypeStruct((rows // count, width), jnp.bfloat16)] * count,
        scratch_shapes=[pltpu.VMEM((2 * depth, width), jnp.bfloat16), pltpu.SemaphoreType.DMA((steps, 2))],
        compiler_params=params(28),
        cost_estimate=cost(4 * rows * depth * width),
        name="project_out",
    )(own_cols, other_cols, in_hbm(own_w), other_w)


def mlp_kernel(count, steps, *refs):
    x_refs, w_refs = refs[:count], refs[count : count + 2]
    out_refs, (acc, hidden, up, down, sems) = refs[-count - 5 : -5], refs[-5:]
    cut = up.shape[1] // steps
    k = pl.program_id(0)
    copies = [
        pltpu.make_async_copy(source.at[:, pl.ds(i * cut, cut)], w.at[:, pl.ds(i * cut, cut)], sems.at[j, i])
        for j, (source, w) in enumerate(zip(w_refs, (up, down)))
        for i in range(steps)
    ]

    @pl.when(k == 0)
    def _():
        for copy in copies:
            copy.start()

    for step in range(steps):

        @pl.when(k == step)
        def _(step=step):
            copies[step].wait()
            x = jnp.concatenate([r[...] for r in x_refs], axis=0)
            w = up[:, step * cut : (step + 1) * cut]
            total = lax.dot_general(x, w, (((1,), (1,)), ((), ())), preferred_element_type=jnp.float32)
            if step > 0:
                total = acc[...] + total
            if step < steps - 1:
                acc[...] = total
            else:
                hidden[...] = jax.nn.gelu(total, approximate=True).astype(jnp.bfloat16)

        @pl.when(k == steps + step)
        def _(step=step):
            copies[steps + step].wait()
            w = down[:, step * cut : (step + 1) * cut]
            r = jnp.dot(hidden[...], w, preferred_element_type=jnp.float32).astype(jnp.bfloat16)
            at = 0
            for out_ref in out_refs:
                n = out_ref.shape[0]
                out_ref[...] = r[at : at + n]
                at += n


def feed_forward(blocks, up, down, *tokens):
    units, width = up.shape
    rows = sum(b.shape[0] for b in blocks)
    steps = 2
    cut = width // steps
    first = lambda k: (0, jnp.minimum(k, steps - 1))
    second = lambda k: (0, jnp.maximum(k - steps, 0))
    return pl.pallas_call(
        functools.partial(mlp_kernel, len(blocks), steps),
        grid=(2 * steps,),
        in_specs=[pl.BlockSpec((b.shape[0], cut), first) for b in blocks] + [ANYWHERE] * (2 + len(tokens)),
        out_specs=[pl.BlockSpec((b.shape[0], cut), second) for b in blocks],
        out_shape=[jax.ShapeDtypeStruct(b.shape, jnp.bfloat16) for b in blocks],
        scratch_shapes=[
            pltpu.VMEM((rows, units), jnp.float32),
            pltpu.VMEM((rows, units), jnp.bfloat16),
            pltpu.VMEM((units, width), jnp.bfloat16),
            pltpu.VMEM((units, width), jnp.bfloat16),
            pltpu.SemaphoreType.DMA((2, steps)),
        ],
        compiler_params=params(60),
        cost_estimate=cost(4 * rows * units * width),
        name="feed_forward",
    )(*blocks, in_hbm(up), in_hbm(down), *tokens)


def swap(value):
    return take_from(value, "c", 1)


def gather_first(own, ring, pair):
    return take_from(own, ring, 1), take_from(own, ring, -1), take_from(own, pair, 1)


def gather_rest(plus, minus, other, ring, pair):
    half = plus.shape[0] // 2
    first = take_from(plus[:half], ring, 1)
    second = take_from(minus[half:], ring, -1)
    other_plus = take_from(other, ring, 1)
    other_minus = take_from(other, ring, -1)
    far = join([first, second])
    return far, other_plus, other_minus, take_from(far, pair, 1)


def move(value, stage, offset):
    pairs = []
    at = lambda yl, z, yh, c: ((yl * 4 + z) * 2 + yh) * 2 + c
    for y in range(4):
        for z in range(4):
            for c in range(2):
                if (c + stage) % 2 == 0:
                    from_y, from_z = y, (z + offset) % 4
                else:
                    from_y, from_z = (y + offset) % 4, z
                pairs.append((at(from_y % 2, from_z, from_y // 2, c), at(y % 2, z, y // 2, c)))
    return lax.ppermute(value, ("yl", "z", "yh", "c"), pairs)


def wide(t):
    return t.astype(jnp.float32)


def sums_kernel(plan, count, *refs):
    for out_ref, terms in zip(refs[count:], plan):
        total = None
        for i, lo, at in terms:
            n = refs[i].shape[0] if at is None else at[1] - at[0]
            part = wide(refs[i][lo : lo + n, :])
            if at is not None and n < out_ref.shape[0]:
                pads = [jnp.zeros((k, part.shape[1]), jnp.float32) for k in (at[0], out_ref.shape[0] - at[1])]
                part = jnp.concatenate([p for p in (pads[0], part, pads[1]) if p.shape[0]], axis=0)
            total = part if total is None else total + part
        out_ref[...] = total.astype(out_ref.dtype)


def sums(*wanted):
    arrays, plan = [], []
    for _, rows, terms in wanted:
        row = []
        for array, lo, at in terms:
            spots = [i for i, a in enumerate(arrays) if a is array]
            if not spots:
                arrays.append(array)
            row.append((spots[0] if spots else len(arrays) - 1, lo, at or (0, rows)))
        plan.append(row)
    width = arrays[0].shape[1]
    return pl.pallas_call(
        functools.partial(sums_kernel, plan, len(arrays)),
        grid=(2,),
        in_specs=[pl.BlockSpec((a.shape[0], width // 2), lambda i: (0, i)) for a in arrays],
        out_specs=[pl.BlockSpec((rows, width // 2), lambda i: (0, i)) for _, rows, _ in wanted],
        out_shape=[jax.ShapeDtypeStruct((rows, width), kind) for kind, rows, _ in wanted],
        compiler_params=params(),
        cost_estimate=cost(1),
        name="sums",
    )(*arrays)


def whole_sum(*terms):
    return jnp.bfloat16, terms[0].shape[0], [(t, 0, None) for t in terms]


def scatter_rows(near, away):
    rows = near[0].shape[0]
    half = rows // 2
    from_minus = take_from(away[1], "z", -1)
    from_plus = take_from(away[2], "z", 1)
    from_pair = take_from(away[3], "yh", 1)
    far_a, far_b, other = sums(
        (jnp.bfloat16, half, [(near[3], 0, None), (from_pair, 0, None)]),
        (jnp.bfloat16, half, [(near[3], half, None), (from_pair, half, None)]),
        whole_sum(away[0], from_plus, from_minus),
    )
    got_a, got_b = take_from(far_a, "z", -1), take_from(far_b, "z", 1)
    got_other = take_from(other, "yh", 1)
    plus, minus = sums(
        (jnp.bfloat16, rows, [(near[1], 0, None), (got_a, 0, (0, half))]),
        (jnp.bfloat16, rows, [(near[2], 0, None), (got_b, 0, (half, rows))]),
    )
    return near[0], take_from(plus, "z", -1), take_from(minus, "z", 1), got_other


def scatter_ring(top, low, rows):
    cut = lambda terms, lo: [(t, lo, None) for t in terms]
    plus, minus, far, own = sums(
        (jnp.bfloat16, rows, cut(top, rows)),
        (jnp.bfloat16, rows, cut(low, 0)),
        (jnp.bfloat16, rows, cut(low, rows)),
        (jnp.float32, rows, cut(top, 0)),
    )
    return own, move(plus, 0, -1), move(minus, 0, 1), move(far, 0, 2)


def on_device(
    latents,
    noise_level,
    context_mask,
    mod_table,
    w_query,
    w_key,
    w_value,
    q_gain,
    k_gain,
    w_out,
    w_up,
    w_down,
):
    rows = latents.shape[0]
    x_id, yl_id = lax.axis_index("x"), lax.axis_index("yl")
    span_id = yl_id * 4 + x_id
    mask_row = lax.dynamic_index_in_dim(context_mask, span_id, 0, keepdims=False)

    from_y = (yl_id + jnp.array([0, 0, 0, 1, 0, 1, 1, 1], jnp.int32)) % 2
    from_x = (x_id + jnp.array([0, 1, 3, 0, 2, 1, 3, 2], jnp.int32)) % 4
    match = (from_y * 4 + from_x)[:, None] == jnp.arange(8, dtype=jnp.int32)[None, :]
    allowed = jnp.sum(jnp.where(match, mask_row[None, :], 0), axis=1)

    up = lax.all_gather(w_up.T, ("x", "c"), axis=0, tiled=True)

    own, table = enter(latents, span_id, noise_level, mod_table)
    plus, minus, other = gather_first(own, "z", "yh")
    own_s = swap(own)
    weights = w_query, w_key, w_value
    far, other_plus, other_minus, other_far = gather_rest(plus, minus, other, "z", "yh")
    first_s = swap(join([plus, minus, other]))
    n = rows
    whole = [(i, 0, n) for i in range(4)]
    near = [own, plus, minus, far, own_s, first_s, swap(far)], [*whole, (4, 0, n), (5, 0, 2 * n), (6, 0, n)]
    done = project(near, 0, (), weights, q_gain, k_gain)
    last_s = swap(join([other_plus, other_minus, other_far], tokens=done[:1]))
    away = [other, other_plus, other_minus, other_far, first_s, last_s], [*whole, (4, 2 * n, 3 * n), (5, 0, 3 * n)]
    queries, own_kv = project(away, 1, done, weights, q_gain, k_gain)

    first = gather_first(own_kv, "x", "yl")
    rest = gather_rest(*first, "x", "yl")
    other_w = swap(w_out)
    carry = attend(queries, [own_kv, *first], allowed, None, False, in_hbm(up), other_w[:8, :HD])
    kept, sent = attend(queries, rest, allowed, carry, True)

    down = lax.all_gather(join([w_down], tokens=[kept]), ("x", "c"), axis=0, tiled=True)
    parts = project_out(kept, swap(sent), w_out, other_w, 8)
    attn_sum = functools.reduce(jnp.add, map(wide, scatter_rows(parts[:4], parts[4:])))
    resid = wide(latents) + table[1] * attn_sum
    own = (normed(resid) * (1.0 + table[2])).astype(jnp.bfloat16)
    plus, minus, far = move(own, 0, 1), move(own, 0, -1), move(own, 0, 2)
    ring_a = join([own, plus])
    ring_b = join([minus, far])
    plus_a, minus_a = move(ring_a, 1, 1), move(ring_a, 1, -1)
    plus_b, minus_b = move(ring_b, 1, 1), move(ring_b, 1, -1)
    far_a, far_b = move(plus_a, 1, 1), move(minus_b, 1, -1)
    blocks = [far_a, far_b, plus_a, minus_b, plus_b, minus_a, ring_a, ring_b]
    far_a, far_b, plus_a, minus_b, plus_b, minus_a, ring_a, ring_b = feed_forward(blocks, up, down)
    got_a, got_b = move(far_a, 1, -1), move(far_b, 1, 1)
    got_plus_b, got_minus_a = move(plus_b, 1, -1), move(minus_a, 1, 1)
    out = sums(whole_sum(plus_a, got_a), whole_sum(minus_b, got_b))
    got_plus_a, got_minus_b = move(out[0], 1, -1), move(out[1], 1, 1)
    terms = scatter_ring((ring_a, got_plus_a, got_minus_a), (ring_b, got_plus_b, got_minus_b), rows)
    mlp_sum = functools.reduce(jnp.add, map(wide, terms))
    return (resid + table[3] * mlp_sum).astype(jnp.bfloat16)


def solution(mesh):
    fine = Mesh(mesh.devices.reshape([SIZES[a] for a in AXES]), AXES)
    head = ("z", "yh", "c")
    return jax.shard_map(
        on_device,
        mesh=fine,
        in_specs=(
            P(AXES, None),
            P(),
            P(),
            P(),
            P(None, head),
            P(None, head),
            P(None, head),
            P(),
            P(),
            P(head, None),
            P(None, AXES),
            P(AXES, None),
        ),
        out_specs=P(AXES, None),
        check_vma=False,
    )
```
